512 devices in a mesh: gx: 64 (over z, y), gy: 8 (over x, core).
Axes of the slice: x: 4, y: 4, z: 16, core: 2. Of those that a mesh axis runs over, the one named last changes fastest.
Arguments:
- field: bfloat16 [128, 128, 20, 1024], P('gx', 'gy'), may hold values from -6 to 6
- spectral_weight: bfloat16 [576, 144, 800], P('gx', 'gy'), may hold values from -1 to 1
- skip_weight: bfloat16 [20, 20], replicated, may hold values from -1.25 to 1.25
- skip_bias: float32 [20], replicated, may hold values from -4 to 4
- hidden_weight: bfloat16 [20, 64], replicated, may hold values from -1.25 to 1.25
- hidden_bias: float32 [64], replicated, may hold values from -4 to 4
- out_weight: bfloat16 [64], replicated, may hold values from -0.75 to 0.75
- block_ids: int32 [64, 8, 200], P('gx', 'gy'), may hold values from -1 to 255, as said below
- send_rows: int32 [64, 8, 200], P('gx', 'gy'), may hold values from -1 to 255, as said below
- recv_rows: int32 [64, 8, 100], P('gx', 'gy'), may hold values from 0 to 255, as said below
Outputs:
- saturation: bfloat16 [64, 8, 100, 128], P('gx', 'gy')
The draws below stay inside these ranges and needn't reach their ends.
Inputs may be any that keep to these rules, and one draw needn't show every extreme that they name: `block_ids`: on each device the listed blocks are distinct local block numbers and fill the first slots; a device lists at most 200 and some device exactly 200; along gx, for each gy index, the lists hold 100 blocks a device on the mean. `send_rows`: -1 exactly where block_ids is -1; distinct on each device; at most 4 blocks of one device go to one owner, and 4 is reached on every draw. `recv_rows`: each owner receives exactly 100 blocks, all from devices with its own gy index; every listed block is named by exactly one slot of its owner.
All inputs are finite; a program needn't handle non-finite values.
Results may differ from the reference program's by a relative error of at most 0.02.
Values may be sent and summed in bfloat16 or wider, within the bound.
A program may use at most 128 MiB of HBM per device.

```python
import math
import jax
import jax.numpy as jnp
from jax import lax

C = 20
HID = 64
MX = 24
MY = 24
MZ = 12
MT = 12
Z = 32
T_SIZE = 32
TB = 4
CX = 2
CY = 16
X = 128
Y = 128
KZT = 144
NZB = 8
NBLK = 256
BAL = 100
MAXB = 200
N_GX = 64
N_GY = 8


def rebalance_plan(key):
    capacity = (MAXB + N_GX - 1) // N_GX
    slot_index = jnp.arange(MAXB, dtype=jnp.int32)

    def one_column(column_key):
        key_spread, key_shuffle, key_order, key_pick = jax.random.split(column_key, 4)
        spread = jax.random.randint(key_spread, (N_GX // 2,), 0, BAL + 1, dtype=jnp.int32)
        spread = spread.at[0].set(BAL)
        counts = jnp.stack([BAL + spread, BAL - spread], axis=1).reshape(N_GX).astype(jnp.int32)
        shuffle = jax.random.permutation(key_shuffle, N_GX).astype(jnp.int32)
        counts = counts[shuffle]
        order = jax.random.permutation(key_order, N_GX).astype(jnp.int32)
        ordered = counts[order]
        ends = jnp.cumsum(ordered).astype(jnp.int32)
        begins = ends - ordered
        starts = jnp.zeros((N_GX,), jnp.int32).at[order].set(begins)
        valid = slot_index[None, :] < counts[:, None]
        position = starts[:, None] + slot_index[None, :]
        sends = jnp.where(valid, position % N_GX * capacity + slot_index[None, :] // N_GX, -1).astype(jnp.int32)
        picks = jax.vmap(lambda sub_key: jax.random.permutation(sub_key, NBLK)[:MAXB])(jax.random.split(key_pick, N_GX))
        listed = jnp.where(valid, picks.astype(jnp.int32), -1).astype(jnp.int32)
        places = jnp.arange(BAL, dtype=jnp.int32)[None, :] * N_GX + jnp.arange(N_GX, dtype=jnp.int32)[:, None]
        ranked = jnp.searchsorted(ends, places, side='right').astype(jnp.int32)
        within = places - begins[ranked]
        receives = (order[ranked] * capacity + within // N_GX).astype(jnp.int32)
        return (listed, sends, receives)
    listed, sends, receives = jax.vmap(one_column)(jax.random.split(key, N_GY))
    return (jnp.transpose(listed, (1, 0, 2)), jnp.transpose(sends, (1, 0, 2)), jnp.transpose(receives, (1, 0, 2)))


def draw_block_ids(key, part):
    return rebalance_plan(key)[0]


def draw_send_rows(key, part):
    return rebalance_plan(key)[1]


def draw_recv_rows(key, part):
    return rebalance_plan(key)[2]


def block_scale(stream_key, dims, shards, low, largest):
    def one(dim, parts):
        steps = jax.random.uniform(jax.random.fold_in(jax.random.fold_in(stream_key, 6), dim), (parts,), jnp.float32, low / len(shards), largest / len(shards))
        return jnp.repeat(jnp.exp(steps), dims[dim] // parts).reshape((-1,) + (1,) * (len(dims) - dim - 1))

    level = one(*shards[0])
    for cut in shards[1:]:
        level = level * one(*cut)
    return level


def normal_values(key, extent, width, reach, cuts=(), kind=jnp.bfloat16):
    values = jax.random.normal(key, extent, jnp.float32) * width
    if len(cuts) > 0:
        values = block_scale(key, extent, cuts, -0.22, 0.18) * values
    return jnp.clip(values, min=-reach, max=reach).astype(kind)


def setup_inputs(seed: int = 0) -> dict:
    key_of = jax.random.split(jax.random.key(seed), 11)
    return {
        "field": normal_values(key_of[0], (X, Y, C, Z * T_SIZE), 1.0, 6.0, ((0, 64), (1, 8))),
        "spectral_weight": normal_values(key_of[1], (MX * MY, KZT, 2 * C * C), (2 * C) ** -0.5, 1.0, ((0, 64), (1, 8))),
        "skip_weight": normal_values(key_of[2], (C, C), C ** -0.5, 1.25),
        "skip_bias": normal_values(key_of[3], (C,), 1.0, 4.0, (), jnp.float32),
        "hidden_weight": normal_values(key_of[4], (C, HID), C ** -0.5, 1.25),
        "hidden_bias": normal_values(key_of[5], (HID,), 1.0, 4.0, (), jnp.float32),
        "out_weight": normal_values(key_of[6], (HID,), HID ** -0.5, 0.75),
        "block_ids": draw_block_ids(jax.random.fold_in(key_of[10], 71), 0),
        "send_rows": draw_send_rows(jax.random.fold_in(key_of[10], 71), 0),
        "recv_rows": draw_recv_rows(jax.random.fold_in(key_of[10], 71), 0),
    }


def signed_freqs(kept):
    return jnp.arange(kept, dtype=jnp.int32) - kept // 2

def phase_angles(freqs, places, length):
    turns = places[:, None] * freqs[None, :] % length
    return turns.astype(jnp.float32) * (2.0 * math.pi / length)

def twiddle(places, length, kept, orient, factor):
    theta = phase_angles(signed_freqs(kept), places, length)
    cosine = jnp.cos(theta) * factor
    sine = jnp.sin(theta) * (orient * factor)
    upper = jnp.stack([cosine, sine], axis=-1)
    lower = jnp.stack([-sine, cosine], axis=-1)
    return jnp.stack([upper, lower], axis=1)

def zt_angles(steps):
    places = jnp.arange(steps * Z, dtype=jnp.int32)
    along_z = phase_angles(signed_freqs(MZ), places % Z, Z)
    along_t = phase_angles(signed_freqs(MT), places // Z, T_SIZE)
    return (along_t[:, :, None] + along_z[:, None, :]).reshape(steps * Z, MT * MZ)

def forward_table():
    theta = zt_angles(T_SIZE)
    table = jnp.stack([jnp.cos(theta), -jnp.sin(theta)], axis=1) / math.sqrt(Z * T_SIZE)
    return table.reshape(Z * T_SIZE, 2 * MZ * MT).astype(jnp.bfloat16)

def block_table():
    theta = jnp.transpose(zt_angles(TB))
    table = jnp.stack([jnp.cos(theta), -jnp.sin(theta)], axis=0) / math.sqrt(MX * MY * MZ * MT)
    return table.reshape(2 * MZ * MT, TB * Z).astype(jnp.bfloat16)

def rotate(coeffs, zt_block):
    theta = jnp.repeat(phase_angles(signed_freqs(MT), zt_block * TB, T_SIZE), MZ, axis=1)[:, None, :]
    cosine = jnp.cos(theta)
    sine = jnp.sin(theta)
    real_part = coeffs[:, :, 0] * cosine - coeffs[:, :, 1] * sine
    imag_part = coeffs[:, :, 0] * sine + coeffs[:, :, 1] * cosine
    joined = jnp.stack([real_part, imag_part], axis=2).astype(jnp.bfloat16)
    return joined.reshape(coeffs.shape[0], coeffs.shape[1], 2 * MZ * MT)

def block_work(coeff, cells, skip_weight, skip_bias, hidden_weight, hidden_bias, out_weight, table):
    f32 = jnp.float32
    spectral = jnp.einsum('bcm,ml->bcl', coeff.astype(f32), table.astype(f32))
    skipped = jnp.einsum('bcl,cd->bdl', cells.astype(f32), skip_weight.astype(f32))
    state = jax.nn.gelu(spectral + skipped + skip_bias[None, :, None]).astype(jnp.bfloat16)
    inner = jnp.einsum('bdl,dh->bhl', state.astype(f32), hidden_weight.astype(f32))
    hidden = jax.nn.gelu(inner + hidden_bias[None, :, None]).astype(jnp.bfloat16)
    return jnp.einsum('bhl,h->bl', hidden.astype(f32), out_weight.astype(f32)).astype(jnp.bfloat16)

def reference(field, spectral_weight, skip_weight, skip_bias, hidden_weight, hidden_bias, out_weight, block_ids, send_rows, recv_rows):
    highest = lax.Precision.HIGHEST
    f32 = jnp.float32
    kzt = MZ * MT
    forward = forward_table()
    y_table = twiddle(jnp.arange(Y, dtype=jnp.int32), Y, MY, -1.0, 1.0 / math.sqrt(Y))

    def forward_slab(slab):
        spec = jnp.dot(slab.reshape(Y * C, Z * T_SIZE), forward, preferred_element_type=jnp.float32)
        spec = spec.astype(jnp.bfloat16).reshape(Y, C, 2, kzt).astype(f32)
        return jnp.einsum('ycik,yiqo->qcok', spec, y_table, precision=highest).astype(jnp.bfloat16)
    spec_yzt = lax.map(forward_slab, field)
    x_table = twiddle(jnp.arange(X, dtype=jnp.int32), X, MX, -1.0, 1.0 / math.sqrt(X))
    spec_all = jnp.einsum('xqcik,xipo->pqcok', spec_yzt.astype(f32), x_table, precision=highest)
    weight = spectral_weight.astype(f32).reshape(MX, MY, kzt, 2, C, C)
    real_in = spec_all[:, :, :, 0]
    imag_in = spec_all[:, :, :, 1]
    mix_real = jnp.einsum('pqck,pqkcd->pqdk', real_in, weight[:, :, :, 0], precision=highest) - jnp.einsum('pqck,pqkcd->pqdk', imag_in, weight[:, :, :, 1], precision=highest)
    mix_imag = jnp.einsum('pqck,pqkcd->pqdk', real_in, weight[:, :, :, 1], precision=highest) + jnp.einsum('pqck,pqkcd->pqdk', imag_in, weight[:, :, :, 0], precision=highest)
    mixed = jnp.stack([mix_real, mix_imag], axis=3).astype(jnp.bfloat16)
    x_back = twiddle(jnp.arange(X, dtype=jnp.int32), X, MX, 1.0, 1.0)
    back_x = jnp.einsum('pqcik,xipo->xqcok', mixed.astype(f32), x_back, precision=highest).astype(jnp.bfloat16)
    capacity = (MAXB + N_GX - 1) // N_GX

    def invert(rows_of):
        target = jnp.where(rows_of >= 0, rows_of, N_GX * capacity)
        return jnp.zeros((N_GX * capacity,), jnp.int32).at[target].set(jnp.arange(MAXB, dtype=jnp.int32), mode='drop')
    inverse = jax.vmap(jax.vmap(invert))(send_rows)
    source = recv_rows // capacity
    owner_x = jnp.arange(N_GX, dtype=jnp.int32)[:, None, None] + jnp.zeros_like(recv_rows)
    owner_y = jnp.arange(N_GY, dtype=jnp.int32)[None, :, None] + jnp.zeros_like(recv_rows)
    lookup = owner_x * capacity + recv_rows % capacity
    slot_of = inverse[source, owner_y, lookup]
    listed = block_ids[source, owner_y, slot_of]
    x_global = source * CX + listed // (CY * NZB)
    y_global = owner_y * CY + listed // NZB % CY
    zt_block = listed % NZB
    group = BAL // 4
    x_groups = x_global.reshape(-1, group)
    y_groups = y_global.reshape(-1, group)
    z_groups = zt_block.reshape(-1, group)
    table = block_table()
    blocked = field.reshape(X, Y, C, NZB, TB * Z)

    def per_group(packed):
        x_list, y_list, z_list = packed
        rows_at = back_x[x_list].astype(f32)
        turn_at = twiddle(y_list, Y, MY, 1.0, 1.0)
        cols_at = jnp.einsum('bqcik,biqo->bcok', rows_at, turn_at, precision=highest).astype(jnp.bfloat16)
        coeff = rotate(cols_at.astype(f32), z_list)
        cells = blocked[x_list, y_list, :, z_list]
        return block_work(coeff, cells, skip_weight, skip_bias, hidden_weight, hidden_bias, out_weight, table)
    result = lax.map(per_group, (x_groups, y_groups, z_groups))
    return result.reshape(N_GX, N_GY, BAL, TB * Z)
```

```python
import functools
import math

import jax
import jax.numpy as jnp
import ml_dtypes
import numpy as np
from jax import lax
from jax.experimental import pallas as pl
from jax.experimental.pallas import tpu as pltpu
from jax.sharding import PartitionSpec as P

C = 20
HID = 64
MX = 24
MY = 24
MZ = 12
MT = 12
Z = 32
T_SIZE = 32
X = 128
Y = 128
KZT = MZ * MT
PK = 18
G = 7
R = 8
LW = G * 128
W2 = 2 * C * C
MESH = pl.DeviceIdType.MESH
f32 = jnp.float32
bf16 = jnp.bfloat16
GA = math.sqrt(2.0 / math.pi)
GB = GA * 0.044715


def constants():
    half = ml_dtypes.bfloat16

    def cos_sin(f, n, length):
        a = 2.0 * np.pi * ((f * n) % length) / length
        return np.cos(a), np.sin(a)

    q = np.arange(Z * T_SIZE)
    forward = np.zeros((Z * T_SIZE, 384))
    backward = np.zeros((384, Z * T_SIZE))
    for j in range(R):
        for k in range(PK):
            kk = PK * j + k
            fz, ft = kk % MZ - MZ // 2, kk // MZ - MT // 2
            a = 2.0 * np.pi * (((fz * (q % Z)) % Z) / Z + ((ft * (q // Z)) % T_SIZE) / T_SIZE)
            lane = 128 * (j // 3) + PK * (j % 3) + k
            forward[:, lane] = np.cos(a) / math.sqrt(Z * T_SIZE)
            forward[:, lane + 64] = -np.sin(a) / math.sqrt(Z * T_SIZE)
            backward[lane] = np.cos(a) / math.sqrt(MX * MY * KZT)
            backward[lane + 64] = -np.sin(a) / math.sqrt(MX * MY * KZT)
    fy = np.arange(MY) - MY // 2
    c, s = cos_sin(fy[:, None], np.arange(Y)[None, :], Y)
    y_fwd = np.concatenate([c, s], 0) / math.sqrt(Y)
    y_bwd = np.concatenate([c.T, s.T], 0)
    fx = np.arange(MX) - MX // 2
    x_fwd = np.zeros((R, 48, 16))
    x_bwd = np.zeros((R, 32, 24))
    for e in range(R):
        x = (16 * np.arange(8)[:, None] + 2 * e + np.arange(2)[None, :]).reshape(-1)
        c, s = cos_sin(fx[:, None], x[None, :], X)
        x_fwd[e] = np.concatenate([c, s], 0) / math.sqrt(X)
        x_bwd[e] = np.concatenate([c.T, s.T], 0)
    gather = np.zeros((LW, 128))
    spread = np.zeros((128, LW))
    for ch in range(C):
        for r in range(2):
            for k in range(PK):
                lane = 128 * (ch // 3) + 64 * r + PK * (ch % 3) + k
                gather[lane, 64 * r + ch] = 1.0
                spread[64 * r + ch, lane] = 1.0
    widen = np.zeros((128, LW))
    widen_swapped = np.zeros((128, LW))
    sum_re = np.zeros((LW, 128))
    sum_im = np.zeros((LW, 128))
    for r in range(2):
        for ch in range(C):
            for d in range(C):
                col = 400 * r + C * ch + d
                widen[64 * r + ch, col] = 1.0
                widen_swapped[64 * (1 - r) + ch, col] = 1.0
                sum_re[col, d] = 1.0 - 2.0 * r
                sum_im[col, 64 + d] = 1.0
    regroup = np.zeros((256, 256))
    for e in range(R):
        for zh in range(R):
            for n in range(4):
                regroup[32 * e + 4 * zh + n, 32 * zh + 4 * e + n] = 1.0
    tables = (
        forward, backward, y_fwd, y_bwd, x_fwd, x_bwd, gather, spread,
        widen, widen_swapped, sum_re, sum_im, regroup,
    )
    return [t.astype(half) for t in tables]


def mm(a, b):
    return lax.dot_general(a, b, (((1,), (0,)), ((), ())), preferred_element_type=f32)


def iota(shape, dim):
    return lax.broadcasted_iota(jnp.int32, shape, dim)


def one_hot(mask):
    return jnp.where(mask, 1.0, 0.0).astype(f32)


def twice_gelu(v):
    return v + v * jnp.tanh(v * (GA + GB * (v * v)))


def kernel(*refs):
    (
        field, weight, skip_w, skip_b, hid_w, hid_b, out_w, b_ids, s_rows, r_rows,
        t_fwd, t_bwd, y_fwd, y_bwd, x_fwd, x_bwd, gather, spread,
        widen, widen_sw, sum_re, sum_im, regroup,
        out,
        send_y, recv_y, ya, send_a, recv_a, xa, xb, send_b, recv_b, spec_b, spec_p,
        pairs, amat, mix, mix_p, mix_b, send_c, recv_c, xc, xd, send_d, recv_d, xe, send_e, recv_e,
        s6, part, blk, send_f, recv_f, send_g, recv_g, wpad, perm, pick, idrows, square, skip_k, hid_k,
        skip_col, hid_col, out_col,
        ss_y, rs_y, ss_a, rs_a, ss_b, rs_b, ss_p, rs_p, ls_p, ss_q, rs_q, ls_q, ss_c, rs_c,
        ss_d, rs_d, ss_e, rs_e, ss_f, rs_f, ss_g, rs_g,
    ) = refs
    i = lax.axis_index("gx")
    j = lax.axis_index("gy")
    zh = lax.div(i, R)
    e = lax.rem(i, R)

    def turn(n, d):
        return lax.rem(n + d, R)

    def on_y(d):
        return turn(j, d), (i, turn(j, d))

    def on_z(d):
        return turn(zh, d), (R * turn(zh, d) + e, j)

    def on_e(d):
        return turn(e, d), (R * zh + turn(e, d), j)

    owners = []
    for n in range(3):
        first = MY * (3 * e + n) + 3 * zh
        owners.append((lax.div(first, 9), lax.div(lax.rem(first, 9), 3)))
    sources = []
    for a in range(3):
        first = 9 * i + 3 * a
        jx, jy = lax.div(first, MY), lax.rem(first, MY)
        sources.append((R * lax.div(jy, 3) + lax.div(jx, 3), lax.rem(jx, 3)))

    barrier = pltpu.get_barrier_semaphore()
    for near in (on_y, on_z, on_e):
        for d in range(1, R):
            pl.semaphore_signal(barrier, inc=1, device_id=near(d)[1], device_id_type=MESH)
    for other, _ in owners + sources:

        @pl.when(other != i)
        def _():
            pl.semaphore_signal(barrier, inc=1, device_id=(other, j), device_id_type=MESH)

    def exchange_copies(near, me, send, recv, send_sem, recv_sem, same=False):
        copies = []
        for d in range(1, R):
            peer, device = near(d)
            copies.append(
                pltpu.make_async_remote_copy(
                    src_ref=send if same else send.at[peer],
                    dst_ref=recv.at[me],
                    send_sem=send_sem.at[d - 1],
                    recv_sem=recv_sem.at[d - 1],
                    device_id=device,
                    device_id_type=MESH,
                )
            )
        return copies

    def exchange(near, me, send, recv, send_sem, recv_sem, same=False, beside=None):
        copies = exchange_copies(near, me, send, recv, send_sem, recv_sem, same)
        for copy in copies:
            copy.start()
        recv[me] = send[...] if same else send[me]
        if beside is not None:
            beside()
        for copy in copies:
            copy.wait()

    lane = iota((1, 128), 1)
    in_half = lane & 63
    piece = [
        (in_half >= PK * m) & (in_half < PK * (m + 1)) for m in range(3)
    ]
    fwd_sign = jnp.where(lane < 64, 1.0, -1.0)

    def regrouped(held, n):
        total = jnp.zeros(held[0].shape, f32)
        for m, rows in enumerate(held):
            if rows is None:
                continue
            shift = (PK * (m - n)) % 128
            moved = rows if shift == 0 else pltpu.roll(rows, shift, 1)
            total = jnp.where(piece[m], moved, total)
        return total

    def combine(cosines, sines, sign):
        return cosines + sign * pltpu.roll(sines, 64, 1)

    for x in range(2):
        got = mm(field[320 * x : 320 * x + 320, :], t_fwd[...])
        for g in range(G):
            for t in range(3):
                held = [
                    got[16 * c : 16 * c + 16, 128 * t : 128 * t + 128] if c < C else None
                    for c in range(3 * g, 3 * g + 3)
                ]
                for n in range(min(3, R - 3 * t)):
                    send_y[3 * t + n, 16 * x : 16 * x + 16, 128 * g : 128 * g + 128] = (
                        regrouped(held, n).astype(bf16)
                    )

    expected = 3 * (R - 1)
    for other, _ in owners + sources:
        expected = expected + jnp.where(other != i, 1, 0)
    pl.semaphore_wait(barrier, expected)

    def prepare():
        wpad[...] = jnp.zeros((288, LW), bf16)
        for p in range(9):
            wpad[32 * p : 32 * p + PK, 0:W2] = weight[p]
        ya[...] = jnp.zeros((384, 128), f32)
        xb[...] = jnp.zeros((576, 128), f32)
        xd[...] = jnp.zeros((384, 128), f32)
        mix[...] = jnp.zeros((72, 128), f32)
        idrows[...] = jnp.full((8, 256), -1, jnp.int32)
        idrows[0:1, 0:200] = b_ids[...]
        idrows[1:2, 0:200] = s_rows[...]
        idrows[2:3, 0:100] = r_rows[...]
        row = iota((256, 256), 0)
        by_block = one_hot(row == idrows[0:1, :]).astype(bf16)
        by_row = one_hot(row == idrows[1:2, :]).astype(bf16)
        perm[...] = lax.dot_general(
            by_row, by_block, (((1,), (1,)), ((), ())), preferred_element_type=f32
        ).astype(bf16)
        place = iota((256, 128), 0)
        name = ((place >> 2) & 7) * 32 + (place >> 5) * 4 + (place & 3)
        pick[...] = one_hot(name == idrows[2:3, 0:128]).T.astype(bf16)
        def spread_map(values, rows, cols, places):
            shift = places.bit_length() - 1
            left = one_hot((iota((rows, 128), 0) >> shift) == iota((rows, 128), 1)).astype(bf16)
            right = one_hot((iota((128, cols), 1) >> shift) == iota((128, cols), 0)).astype(bf16)
            wide = mm(mm(left, values.T.astype(bf16)).astype(bf16), right)
            same = (iota((rows, cols), 0) & (places - 1)) == (iota((rows, cols), 1) & (places - 1))
            return jnp.where(same, wide, 0.0).astype(bf16)

        square[...] = jnp.zeros((128, 128), f32)
        square[0:C, 0:C] = skip_w[...].astype(f32)
        skip_k[...] = spread_map(square[...], 320, 320, 16)
        square[0:C, 0:HID] = hid_w[...].astype(f32)
        hid_k[...] = spread_map(square[...], 512, 160, 8)

        def column(values, places, width, rows):
            shift = places.bit_length() - 1
            at = one_hot((iota((rows, width), 0) >> shift) == iota((rows, width), 1))
            return jnp.broadcast_to(
                jnp.sum(at * values, axis=1, keepdims=True), (rows, 256)
            )

        skip_col[...] = column(skip_b[...], 16, C, 320)
        hid_col[...] = column(hid_b[...], 8, HID, 512)
        out_col[...] = column(0.5 * out_w[...].astype(f32), 8, HID, 512)

    exchange(on_y, j, send_y, recv_y, ss_y, rs_y, beside=prepare)

    for x in range(2):
        data = recv_y[:, 16 * x : 16 * x + 16, :].reshape(Y, LW)
        got = mm(y_fwd[...], data)
        for g in range(G):
            part_g = got[:, 128 * g : 128 * g + 128]
            ya[pl.ds(192 * x + g, MY, stride=8), :] = combine(
                part_g[0:MY], part_g[MY : 2 * MY], fwd_sign
            )
    for p in range(R):
        send_a[p] = jnp.concatenate(
            [ya[24 * p : 24 * p + 24, :], ya[192 + 24 * p : 216 + 24 * p, :]], axis=0
        ).astype(bf16)
    exchange(on_z, zh, send_a, recv_a, ss_a, rs_a)

    for p in range(R):
        xa[48 * p : 48 * p + 48, :] = recv_a[p].astype(f32)
    used = [8 * a + g for a in range(3) for g in range(G)]
    data = jnp.concatenate(
        [xa[pl.ds(u, 16, stride=24), :] for u in used], axis=1
    ).astype(bf16)
    got = mm(x_fwd[e], data)
    for n, u in enumerate(used):
        part_u = got[:, 128 * n : 128 * n + 128]
        xb[pl.ds(u, MX, stride=24), :] = combine(part_u[0:MX], part_u[MX : 2 * MX], fwd_sign)
    for p in range(R):
        send_b[p] = jnp.concatenate(
            [xb[72 * p : 72 * p + 72, :], jnp.zeros((8, 128), f32)], axis=0
        ).astype(bf16)
    exchange(on_e, e, send_b, recv_b, ss_b, rs_b)
    total = recv_b[0].astype(f32)
    for p in range(1, R):
        total = total + recv_b[p].astype(f32)
    for n in range(3):
        spec_b[n] = total[24 * n : 24 * n + 24]

    def own_copy(src, n, dst, a, send_sem, recv_sem, device):
        return pltpu.make_async_remote_copy(
            src_ref=src.at[n],
            dst_ref=dst.at[a],
            send_sem=send_sem.at[n],
            recv_sem=recv_sem.at[a],
            device_id=(device, j),
            device_id_type=MESH,
        )

    def hand_over(src, dst, targets, origins, send_sem, recv_sem, local_sem):
        for n, (device, a) in enumerate(targets):

            @pl.when(device != i)
            def _():
                own_copy(src, n, dst, a, send_sem, recv_sem, device).start()

            @pl.when(device == i)
            def _():
                copy = pltpu.make_async_copy(src.at[n], dst.at[a], local_sem.at[n])
                copy.start()
                copy.wait()

        for n, (device, a) in enumerate(targets):

            @pl.when(device != i)
            def _():
                own_copy(src, n, dst, a, send_sem, recv_sem, device).wait_send()

        for a, (device, n) in enumerate(origins):

            @pl.when(device != i)
            def _():
                own_copy(src, n, dst, a, send_sem, recv_sem, device).wait_recv()

    hand_over(spec_b, spec_p, owners, sources, ss_p, rs_p, ls_p)

    own_k = one_hot(
        (iota((32, 128), 1) & 63 < 3 * PK)
        & (lax.rem(iota((32, 128), 1) & 63, PK) == iota((32, 128), 0))
    )
    for n in range(3):
        pairs[24 * n : 24 * n + 24, :] = spec_p[n]
    for p in range(9):
        for g in range(G):
            row = jnp.broadcast_to(pairs[8 * p + g : 8 * p + g + 1, :], (32, 128))
            amat[32 * p : 32 * p + 32, 128 * g : 128 * g + 128] = (row * own_k).astype(bf16)
    compact = mm(amat[...], gather[...]).astype(bf16)
    weights = wpad[...].astype(f32)
    straight = (mm(compact, widen[...]) * weights).astype(bf16)
    crossed = (mm(compact, widen_sw[...]) * weights).astype(bf16)
    mixed = (mm(straight, sum_re[...]) + mm(crossed, sum_im[...])).astype(bf16)
    wide = mm(mixed, spread[...])
    for p in range(9):
        for g in range(G):
            tile = wide[32 * p : 32 * p + 32, 128 * g : 128 * g + 128] * own_k
            mix[8 * p + g : 8 * p + g + 1, :] = jnp.sum(tile, axis=0, keepdims=True)
    for a in range(3):
        mix_p[a] = mix[24 * a : 24 * a + 24, :]

    hand_over(mix_p, mix_b, sources, owners, ss_q, rs_q, ls_q)
    send_c[...] = jnp.concatenate(
        [mix_b[0], mix_b[1], mix_b[2], jnp.zeros((8, 128), f32)], axis=0
    ).astype(bf16)
    exchange(on_e, e, send_c, recv_c, ss_c, rs_c, same=True)

    for p in range(R):
        xc[72 * p : 72 * p + 72, :] = recv_c[p].astype(f32)[0:72]
    data = jnp.concatenate(
        [xc[pl.ds(u, MX, stride=24), :] for u in used], axis=1
    ).astype(bf16)
    got = mm(x_bwd[e], data)
    for n, u in enumerate(used):
        part_u = got[:, 128 * n : 128 * n + 128]
        xd[pl.ds(u, 16, stride=24), :] = combine(part_u[0:16], part_u[16:32], -fwd_sign)
    for p in range(R):
        send_d[p] = xd[48 * p : 48 * p + 48, :].astype(bf16)
    exchange(on_z, zh, send_d, recv_d, ss_d, rs_d)

    for p in range(R):
        got = recv_d[p].astype(f32)
        xe[24 * p : 24 * p + 24, :] = got[0:24]
        xe[192 + 24 * p : 216 + 24 * p, :] = got[24:48]
    for x in range(2):
        data = jnp.concatenate(
            [xe[pl.ds(192 * x + g, MY, stride=8), :] for g in range(G)], axis=1
        ).astype(bf16)
        got = mm(y_bwd[...], data)
        for g in range(G):
            part_g = got[:, 128 * g : 128 * g + 128]
            turned = combine(part_g[0:Y], part_g[Y : 2 * Y], -fwd_sign).astype(bf16)
            send_e[:, 16 * x : 16 * x + 16, 128 * g : 128 * g + 128] = turned.reshape(R, 16, 128)
    exchange(on_y, j, send_e, recv_e, ss_e, rs_e)

    for t in range(3):
        for g in range(G):
            held = [
                recv_e[n, :, 128 * g : 128 * g + 128].astype(f32) if n < R else None
                for n in range(3 * t, 3 * t + 3)
            ]
            for m in range(min(3, C - 3 * g)):
                total = regrouped(held, m).astype(bf16)
                for x in range(2):
                    row = 320 * x + 16 * (3 * g + m)
                    s6[row : row + 16, 128 * t : 128 * t + 128] = total[16 * x : 16 * x + 16]

    @pl.loop(0, 2)
    def _(x):
        rows = pl.ds(pl.multiple_of(x * 320, 320), 320)
        for c in range(4):
            cut = slice(256 * c, 256 * c + 256)
            value = mm(s6[rows, :], t_bwd[:, cut]) + mm(skip_k[...], field[rows, cut])
            state = 0.5 * twice_gelu(value + skip_col[...])
            halves = state.reshape(C, 2, 8, 256)
            for h in range(2):
                inner = mm(hid_k[...], halves[:, h].reshape(160, 256).astype(bf16))
                weighed = twice_gelu(inner + hid_col[...]) * out_col[...]
                part[pl.ds(pl.multiple_of(x * 16, 16) + 8 * h, 8), cut] = jnp.sum(
                    weighed.reshape(HID, 8, 256), axis=0
                )

    for b in range(8):
        blk[pl.ds(b, 32, stride=8), :] = part[:, 128 * b : 128 * b + 128]

    send_f[...] = mm(perm[...], blk[...].astype(bf16)).astype(bf16).reshape(R, 32, 128)
    exchange(on_z, zh, send_f, recv_f, ss_f, rs_f)
    send_g[...] = mm(regroup[...], recv_f[...].reshape(256, 128)).astype(bf16).reshape(R, 32, 128)
    exchange(on_e, e, send_g, recv_g, ss_g, rs_g)
    owned = mm(pick[...], recv_g[...].reshape(256, 128))
    out[...] = owned[0:100].astype(bf16)


def scratch():
    v = pltpu.VMEM
    dma = pltpu.SemaphoreType.DMA
    buffers = [
        v((R, 32, LW), bf16),
        v((R, 32, LW), bf16),
        v((384, 128), f32),
        v((R, 48, 128), bf16),
        v((R, 48, 128), bf16),
        v((384, 128), f32),
        v((576, 128), f32),
        v((R, 80, 128), bf16),
        v((R, 80, 128), bf16),
        v((3, 24, 128), f32),
        v((3, 24, 128), f32),
        v((72, 128), f32),
        v((288, LW), bf16),
        v((72, 128), f32),
        v((3, 24, 128), f32),
        v((3, 24, 128), f32),
        v((80, 128), bf16),
        v((R, 80, 128), bf16),
        v((576, 128), f32),
        v((384, 128), f32),
        v((R, 48, 128), bf16),
        v((R, 48, 128), bf16),
        v((384, 128), f32),
        v((R, 32, LW), bf16),
        v((R, 32, LW), bf16),
        v((640, 384), bf16),
        v((32, 1024), f32),
        v((256, 128), f32),
        v((R, 32, 128), bf16),
        v((R, 32, 128), bf16),
        v((R, 32, 128), bf16),
        v((R, 32, 128), bf16),
        v((288, LW), bf16),
        v((256, 256), bf16),
        v((128, 256), bf16),
        v((8, 256), jnp.int32),
        v((128, 128), f32),
        v((320, 320), bf16),
        v((512, 160), bf16),
        v((320, 256), f32),
        v((512, 256), f32),
        v((512, 256), f32),
    ]
    sems = []
    for count in (7, 7, 7, 7, 7, 7, 3, 3, 3, 3, 3, 3, 7, 7, 7, 7, 7, 7, 7, 7, 7, 7):
        sems.append(dma((count,)))
    return buffers + sems


def local(
    field,
    spectral_weight,
    skip_weight,
    skip_bias,
    hidden_weight,
    hidden_bias,
    out_weight,
    block_ids,
    send_rows,
    recv_rows,
):
    tables = [jnp.asarray(t) for t in constants()]
    args = [
        jnp.transpose(field, (0, 2, 1, 3)).reshape(640, Z * T_SIZE),
        spectral_weight,
        skip_weight,
        skip_bias.reshape(1, C),
        hidden_weight,
        hidden_bias.reshape(1, HID),
        out_weight.reshape(1, HID),
        block_ids.reshape(1, 200),
        send_rows.reshape(1, 200),
        recv_rows.reshape(1, 100),
    ] + tables
    vmem = pl.BlockSpec(memory_space=pltpu.VMEM)
    result = pl.pallas_call(
        kernel,
        out_shape=jax.ShapeDtypeStruct((100, 128), bf16),
        in_specs=[vmem] * len(args),
        out_specs=vmem,
        scratch_shapes=scratch(),
        compiler_params=pltpu.CompilerParams(
            collective_id=0, has_side_effects=True, vmem_limit_bytes=56 * 1024 * 1024
        ),
    )(*args)
    return result.reshape(1, 1, 100, 128)


def solution(mesh):
    placed = (
        P("gx", "gy", None, None),
        P("gx", "gy", None),
        P(),
        P(),
        P(),
        P(),
        P(),
        P("gx", "gy", None),
        P("gx", "gy", None),
        P("gx", "gy", None),
    )
    return jax.shard_map(
        local, mesh=mesh, in_specs=placed, out_specs=P("gx", "gy", None, None), check_vma=False
    )
```

```python
import functools
import math

import jax
import jax.numpy as jnp
import ml_dtypes
import numpy as np
from jax import lax
from jax.experimental import pallas as pl
from jax.experimental.pallas import tpu as pltpu
from jax.sharding import PartitionSpec as P

C = 20
HID = 64
MX = 24
MY = 24
MZ = 12
MT = 12
Z = 32
T_SIZE = 32
X = 128
Y = 128
KZT = MZ * MT
PK = 18
G = 7
R = 8
LW = G * 128
W2 = 2 * C * C
MESH = pl.DeviceIdType.MESH
f32 = jnp.float32
bf16 = jnp.bfloat16
GA = math.sqrt(2.0 / math.pi)
GB = GA * 0.044715


def constants():
    half = ml_dtypes.bfloat16

    def cos_sin(f, n, length):
        a = 2.0 * np.pi * ((f * n) % length) / length
        return np.cos(a), np.sin(a)

    q = np.arange(Z * T_SIZE)
    forward = np.zeros((Z * T_SIZE, 384))
    backward = np.zeros((384, Z * T_SIZE))
    for j in range(R):
        for k in range(PK):
            kk = PK * j + k
            fz, ft = kk % MZ - MZ // 2, kk // MZ - MT // 2
            a = 2.0 * np.pi * (((fz * (q % Z)) % Z) / Z + ((ft * (q // Z)) % T_SIZE) / T_SIZE)
            lane = 128 * (j // 3) + PK * (j % 3) + k
            forward[:, lane] = np.cos(a) / math.sqrt(Z * T_SIZE)
            forward[:, lane + 64] = -np.sin(a) / math.sqrt(Z * T_SIZE)
            backward[lane] = np.cos(a) / math.sqrt(MX * MY * KZT)
            backward[lane + 64] = -np.sin(a) / math.sqrt(MX * MY * KZT)
    fy = np.arange(MY) - MY // 2
    c, s = cos_sin(fy[:, None], np.arange(Y)[None, :], Y)
    y_fwd = np.concatenate([c, s], 0) / math.sqrt(Y)
    y_bwd = np.concatenate([c.T, s.T], 0)
    fx = np.arange(MX) - MX // 2
    x_fwd = np.zeros((R, 48, 16))
    x_bwd = np.zeros((R, 32, 24))
    for e in range(R):
        x = (16 * np.arange(8)[:, None] + 2 * e + np.arange(2)[None, :]).reshape(-1)
        c, s = cos_sin(fx[:, None], x[None, :], X)
        x_fwd[e] = np.concatenate([c, s], 0) / math.sqrt(X)
        x_bwd[e] = np.concatenate([c.T, s.T], 0)
    gather = np.zeros((LW, 128))
    spread = np.zeros((128, LW))
    for ch in range(C):
        for r in range(2):
            for k in range(PK):
                lane = 128 * (ch // 3) + 64 * r + PK * (ch % 3) + k
                gather[lane, 64 * r + ch] = 1.0
                spread[64 * r + ch, lane] = 1.0
    widen = np.zeros((128, LW))
    widen_swapped = np.zeros((128, LW))
    sum_re = np.zeros((LW, 128))
    sum_im = np.zeros((LW, 128))
    for r in range(2):
        for ch in range(C):
            for d in range(C):
                col = 400 * r + C * ch + d
                widen[64 * r + ch, col] = 1.0
                widen_swapped[64 * (1 - r) + ch, col] = 1.0
                sum_re[col, d] = 1.0 - 2.0 * r
                sum_im[col, 64 + d] = 1.0
    regroup = np.zeros((256, 256))
    for e in range(R):
        for zh in range(R):
            for n in range(4):
                regroup[32 * e + 4 * zh + n, 32 * zh + 4 * e + n] = 1.0
    tables = (
        forward, backward, y_fwd, y_bwd, x_fwd, x_bwd, gather, spread,
        widen, widen_swapped, sum_re, sum_im, regroup,
    )
    return [t.astype(half) for t in tables]


def mm(a, b):
    return lax.dot_general(a, b, (((1,), (0,)), ((), ())), preferred_element_type=f32)


def iota(shape, dim):
    return lax.broadcasted_iota(jnp.int32, shape, dim)


def one_hot(mask):
    return jnp.where(mask, 1.0, 0.0).astype(f32)


def twice_gelu(v):
    return v + v * jnp.tanh(v * (GA + GB * (v * v)))


def kernel(*refs):
    (
        field_in, weight_in, skip_w, skip_b, hid_w, hid_b, out_w, b_ids, s_rows, r_rows,
        t_fwd_in, t_bwd_in, y_fwd_in, y_bwd_in, x_fwd_in, x_bwd_in, gather_in, spread_in,
        widen_in, widen_sw_in, sum_re_in, sum_im_in, regroup_in,
        out,
        field, weight, t_fwd, t_bwd, y_fwd, y_bwd, x_fwd, x_bwd, gather, spread,
        widen, widen_sw, sum_re, sum_im, regroup,
        send_y, recv_y, ya, send_a, recv_a, xa, xb, send_b, recv_b, spec_b, spec_p,
        pairs, amat, mix, mix_p, mix_b, send_c, recv_c, xc, xd, send_d, recv_d, xe, send_e, recv_e,
        s6, part, blk, send_f, recv_f, send_g, recv_g, wpad, perm, pick, idrows, square, skip_k, hid_k,
        skip_col, hid_col, out_col,
        fetched,
        ss_y, rs_y, ss_a, rs_a, ss_b, rs_b, ss_p, rs_p, ls_p, ss_q, rs_q, ls_q, ss_c, rs_c,
        ss_d, rs_d, ss_e, rs_e, ss_f, rs_f, ss_g, rs_g,
    ) = refs
    i = lax.axis_index("gx")
    j = lax.axis_index("gy")
    zh = lax.div(i, R)
    e = lax.rem(i, R)

    def turn(n, d):
        return lax.rem(n + d, R)

    def on_y(d):
        return turn(j, d), (i, turn(j, d))

    def on_z(d):
        return turn(zh, d), (R * turn(zh, d) + e, j)

    def on_e(d):
        return turn(e, d), (R * zh + turn(e, d), j)

    owners = []
    for n in range(3):
        first = MY * (3 * e + n) + 3 * zh
        owners.append((lax.div(first, 9), lax.div(lax.rem(first, 9), 3)))
    sources = []
    for a in range(3):
        first = 9 * i + 3 * a
        jx, jy = lax.div(first, MY), lax.rem(first, MY)
        sources.append((R * lax.div(jy, 3) + lax.div(jx, 3), lax.rem(jx, 3)))

    barrier = pltpu.get_barrier_semaphore()
    for near in (on_y, on_z, on_e):
        for d in range(1, R):
            pl.semaphore_signal(barrier, inc=1, device_id=near(d)[1], device_id_type=MESH)
    for other, _ in owners + sources:

        @pl.when(other != i)
        def _():
            pl.semaphore_signal(barrier, inc=1, device_id=(other, j), device_id_type=MESH)

    fetch = []
    wanted = [
        (field_in.at[0], field.at[0]), (t_fwd_in, t_fwd), (field_in.at[1], field.at[1]),
        (y_fwd_in, y_fwd), (weight_in, weight), (x_fwd_in, x_fwd), (gather_in, gather),
        (widen_in, widen), (widen_sw_in, widen_sw), (sum_re_in, sum_re), (sum_im_in, sum_im),
        (spread_in, spread), (x_bwd_in, x_bwd), (y_bwd_in, y_bwd), (t_bwd_in, t_bwd),
        (regroup_in, regroup),
    ]
    for n, (source, target) in enumerate(wanted):
        fetch.append(pltpu.make_async_copy(source, target, fetched.at[n]))
        fetch[n].start()

    def exchange_copies(near, me, send, recv, send_sem, recv_sem, same=False):
        copies = []
        for d in range(1, R):
            peer, device = near(d)
            copies.append(
                pltpu.make_async_remote_copy(
                    src_ref=send if same else send(peer),
                    dst_ref=recv(me),
                    send_sem=send_sem.at[d - 1],
                    recv_sem=recv_sem.at[d - 1],
                    device_id=device,
                    device_id_type=MESH,
                )
            )
        return copies

    def start(copies):
        for copy in copies:
            copy.start()

    def finish(copies):
        for copy in copies:
            copy.wait()

    def exchange(near, me, send, recv, send_sem, recv_sem, same=False):
        copies = exchange_copies(
            near, me, send if same else lambda p: send.at[p], lambda p: recv.at[p],
            send_sem, recv_sem, same,
        )
        start(copies)
        recv[me] = send[...] if same else send[me]
        finish(copies)

    def copies_y(x, send, recv, send_sem, recv_sem):
        return exchange_copies(
            on_y, j, lambda p: send.at[p, x], lambda p: recv.at[x, p], send_sem.at[x], recv_sem.at[x]
        )

    def copies_z(x, send, recv, send_sem, recv_sem):
        return exchange_copies(
            on_z, zh, lambda p: send.at[p, x], lambda p: recv.at[p, x], send_sem.at[x], recv_sem.at[x]
        )

    lane = iota((1, 128), 1)
    in_half = lane & 63
    piece = [
        (in_half >= PK * m) & (in_half < PK * (m + 1)) for m in range(3)
    ]
    fwd_sign = jnp.where(lane < 64, 1.0, -1.0)

    def regrouped(held, n):
        total = jnp.zeros(held[0].shape, f32)
        for m, rows in enumerate(held):
            if rows is None:
                continue
            shift = (PK * (m - n)) % 128
            moved = rows if shift == 0 else pltpu.roll(rows, shift, 1)
            total = jnp.where(piece[m], moved, total)
        return total

    def combine(cosines, sines, sign):
        return cosines + sign * pltpu.roll(sines, 64, 1)

    def along_zt(x):
        got = mm(field[x], t_fwd[...])
        for g in range(G):
            for t in range(3):
                held = [
                    got[16 * c : 16 * c + 16, 128 * t : 128 * t + 128] if c < C else None
                    for c in range(3 * g, 3 * g + 3)
                ]
                for n in range(min(3, R - 3 * t)):
                    send_y[3 * t + n, x, :, 128 * g : 128 * g + 128] = (
                        regrouped(held, n).astype(bf16)
                    )

    fetch[0].wait()
    fetch[1].wait()
    along_zt(0)

    expected = 3 * (R - 1)
    for other, _ in owners + sources:
        expected = expected + jnp.where(other != i, 1, 0)
    pl.semaphore_wait(barrier, expected)

    going_y = [copies_y(x, send_y, recv_y, ss_y, rs_y) for x in range(2)]
    start(going_y[0])
    fetch[2].wait()
    along_zt(1)
    start(going_y[1])
    for x in range(2):
        recv_y[x, j] = send_y[j, x]
    for copy in fetch[3:]:
        copy.wait()

    def prepare():
        wpad[...] = jnp.zeros((288, LW), bf16)
        for p in range(9):
            wpad[32 * p : 32 * p + PK, 0:W2] = weight[p]
        ya[...] = jnp.zeros((384, 128), f32)
        xb[...] = jnp.zeros((576, 128), f32)
        xd[...] = jnp.zeros((384, 128), f32)
        mix[...] = jnp.zeros((72, 128), f32)
        idrows[...] = jnp.full((8, 256), -1, jnp.int32)
        idrows[0:1, 0:200] = b_ids[...]
        idrows[1:2, 0:200] = s_rows[...]
        idrows[2:3, 0:100] = r_rows[...]
        row = iota((256, 256), 0)
        by_block = one_hot(row == idrows[0:1, :]).astype(bf16)
        by_row = one_hot(row == idrows[1:2, :]).astype(bf16)
        perm[...] = lax.dot_general(
            by_row, by_block, (((1,), (1,)), ((), ())), preferred_element_type=f32
        ).astype(bf16)
        place = iota((256, 128), 0)
        name = ((place >> 2) & 7) * 32 + (place >> 5) * 4 + (place & 3)
        pick[...] = one_hot(name == idrows[2:3, 0:128]).T.astype(bf16)
        def spread_map(values, rows, cols, places):
            shift = places.bit_length() - 1
            left = one_hot((iota((rows, 128), 0) >> shift) == iota((rows, 128), 1)).astype(bf16)
            right = one_hot((iota((128, cols), 1) >> shift) == iota((128, cols), 0)).astype(bf16)
            wide = mm(mm(left, values.T.astype(bf16)).astype(bf16), right)
            same = (iota((rows, cols), 0) & (places - 1)) == (iota((rows, cols), 1) & (places - 1))
            return jnp.where(same, wide, 0.0).astype(bf16)

        square[...] = jnp.zeros((128, 128), f32)
        square[0:C, 0:C] = skip_w[...].astype(f32)
        skip_k[...] = spread_map(square[...], 320, 320, 16)
        square[0:C, 0:HID] = hid_w[...].astype(f32)
        hid_k[...] = spread_map(square[...], 512, 160, 8)

        def column(values, places, width, rows):
            shift = places.bit_length() - 1
            at = one_hot((iota((rows, width), 0) >> shift) == iota((rows, width), 1))
            return jnp.broadcast_to(
                jnp.sum(at * values, axis=1, keepdims=True), (rows, 256)
            )

        skip_col[...] = column(skip_b[...], 16, C, 320)
        hid_col[...] = column(hid_b[...], 8, HID, 512)
        out_col[...] = column(0.5 * out_w[...].astype(f32), 8, HID, 512)

    prepare()

    going_a = [copies_z(x, send_a, recv_a, ss_a, rs_a) for x in range(2)]
    for x in range(2):
        finish(going_y[x])
        got = mm(y_fwd[...], recv_y[x].reshape(Y, LW))
        for g in range(G):
            part_g = got[:, 128 * g : 128 * g + 128]
            ya[pl.ds(192 * x + g, MY, stride=8), :] = combine(
                part_g[0:MY], part_g[MY : 2 * MY], fwd_sign
            )
        send_a[:, x] = ya[192 * x : 192 * x + 192, :].astype(bf16).reshape(R, 24, 128)
        start(going_a[x])
        recv_a[zh, x] = send_a[zh, x]
    finish(going_a[0])
    finish(going_a[1])

    for p in range(R):
        xa[48 * p : 48 * p + 48, :] = recv_a[p].astype(f32).reshape(48, 128)
    used = [8 * a + g for a in range(3) for g in range(G)]
    data = jnp.concatenate(
        [xa[pl.ds(u, 16, stride=24), :] for u in used], axis=1
    ).astype(bf16)
    got = mm(x_fwd[e], data)
    for n, u in enumerate(used):
        part_u = got[:, 128 * n : 128 * n + 128]
        xb[pl.ds(u, MX, stride=24), :] = combine(part_u[0:MX], part_u[MX : 2 * MX], fwd_sign)
    for p in range(R):
        send_b[p] = jnp.concatenate(
            [xb[72 * p : 72 * p + 72, :], jnp.zeros((8, 128), f32)], axis=0
        ).astype(bf16)
    exchange(on_e, e, send_b, recv_b, ss_b, rs_b)
    total = recv_b[0].astype(f32)
    for p in range(1, R):
        total = total + recv_b[p].astype(f32)
    for n in range(3):
        spec_b[n] = total[24 * n : 24 * n + 24]

    def own_copy(src, n, dst, a, send_sem, recv_sem, device):
        return pltpu.make_async_remote_copy(
            src_ref=src.at[n],
            dst_ref=dst.at[a],
            send_sem=send_sem.at[n],
            recv_sem=recv_sem.at[a],
            device_id=(device, j),
            device_id_type=MESH,
        )

    def hand_over(src, dst, targets, origins, send_sem, recv_sem, local_sem):
        for n, (device, a) in enumerate(targets):

            @pl.when(device != i)
            def _():
                own_copy(src, n, dst, a, send_sem, recv_sem, device).start()

            @pl.when(device == i)
            def _():
                copy = pltpu.make_async_copy(src.at[n], dst.at[a], local_sem.at[n])
                copy.start()
                copy.wait()

        for n, (device, a) in enumerate(targets):

            @pl.when(device != i)
            def _():
                own_copy(src, n, dst, a, send_sem, recv_sem, device).wait_send()

        for a, (device, n) in enumerate(origins):

            @pl.when(device != i)
            def _():
                own_copy(src, n, dst, a, send_sem, recv_sem, device).wait_recv()

    hand_over(spec_b, spec_p, owners, sources, ss_p, rs_p, ls_p)

    own_k = one_hot(
        (iota((32, 128), 1) & 63 < 3 * PK)
        & (lax.rem(iota((32, 128), 1) & 63, PK) == iota((32, 128), 0))
    )
    for n in range(3):
        pairs[24 * n : 24 * n + 24, :] = spec_p[n]
    for p in range(9):
        for g in range(G):
            row = jnp.broadcast_to(pairs[8 * p + g : 8 * p + g + 1, :], (32, 128))
            amat[32 * p : 32 * p + 32, 128 * g : 128 * g + 128] = (row * own_k).astype(bf16)
    compact = mm(amat[...], gather[...]).astype(bf16)
    weights = wpad[...].astype(f32)
    straight = (mm(compact, widen[...]) * weights).astype(bf16)
    crossed = (mm(compact, widen_sw[...]) * weights).astype(bf16)
    mixed = (mm(straight, sum_re[...]) + mm(crossed, sum_im[...])).astype(bf16)
    wide = mm(mixed, spread[...])
    for p in range(9):
        for g in range(G):
            tile = wide[32 * p : 32 * p + 32, 128 * g : 128 * g + 128] * own_k
            mix[8 * p + g : 8 * p + g + 1, :] = jnp.sum(tile, axis=0, keepdims=True)
    for a in range(3):
        mix_p[a] = mix[24 * a : 24 * a + 24, :]

    hand_over(mix_p, mix_b, sources, owners, ss_q, rs_q, ls_q)
    send_c[...] = jnp.concatenate(
        [mix_b[0], mix_b[1], mix_b[2], jnp.zeros((8, 128), f32)], axis=0
    ).astype(bf16)
    exchange(on_e, e, send_c, recv_c, ss_c, rs_c, same=True)

    for p in range(R):
        xc[72 * p : 72 * p + 72, :] = recv_c[p].astype(f32)[0:72]
    data = jnp.concatenate(
        [xc[pl.ds(u, MX, stride=24), :] for u in used], axis=1
    ).astype(bf16)
    got = mm(x_bwd[e], data)
    for n, u in enumerate(used):
        part_u = got[:, 128 * n : 128 * n + 128]
        xd[pl.ds(u, 16, stride=24), :] = combine(part_u[0:16], part_u[16:32], -fwd_sign)
    going_d = [copies_z(x, send_d, recv_d, ss_d, rs_d) for x in range(2)]
    for x in range(2):
        for p in range(R):
            send_d[p, x] = xd[48 * p + 24 * x : 48 * p + 24 * x + 24, :].astype(bf16)
        start(going_d[x])
        recv_d[zh, x] = send_d[zh, x]

    going_e = [copies_y(x, send_e, recv_e, ss_e, rs_e) for x in range(2)]
    for x in range(2):
        finish(going_d[x])
        for p in range(R):
            xe[192 * x + 24 * p : 192 * x + 24 * p + 24, :] = recv_d[p, x].astype(f32)
        data = jnp.concatenate(
            [xe[pl.ds(192 * x + g, MY, stride=8), :] for g in range(G)], axis=1
        ).astype(bf16)
        got = mm(y_bwd[...], data)
        for g in range(G):
            part_g = got[:, 128 * g : 128 * g + 128]
            turned = combine(part_g[0:Y], part_g[Y : 2 * Y], -fwd_sign).astype(bf16)
            send_e[:, x, :, 128 * g : 128 * g + 128] = turned.reshape(R, 16, 128)
        start(going_e[x])
        recv_e[x, j] = send_e[j, x]

    @pl.loop(0, 2)
    def _(x):
        finish(copies_y(x, send_e, recv_e, ss_e, rs_e))
        for t in range(3):
            for g in range(G):
                held = [
                    recv_e[x, n, :, 128 * g : 128 * g + 128].astype(f32) if n < R else None
                    for n in range(3 * t, 3 * t + 3)
                ]
                for m in range(min(3, C - 3 * g)):
                    row = 16 * (3 * g + m)
                    s6[row : row + 16, 128 * t : 128 * t + 128] = regrouped(held, m).astype(bf16)
        for c in range(4):
            cut = slice(256 * c, 256 * c + 256)
            value = mm(s6[...], t_bwd[:, cut]) + mm(skip_k[...], field[x, :, cut])
            state = 0.5 * twice_gelu(value + skip_col[...])
            halves = state.reshape(C, 2, 8, 256)
            for h in range(2):
                inner = mm(hid_k[...], halves[:, h].reshape(160, 256).astype(bf16))
                weighed = twice_gelu(inner + hid_col[...]) * out_col[...]
                part[pl.ds(pl.multiple_of(x * 16, 16) + 8 * h, 8), cut] = jnp.sum(
                    weighed.reshape(HID, 8, 256), axis=0
                )

    for b in range(8):
        blk[pl.ds(b, 32, stride=8), :] = part[:, 128 * b : 128 * b + 128]

    send_f[...] = mm(perm[...], blk[...].astype(bf16)).astype(bf16).reshape(R, 32, 128)
    exchange(on_z, zh, send_f, recv_f, ss_f, rs_f)
    send_g[...] = mm(regroup[...], recv_f[...].reshape(256, 128)).astype(bf16).reshape(R, 32, 128)
    exchange(on_e, e, send_g, recv_g, ss_g, rs_g)
    owned = mm(pick[...], recv_g[...].reshape(256, 128))
    out[...] = owned[0:100].astype(bf16)


def scratch():
    v = pltpu.VMEM
    dma = pltpu.SemaphoreType.DMA
    buffers = [
        v((2, 320, 1024), bf16),
        v((9, PK, W2), bf16),
        v((1024, 384), bf16),
        v((384, 1024), bf16),
        v((48, 128), bf16),
        v((256, 24), bf16),
        v((R, 48, 16), bf16),
        v((R, 32, 24), bf16),
        v((LW, 128), bf16),
        v((128, LW), bf16),
        v((128, LW), bf16),
        v((128, LW), bf16),
        v((LW, 128), bf16),
        v((LW, 128), bf16),
        v((256, 256), bf16),
        v((R, 2, 16, LW), bf16),
        v((2, R, 16, LW), bf16),
        v((384, 128), f32),
        v((R, 2, 24, 128), bf16),
        v((R, 2, 24, 128), bf16),
        v((384, 128), f32),
        v((576, 128), f32),
        v((R, 80, 128), bf16),
        v((R, 80, 128), bf16),
        v((3, 24, 128), f32),
        v((3, 24, 128), f32),
        v((72, 128), f32),
        v((288, LW), bf16),
        v((72, 128), f32),
        v((3, 24, 128), f32),
        v((3, 24, 128), f32),
        v((80, 128), bf16),
        v((R, 80, 128), bf16),
        v((576, 128), f32),
        v((384, 128), f32),
        v((R, 2, 24, 128), bf16),
        v((R, 2, 24, 128), bf16),
        v((384, 128), f32),
        v((R, 2, 16, LW), bf16),
        v((2, R, 16, LW), bf16),
        v((320, 384), bf16),
        v((32, 1024), f32),
        v((256, 128), f32),
        v((R, 32, 128), bf16),
        v((R, 32, 128), bf16),
        v((R, 32, 128), bf16),
        v((R, 32, 128), bf16),
        v((288, LW), bf16),
        v((256, 256), bf16),
        v((128, 256), bf16),
        v((8, 256), jnp.int32),
        v((128, 128), f32),
        v((320, 320), bf16),
        v((512, 160), bf16),
        v((320, 256), f32),
        v((512, 256), f32),
        v((512, 256), f32),
    ]
    pairs_of = lambda count: [dma((count,)), dma((count,))]
    by_x = [dma((2, 7)), dma((2, 7))]
    sems = [dma((16,))] + by_x + by_x + pairs_of(7)
    sems += [dma((3,))] * 6 + pairs_of(7) + by_x + by_x + pairs_of(7) + pairs_of(7)
    return buffers + sems


def local(
    field,
    spectral_weight,
    skip_weight,
    skip_bias,
    hidden_weight,
    hidden_bias,
    out_weight,
    block_ids,
    send_rows,
    recv_rows,
):
    tables = [jnp.asarray(t) for t in constants()]
    args = [
        jnp.transpose(field, (0, 2, 1, 3)).reshape(2, 320, Z * T_SIZE),
        spectral_weight,
        skip_weight,
        skip_bias.reshape(1, C),
        hidden_weight,
        hidden_bias.reshape(1, HID),
        out_weight.reshape(1, HID),
        block_ids.reshape(1, 200),
        send_rows.reshape(1, 200),
        recv_rows.reshape(1, 100),
    ] + tables
    vmem = pl.BlockSpec(memory_space=pltpu.VMEM)
    hbm = pl.BlockSpec(memory_space=pl.ANY)
    result = pl.pallas_call(
        kernel,
        out_shape=jax.ShapeDtypeStruct((100, 128), bf16),
        in_specs=[hbm] * 2 + [vmem] * 8 + [hbm] * len(tables),
        out_specs=vmem,
        scratch_shapes=scratch(),
        compiler_params=pltpu.CompilerParams(
            collective_id=0, has_side_effects=True, vmem_limit_bytes=56 * 1024 * 1024
        ),
    )(*args)
    return result.reshape(1, 1, 100, 128)


def solution(mesh):
    placed = (
        P("gx", "gy", None, None),
        P("gx", "gy", None),
        P(),
        P(),
        P(),
        P(),
        P(),
        P("gx", "gy", None),
        P("gx", "gy", None),
        P("gx", "gy", None),
    )
    return jax.shard_map(
        local, mesh=mesh, in_specs=placed, out_specs=P("gx", "gy", None, None), check_vma=False
    )
```

```python
import functools
import math

import jax
import jax.numpy as jnp
import ml_dtypes
import numpy as np
from jax import lax
from jax.experimental import pallas as pl
from jax.experimental.pallas import tpu as pltpu
from jax.sharding import PartitionSpec as P

C = 20
HID = 64
MX = 24
MY = 24
MZ = 12
MT = 12
Z = 32
T_SIZE = 32
X = 128
Y = 128
KZT = MZ * MT
PK = 18
G = 7
R = 8
LW = G * 128
W2 = 2 * C * C
MESH = pl.DeviceIdType.MESH
f32 = jnp.float32
bf16 = jnp.bfloat16
GA = math.sqrt(2.0 / math.pi)
GB = GA * 0.044715


def constants():
    half = ml_dtypes.bfloat16

    def cos_sin(f, n, length):
        a = 2.0 * np.pi * ((f * n) % length) / length
        return np.cos(a), np.sin(a)

    q = np.arange(Z * T_SIZE)
    forward = np.zeros((Z * T_SIZE, 384))
    backward = np.zeros((384, Z * T_SIZE))
    for j in range(R):
        for k in range(PK):
            kk = PK * j + k
            fz, ft = kk % MZ - MZ // 2, kk // MZ - MT // 2
            a = 2.0 * np.pi * (((fz * (q % Z)) % Z) / Z + ((ft * (q // Z)) % T_SIZE) / T_SIZE)
            lane = 128 * (j // 3) + PK * (j % 3) + k
            forward[:, lane] = np.cos(a) / math.sqrt(Z * T_SIZE)
            forward[:, lane + 64] = -np.sin(a) / math.sqrt(Z * T_SIZE)
            backward[lane] = np.cos(a) / math.sqrt(MX * MY * KZT)
            backward[lane + 64] = -np.sin(a) / math.sqrt(MX * MY * KZT)
    fy = np.arange(MY) - MY // 2
    c, s = cos_sin(fy[:, None], np.arange(Y)[None, :], Y)
    y_fwd = np.concatenate([c, s], 0) / math.sqrt(Y)
    y_bwd = np.concatenate([c.T, s.T], 0)
    fx = np.arange(MX) - MX // 2
    x_fwd = np.zeros((R, 48, 16))
    x_bwd = np.zeros((R, 32, 24))
    for e in range(R):
        x = (16 * np.arange(8)[:, None] + 2 * e + np.arange(2)[None, :]).reshape(-1)
        c, s = cos_sin(fx[:, None], x[None, :], X)
        x_fwd[e] = np.concatenate([c, s], 0) / math.sqrt(X)
        x_bwd[e] = np.concatenate([c.T, s.T], 0)
    gather = np.zeros((LW, 128))
    spread = np.zeros((128, LW))
    for ch in range(C):
        for r in range(2):
            for k in range(PK):
                lane = 128 * (ch // 3) + 64 * r + PK * (ch % 3) + k
                gather[lane, 64 * r + ch] = 1.0
                spread[64 * r + ch, lane] = 1.0
    widen = np.zeros((128, LW))
    widen_swapped = np.zeros((128, LW))
    sum_re = np.zeros((LW, 128))
    sum_im = np.zeros((LW, 128))
    for r in range(2):
        for ch in range(C):
            for d in range(C):
                col = 400 * r + C * ch + d
                widen[64 * r + ch, col] = 1.0
                widen_swapped[64 * (1 - r) + ch, col] = 1.0
                sum_re[col, d] = 1.0 - 2.0 * r
                sum_im[col, 64 + d] = 1.0
    regroup = np.zeros((256, 256))
    for e in range(R):
        for zh in range(R):
            for n in range(4):
                regroup[32 * e + 4 * zh + n, 32 * zh + 4 * e + n] = 1.0
    tables = (
        forward, backward, y_fwd, y_bwd, x_fwd, x_bwd, gather, spread,
        widen, widen_swapped, sum_re, sum_im, regroup,
    )
    return [t.astype(half) for t in tables]


def mm(a, b):
    return lax.dot_general(a, b, (((1,), (0,)), ((), ())), preferred_element_type=f32)


def iota(shape, dim):
    return lax.broadcasted_iota(jnp.int32, shape, dim)


def one_hot(mask):
    return jnp.where(mask, 1.0, 0.0).astype(f32)


def twice_gelu(v):
    return v + v * jnp.tanh(v * (GA + GB * (v * v)))


def kernel(*refs):
    (
        field_in, weight_in, skip_w, skip_b, hid_w, hid_b, out_w, b_ids, s_rows, r_rows,
        t_fwd_in, t_bwd_in, y_fwd_in, y_bwd_in, x_fwd_in, x_bwd_in, gather_in, spread_in,
        widen_in, widen_sw_in, sum_re_in, sum_im_in, regroup_in,
        out,
        field, weight, t_fwd, t_bwd, y_fwd, y_bwd, x_fwd, x_bwd, gather, spread,
        widen, widen_sw, sum_re, sum_im, regroup,
        send_y, recv_y, ya, send_a, recv_a, xa, xb, send_b, recv_b,
        pairs, amat, mix, send_c, recv_c, xc, xd, send_d, recv_d, xe, send_e, recv_e,
        s6, part, blk, send_f, recv_f, send_g, recv_g, wpad, perm, pick, idrows, square, skip_k, hid_k,
        skip_col, hid_col, out_col,
        fetched,
        ss_y, rs_y, ss_a, rs_a, ss_b, rs_b, ss_p, rs_p, ls_p, ss_c, rs_c,
        ss_d, rs_d, ss_e, rs_e, ss_f, rs_f, ss_g, rs_g,
    ) = refs
    i = lax.axis_index("gx")
    j = lax.axis_index("gy")
    zh = lax.div(i, R)
    e = lax.rem(i, R)

    def turn(n, d):
        return lax.rem(n + d, R)

    def on_y(d):
        return turn(j, d), (i, turn(j, d))

    def on_z(d):
        return turn(zh, d), (R * turn(zh, d) + e, j)

    def on_e(d):
        return turn(e, d), (R * zh + turn(e, d), j)

    owners = []
    for n in range(3):
        first = MY * (3 * e + n) + 3 * zh
        owners.append((lax.div(first, 9), lax.div(lax.rem(first, 9), 3)))
    sources = []
    for a in range(3):
        first = 9 * i + 3 * a
        jx, jy = lax.div(first, MY), lax.rem(first, MY)
        sources.append((R * lax.div(jy, 3) + lax.div(jx, 3), lax.rem(jx, 3)))

    barrier = pltpu.get_barrier_semaphore()
    for near in (on_y, on_z, on_e):
        for d in range(1, R):
            pl.semaphore_signal(barrier, inc=1, device_id=near(d)[1], device_id_type=MESH)
    for other, _ in owners + sources:

        @pl.when(other != i)
        def _():
            pl.semaphore_signal(barrier, inc=1, device_id=(other, j), device_id_type=MESH)

    fetch = []
    wanted = [
        (field_in.at[0], field.at[0]), (t_fwd_in, t_fwd), (field_in.at[1], field.at[1]),
        (y_fwd_in, y_fwd), (x_fwd_in, x_fwd), (gather_in, gather),
        (widen_in, widen), (widen_sw_in, widen_sw), (sum_re_in, sum_re), (sum_im_in, sum_im),
        (spread_in, spread), (x_bwd_in, x_bwd), (y_bwd_in, y_bwd), (t_bwd_in, t_bwd),
        (regroup_in, regroup),
    ]
    for n, (source, target) in enumerate(wanted):
        fetch.append(pltpu.make_async_copy(source, target, fetched.at[n]))
        fetch[n].start()

    sent = []

    def await_bytes(view, sem):
        pltpu.make_async_copy(view, view, sem).wait()

    def start(near, me, send, recv, send_sem, recv_sem):
        for d in range(1, R):
            peer, device = near(d)
            pltpu.make_async_remote_copy(
                src_ref=send(peer),
                dst_ref=recv(me),
                send_sem=send_sem,
                recv_sem=recv_sem,
                device_id=device,
                device_id_type=MESH,
            ).start()

    def exchange(near, me, send, recv, send_sem, recv_sem, same=False):
        start(
            near, me, (lambda p: send) if same else (lambda p: send.at[p]), lambda p: recv.at[p],
            send_sem.at[0], recv_sem.at[0],
        )
        recv[me] = send[...] if same else send[me]
        seven = recv.at[pl.ds(0, R - 1)]
        sent.append((seven, send_sem.at[0]))
        await_bytes(seven, recv_sem.at[0])

    def start_y(x, send, recv, send_sem, recv_sem):
        start(
            on_y, j, lambda p: send.at[p, x], lambda p: recv.at[x, p], send_sem.at[x], recv_sem.at[x]
        )
        recv[x, j] = send[j, x]
        sent.append((recv.at[x, pl.ds(0, R - 1)], send_sem.at[x]))

    def finish_y(x, recv, recv_sem):
        await_bytes(recv.at[x, pl.ds(0, R - 1)], recv_sem.at[x])

    def start_z(x, send, recv, send_sem, recv_sem):
        start(
            on_z, zh, lambda p: send.at[p, x], lambda p: recv.at[x, p], send_sem.at[x], recv_sem.at[x]
        )
        recv[x, zh] = send[zh, x]
        sent.append((recv.at[x, pl.ds(0, R - 1)], send_sem.at[x]))

    def weights_copy(n, a, device):
        return pltpu.make_async_remote_copy(
            src_ref=weight_in.at[n],
            dst_ref=weight.at[a],
            send_sem=ss_p.at[n],
            recv_sem=rs_p.at[a],
            device_id=(device, j),
            device_id_type=MESH,
        )

    def weights_kept(n, a):
        return pltpu.make_async_copy(weight_in.at[n], weight.at[a], ls_p.at[n])

    def start_weights():
        for n, (device, a) in enumerate(sources):

            @pl.when(device != i)
            def _():
                weights_copy(n, a, device).start()

            @pl.when(device == i)
            def _():
                weights_kept(n, a).start()

    def finish_weights():
        for n, (device, a) in enumerate(sources):

            @pl.when(device == i)
            def _():
                weights_kept(n, a).wait()

        for a, (device, n) in enumerate(owners):

            @pl.when(device != i)
            def _():
                weights_copy(n, a, device).wait_recv()

    def finish_sends():
        for n, (device, a) in enumerate(sources):

            @pl.when(device != i)
            def _():
                weights_copy(n, a, device).wait_send()

        for view, sem in sent:
            await_bytes(view, sem)

    lane = iota((1, 128), 1)
    in_half = lane & 63
    piece = [
        (in_half >= PK * m) & (in_half < PK * (m + 1)) for m in range(3)
    ]
    fwd_sign = jnp.where(lane < 64, 1.0, -1.0)

    def regrouped(held, n):
        total = jnp.zeros(held[0].shape, f32)
        for m, rows in enumerate(held):
            if rows is None:
                continue
            shift = (PK * (m - n)) % 128
            moved = rows if shift == 0 else pltpu.roll(rows, shift, 1)
            total = jnp.where(piece[m], moved, total)
        return total

    def combine(cosines, sines, sign):
        return cosines + sign * pltpu.roll(sines, 64, 1)

    def along_zt(x):
        got = mm(field[x], t_fwd[...])
        for g in range(G):
            for t in range(3):
                held = [
                    got[16 * c : 16 * c + 16, 128 * t : 128 * t + 128] if c < C else None
                    for c in range(3 * g, 3 * g + 3)
                ]
                for n in range(min(3, R - 3 * t)):
                    send_y[3 * t + n, x, :, 128 * g : 128 * g + 128] = (
                        regrouped(held, n).astype(bf16)
                    )

    fetch[0].wait()
    fetch[1].wait()
    along_zt(0)

    expected = 3 * (R - 1)
    for other, _ in owners + sources:
        expected = expected + jnp.where(other != i, 1, 0)
    pl.semaphore_wait(barrier, expected)

    start_y(0, send_y, recv_y, ss_y, rs_y)
    start_weights()
    fetch[2].wait()
    along_zt(1)
    start_y(1, send_y, recv_y, ss_y, rs_y)
    for copy in fetch[3:]:
        copy.wait()

    def prepare():
        wpad[...] = jnp.zeros((288, LW), bf16)
        ya[...] = jnp.zeros((384, 128), f32)
        xb[...] = jnp.zeros((576, 128), f32)
        xd[...] = jnp.zeros((384, 128), f32)
        mix[...] = jnp.zeros((72, 128), f32)
        idrows[...] = jnp.full((8, 256), -1, jnp.int32)
        idrows[0:1, 0:200] = b_ids[...]
        idrows[1:2, 0:200] = s_rows[...]
        idrows[2:3, 0:100] = r_rows[...]
        row = iota((256, 256), 0)
        by_block = one_hot(row == idrows[0:1, :]).astype(bf16)
        by_row = one_hot(row == idrows[1:2, :]).astype(bf16)
        perm[...] = lax.dot_general(
            by_row, by_block, (((1,), (1,)), ((), ())), preferred_element_type=f32
        ).astype(bf16)
        place = iota((256, 128), 0)
        name = ((place >> 2) & 7) * 32 + (place >> 5) * 4 + (place & 3)
        pick[...] = one_hot(name == idrows[2:3, 0:128]).T.astype(bf16)
        def spread_map(values, rows, cols, places):
            shift = places.bit_length() - 1
            left = one_hot((iota((rows, 128), 0) >> shift) == iota((rows, 128), 1)).astype(bf16)
            right = one_hot((iota((128, cols), 1) >> shift) == iota((128, cols), 0)).astype(bf16)
            wide = mm(mm(left, values.T.astype(bf16)).astype(bf16), right)
            same = (iota((rows, cols), 0) & (places - 1)) == (iota((rows, cols), 1) & (places - 1))
            return jnp.where(same, wide, 0.0).astype(bf16)

        square[...] = jnp.zeros((128, 128), f32)
        square[0:C, 0:C] = skip_w[...].astype(f32)
        skip_k[...] = spread_map(square[...], 320, 320, 16)
        square[0:C, 0:HID] = hid_w[...].astype(f32)
        hid_k[...] = spread_map(square[...], 512, 160, 8)

        def column(values, places, width, rows):
            shift = places.bit_length() - 1
            at = one_hot((iota((rows, width), 0) >> shift) == iota((rows, width), 1))
            return jnp.broadcast_to(
                jnp.sum(at * values, axis=1, keepdims=True), (rows, 256)
            )

        skip_col[...] = column(skip_b[...], 16, C, 320)
        hid_col[...] = column(hid_b[...], 8, HID, 512)
        out_col[...] = column(0.5 * out_w[...].astype(f32), 8, HID, 512)

    prepare()

    for x in range(2):
        finish_y(x, recv_y, rs_y)
        got = mm(y_fwd[...], recv_y[x].reshape(Y, LW))
        for g in range(G):
            part_g = got[:, 128 * g : 128 * g + 128]
            ya[pl.ds(192 * x + g, MY, stride=8), :] = combine(
                part_g[0:MY], part_g[MY : 2 * MY], fwd_sign
            )
        send_a[:, x] = ya[192 * x : 192 * x + 192, :].astype(bf16).reshape(R, 24, 128)
        start_z(x, send_a, recv_a, ss_a, rs_a)
    for x in range(2):
        finish_y(x, recv_a, rs_a)

    for p in range(R):
        for x in range(2):
            xa[48 * p + 24 * x : 48 * p + 24 * x + 24, :] = recv_a[x, p].astype(f32)
    used = [8 * a + g for a in range(3) for g in range(G)]
    data = jnp.concatenate(
        [xa[pl.ds(u, 16, stride=24), :] for u in used], axis=1
    ).astype(bf16)
    got = mm(x_fwd[e], data)
    for n, u in enumerate(used):
        part_u = got[:, 128 * n : 128 * n + 128]
        xb[pl.ds(u, MX, stride=24), :] = combine(part_u[0:MX], part_u[MX : 2 * MX], fwd_sign)
    for p in range(R):
        send_b[p] = xb[72 * p : 72 * p + 72, :].astype(bf16)
    exchange(on_e, e, send_b, recv_b, ss_b, rs_b)
    total = recv_b[0].astype(f32)
    for p in range(1, R):
        total = total + recv_b[p].astype(f32)
    pairs[...] = total
    finish_weights()
    for p in range(9):
        wpad[32 * p : 32 * p + PK, 0:W2] = weight[p // 3, p % 3]

    own_k = one_hot(
        (iota((32, 128), 1) & 63 < 3 * PK)
        & (lax.rem(iota((32, 128), 1) & 63, PK) == iota((32, 128), 0))
    )
    for p in range(9):
        for g in range(G):
            row = jnp.broadcast_to(pairs[8 * p + g : 8 * p + g + 1, :], (32, 128))
            amat[32 * p : 32 * p + 32, 128 * g : 128 * g + 128] = (row * own_k).astype(bf16)
    compact = mm(amat[...], gather[...]).astype(bf16)
    weights = wpad[...].astype(f32)
    straight = (mm(compact, widen[...]) * weights).astype(bf16)
    crossed = (mm(compact, widen_sw[...]) * weights).astype(bf16)
    mixed = (mm(straight, sum_re[...]) + mm(crossed, sum_im[...])).astype(bf16)
    wide = mm(mixed, spread[...])
    for p in range(9):
        for g in range(G):
            tile = wide[32 * p : 32 * p + 32, 128 * g : 128 * g + 128] * own_k
            mix[8 * p + g : 8 * p + g + 1, :] = jnp.sum(tile, axis=0, keepdims=True)
    send_c[...] = mix[...].astype(bf16)
    exchange(on_e, e, send_c, recv_c, ss_c, rs_c, same=True)

    for p in range(R):
        xc[72 * p : 72 * p + 72, :] = recv_c[p].astype(f32)
    data = jnp.concatenate(
        [xc[pl.ds(u, MX, stride=24), :] for u in used], axis=1
    ).astype(bf16)
    got = mm(x_bwd[e], data)
    for n, u in enumerate(used):
        part_u = got[:, 128 * n : 128 * n + 128]
        xd[pl.ds(u, 16, stride=24), :] = combine(part_u[0:16], part_u[16:32], -fwd_sign)
    for x in range(2):
        for p in range(R):
            send_d[p, x] = xd[48 * p + 24 * x : 48 * p + 24 * x + 24, :].astype(bf16)
        start_z(x, send_d, recv_d, ss_d, rs_d)

    for x in range(2):
        finish_y(x, recv_d, rs_d)
        for p in range(R):
            xe[192 * x + 24 * p : 192 * x + 24 * p + 24, :] = recv_d[x, p].astype(f32)
        data = jnp.concatenate(
            [xe[pl.ds(192 * x + g, MY, stride=8), :] for g in range(G)], axis=1
        ).astype(bf16)
        got = mm(y_bwd[...], data)
        for g in range(G):
            part_g = got[:, 128 * g : 128 * g + 128]
            turned = combine(part_g[0:Y], part_g[Y : 2 * Y], -fwd_sign).astype(bf16)
            send_e[:, x, :, 128 * g : 128 * g + 128] = turned.reshape(R, 16, 128)
        start_y(x, send_e, recv_e, ss_e, rs_e)

    @pl.loop(0, 2)
    def _(x):
        finish_y(x, recv_e, rs_e)
        for t in range(3):
            for g in range(G):
                held = [
                    recv_e[x, n, :, 128 * g : 128 * g + 128].astype(f32) if n < R else None
                    for n in range(3 * t, 3 * t + 3)
                ]
                for m in range(min(3, C - 3 * g)):
                    row = 16 * (3 * g + m)
                    s6[row : row + 16, 128 * t : 128 * t + 128] = regrouped(held, m).astype(bf16)
        for c in range(4):
            cut = slice(256 * c, 256 * c + 256)
            value = mm(s6[...], t_bwd[:, cut]) + mm(skip_k[...], field[x, :, cut])
            state = 0.5 * twice_gelu(value + skip_col[...])
            halves = state.reshape(C, 2, 8, 256)
            for h in range(2):
                inner = mm(hid_k[...], halves[:, h].reshape(160, 256).astype(bf16))
                weighed = twice_gelu(inner + hid_col[...]) * out_col[...]
                part[pl.ds(pl.multiple_of(x * 16, 16) + 8 * h, 8), cut] = jnp.sum(
                    weighed.reshape(HID, 8, 256), axis=0
                )

    for b in range(8):
        blk[pl.ds(b, 32, stride=8), :] = part[:, 128 * b : 128 * b + 128]

    send_f[...] = mm(perm[...], blk[...].astype(bf16)).astype(bf16).reshape(R, 32, 128)
    exchange(on_z, zh, send_f, recv_f, ss_f, rs_f)
    send_g[...] = mm(regroup[...], recv_f[...].reshape(256, 128)).astype(bf16).reshape(R, 32, 128)
    exchange(on_e, e, send_g, recv_g, ss_g, rs_g)
    owned = mm(pick[...], recv_g[...].reshape(256, 128))
    out[...] = owned[0:100].astype(bf16)
    finish_sends()


def scratch():
    v = pltpu.VMEM
    dma = pltpu.SemaphoreType.DMA
    buffers = [
        v((2, 320, 1024), bf16),
        v((3, 3, PK, W2), bf16),
        v((1024, 384), bf16),
        v((384, 1024), bf16),
        v((48, 128), bf16),
        v((256, 24), bf16),
        v((R, 48, 16), bf16),
        v((R, 32, 24), bf16),
        v((LW, 128), bf16),
        v((128, LW), bf16),
        v((128, LW), bf16),
        v((128, LW), bf16),
        v((LW, 128), bf16),
        v((LW, 128), bf16),
        v((256, 256), bf16),
        v((R, 2, 16, LW), bf16),
        v((2, R, 16, LW), bf16),
        v((384, 128), f32),
        v((R, 2, 24, 128), bf16),
        v((2, R, 24, 128), bf16),
        v((384, 128), f32),
        v((576, 128), f32),
        v((R, 72, 128), bf16),
        v((R, 72, 128), bf16),
        v((72, 128), f32),
        v((288, LW), bf16),
        v((72, 128), f32),
        v((72, 128), bf16),
        v((R, 72, 128), bf16),
        v((576, 128), f32),
        v((384, 128), f32),
        v((R, 2, 24, 128), bf16),
        v((2, R, 24, 128), bf16),
        v((384, 128), f32),
        v((R, 2, 16, LW), bf16),
        v((2, R, 16, LW), bf16),
        v((320, 384), bf16),
        v((32, 1024), f32),
        v((256, 128), f32),
        v((R, 32, 128), bf16),
        v((R, 32, 128), bf16),
        v((R, 32, 128), bf16),
        v((R, 32, 128), bf16),
        v((288, LW), bf16),
        v((256, 256), bf16),
        v((128, 256), bf16),
        v((8, 256), jnp.int32),
        v((128, 128), f32),
        v((320, 320), bf16),
        v((512, 160), bf16),
        v((320, 256), f32),
        v((512, 256), f32),
        v((512, 256), f32),
    ]
    one, by_x = [dma((1,))] * 2, [dma((2,))] * 2
    sems = [dma((15,))] + by_x + by_x + one + [dma((3,))] * 3 + one + by_x + by_x + one + one
    return buffers + sems


def local(
    field,
    spectral_weight,
    skip_weight,
    skip_bias,
    hidden_weight,
    hidden_bias,
    out_weight,
    block_ids,
    send_rows,
    recv_rows,
):
    tables = [jnp.asarray(t) for t in constants()]
    args = [
        jnp.transpose(field, (0, 2, 1, 3)).reshape(2, 320, Z * T_SIZE),
        spectral_weight.reshape(3, 3, PK, W2),
        skip_weight,
        skip_bias.reshape(1, C),
        hidden_weight,
        hidden_bias.reshape(1, HID),
        out_weight.reshape(1, HID),
        block_ids.reshape(1, 200),
        send_rows.reshape(1, 200),
        recv_rows.reshape(1, 100),
    ] + tables
    vmem = pl.BlockSpec(memory_space=pltpu.VMEM)
    hbm = pl.BlockSpec(memory_space=pl.ANY)
    result = pl.pallas_call(
        kernel,
        out_shape=jax.ShapeDtypeStruct((100, 128), bf16),
        in_specs=[hbm] * 2 + [vmem] * 8 + [hbm] * len(tables),
        out_specs=vmem,
        scratch_shapes=scratch(),
        compiler_params=pltpu.CompilerParams(
            collective_id=0, has_side_effects=True, vmem_limit_bytes=56 * 1024 * 1024
        ),
    )(*args)
    return result.reshape(1, 1, 100, 128)


def solution(mesh):
    placed = (
        P("gx", "gy", None, None),
        P("gx", "gy", None),
        P(),
        P(),
        P(),
        P(),
        P(),
        P("gx", "gy", None),
        P("gx", "gy", None),
        P("gx", "gy", None),
    )
    return jax.shard_map(
        local, mesh=mesh, in_specs=placed, out_specs=P("gx", "gy", None, None), check_vma=False
    )
```

```python
import functools
import math

import jax
import jax.numpy as jnp
import ml_dtypes
import numpy as np
from jax import lax
from jax.experimental import pallas as pl
from jax.experimental.pallas import tpu as pltpu
from jax.sharding import PartitionSpec as P

C = 20
HID = 64
MX = 24
MY = 24
MZ = 12
MT = 12
Z = 32
T_SIZE = 32
X = 128
Y = 128
KZT = MZ * MT
PK = 18
G = 7
R = 8
LW = G * 128
W2 = 2 * C * C
MESH = pl.DeviceIdType.MESH
f32 = jnp.float32
bf16 = jnp.bfloat16
GA = math.sqrt(2.0 / math.pi)
GB = GA * 0.044715


def constants():
    half = ml_dtypes.bfloat16

    def cos_sin(f, n, length):
        a = 2.0 * np.pi * ((f * n) % length) / length
        return np.cos(a), np.sin(a)

    q = np.arange(Z * T_SIZE)
    forward = np.zeros((Z * T_SIZE, 384))
    backward = np.zeros((384, Z * T_SIZE))
    for j in range(R):
        for k in range(PK):
            kk = PK * j + k
            fz, ft = kk % MZ - MZ // 2, kk // MZ - MT // 2
            a = 2.0 * np.pi * (((fz * (q % Z)) % Z) / Z + ((ft * (q // Z)) % T_SIZE) / T_SIZE)
            lane = 128 * (j // 3) + PK * (j % 3) + k
            forward[:, lane] = np.cos(a) / math.sqrt(Z * T_SIZE)
            forward[:, lane + 64] = -np.sin(a) / math.sqrt(Z * T_SIZE)
            backward[lane] = np.cos(a) / math.sqrt(MX * MY * KZT)
            backward[lane + 64] = -np.sin(a) / math.sqrt(MX * MY * KZT)
    fy = np.arange(MY) - MY // 2
    c, s = cos_sin(fy[:, None], np.arange(Y)[None, :], Y)
    y_fwd = np.concatenate([c, s], 0) / math.sqrt(Y)
    y_bwd = np.concatenate([c.T, s.T], 0)
    fx = np.arange(MX) - MX // 2
    x_fwd = np.zeros((R, 48, 16))
    x_bwd = np.zeros((R, 32, 24))
    for e in range(R):
        x = (16 * np.arange(8)[:, None] + 2 * e + np.arange(2)[None, :]).reshape(-1)
        c, s = cos_sin(fx[:, None], x[None, :], X)
        x_fwd[e] = np.concatenate([c, s], 0) / math.sqrt(X)
        x_bwd[e] = np.concatenate([c.T, s.T], 0)
    gather = np.zeros((LW, 128))
    spread = np.zeros((128, LW))
    for ch in range(C):
        for r in range(2):
            for k in range(PK):
                lane = 128 * (ch // 3) + 64 * r + PK * (ch % 3) + k
                gather[lane, 64 * r + ch] = 1.0
                spread[64 * r + ch, lane] = 1.0
    widen = np.zeros((128, LW))
    widen_swapped = np.zeros((128, LW))
    sum_re = np.zeros((LW, 128))
    sum_im = np.zeros((LW, 128))
    for r in range(2):
        for ch in range(C):
            for d in range(C):
                col = 400 * r + C * ch + d
                widen[64 * r + ch, col] = 1.0
                widen_swapped[64 * (1 - r) + ch, col] = 1.0
                sum_re[col, d] = 1.0 - 2.0 * r
                sum_im[col, 64 + d] = 1.0
    regroup = np.zeros((256, 256))
    for e in range(R):
        for zh in range(R):
            for n in range(4):
                regroup[32 * e + 4 * zh + n, 32 * zh + 4 * e + n] = 1.0
    tables = (
        forward, backward, y_fwd, y_bwd, x_fwd, x_bwd, gather, spread,
        widen, widen_swapped, sum_re, sum_im, regroup,
    )
    return [t.astype(half) for t in tables]


def mm(a, b):
    return lax.dot_general(a, b, (((1,), (0,)), ((), ())), preferred_element_type=f32)


def iota(shape, dim):
    return lax.broadcasted_iota(jnp.int32, shape, dim)


def one_hot(mask):
    return jnp.where(mask, 1.0, 0.0).astype(f32)


def twice_gelu(v):
    return v + v * jnp.tanh(v * (GA + GB * (v * v)))


def kernel(*refs):
    (
        field_in, weight_in, skip_w, skip_b, hid_w, hid_b, out_w, b_ids, s_rows, r_rows,
        t_fwd_in, t_bwd_in, y_fwd_in, y_bwd_in, x_fwd_in, x_bwd_in, gather_in, spread_in,
        widen_in, widen_sw_in, sum_re_in, sum_im_in, regroup_in,
        out,
        field, weight, t_fwd, t_bwd, y_fwd, y_bwd, x_fwd, x_bwd, gather, spread,
        widen, widen_sw, sum_re, sum_im, regroup,
        send_y, recv_y, ya, send_a, recv_a, xa, xb, send_b, recv_b,
        pairs, amat, mix, send_c, recv_c, xc, xd, send_d, recv_d, xe, send_e, recv_e,
        s6, s1, wide, part, blk, send_f, recv_f, send_g, recv_g, wpad, perm, pick, idrows, square, skip_k, hid_k,
        skip_col, hid_col, out_col,
        fetched,
        ss_y, rs_y, ss_a, rs_a, ss_b, rs_b, ss_p, rs_p, ls_p, ss_c, rs_c,
        ss_d, rs_d, ss_e, rs_e, ss_f, rs_f, ss_g, rs_g,
    ) = refs
    i = lax.axis_index("gx")
    j = lax.axis_index("gy")
    zh = lax.div(i, R)
    e = lax.rem(i, R)

    def turn(n, d):
        return lax.rem(n + d, R)

    def on_y(d):
        return turn(j, d), (i, turn(j, d))

    def on_z(d):
        return turn(zh, d), (R * turn(zh, d) + e, j)

    def on_e(d):
        return turn(e, d), (R * zh + turn(e, d), j)

    owners = []
    for n in range(3):
        first = MY * (3 * e + n) + 3 * zh
        owners.append((lax.div(first, 9), lax.div(lax.rem(first, 9), 3)))
    sources = []
    for a in range(3):
        first = 9 * i + 3 * a
        jx, jy = lax.div(first, MY), lax.rem(first, MY)
        sources.append((R * lax.div(jy, 3) + lax.div(jx, 3), lax.rem(jx, 3)))

    barrier = pltpu.get_barrier_semaphore()
    for near in (on_y, on_z, on_e):
        for d in range(1, R):
            pl.semaphore_signal(barrier, inc=1, device_id=near(d)[1], device_id_type=MESH)
    for other, _ in owners + sources:

        @pl.when(other != i)
        def _():
            pl.semaphore_signal(barrier, inc=1, device_id=(other, j), device_id_type=MESH)

    fetch = []
    wanted = [
        (t_fwd_in, t_fwd), (field_in.at[0], field.at[0]), (field_in.at[1], field.at[1]),
        (y_fwd_in, y_fwd), (x_fwd_in, x_fwd), (gather_in, gather),
        (widen_in, widen), (widen_sw_in, widen_sw), (sum_re_in, sum_re), (sum_im_in, sum_im),
        (spread_in, spread), (x_bwd_in, x_bwd), (y_bwd_in, y_bwd), (t_bwd_in, t_bwd),
        (regroup_in, regroup),
    ]
    for n, (source, target) in enumerate(wanted):
        fetch.append(pltpu.make_async_copy(source, target, fetched.at[n]))
        fetch[n].start()

    sent = []

    def await_bytes(view, sem):
        pltpu.make_async_copy(view, view, sem).wait()

    def start(near, me, send, recv, send_sem, recv_sem):
        for d in range(1, R):
            peer, device = near(d)
            pltpu.make_async_remote_copy(
                src_ref=send(peer),
                dst_ref=recv(me),
                send_sem=send_sem,
                recv_sem=recv_sem,
                device_id=device,
                device_id_type=MESH,
            ).start()

    def exchange(near, me, send, recv, send_sem, recv_sem, same=False, beside=None):
        start(
            near, me, (lambda p: send) if same else (lambda p: send.at[p]), lambda p: recv.at[p],
            send_sem.at[0], recv_sem.at[0],
        )
        recv[me] = send[...] if same else send[me]
        seven = recv.at[pl.ds(0, R - 1)]
        sent.append((seven, send_sem.at[0]))
        if beside is not None:
            beside()
        await_bytes(seven, recv_sem.at[0])

    def start_y(x, send, recv, send_sem, recv_sem):
        start(
            on_y, j, lambda p: send.at[p, x], lambda p: recv.at[x, p], send_sem.at[x], recv_sem.at[x]
        )
        recv[x, j] = send[j, x]

    def finish_y(x, recv, recv_sem):
        await_bytes(recv.at[x, pl.ds(0, R - 1)], recv_sem.at[x])

    def start_z(x, send, recv, send_sem, recv_sem):
        start(
            on_z, zh, lambda p: send.at[p, x], lambda p: recv.at[x, p], send_sem.at[x], recv_sem.at[x]
        )
        recv[x, zh] = send[zh, x]

    def weights_copy(n, a, device):
        return pltpu.make_async_remote_copy(
            src_ref=weight_in.at[n],
            dst_ref=weight.at[a],
            send_sem=ss_p.at[n],
            recv_sem=rs_p.at[a],
            device_id=(device, j),
            device_id_type=MESH,
        )

    def weights_kept(n, a):
        return pltpu.make_async_copy(weight_in.at[n], weight.at[a], ls_p.at[n])

    def start_weights():
        for n, (device, a) in enumerate(sources):

            @pl.when(device != i)
            def _():
                weights_copy(n, a, device).start()

            @pl.when(device == i)
            def _():
                weights_kept(n, a).start()

    def finish_weights():
        for n, (device, a) in enumerate(sources):

            @pl.when(device == i)
            def _():
                weights_kept(n, a).wait()

        for a, (device, n) in enumerate(owners):

            @pl.when(device != i)
            def _():
                weights_copy(n, a, device).wait_recv()

    def finish_sends():
        for n, (device, a) in enumerate(sources):

            @pl.when(device != i)
            def _():
                weights_copy(n, a, device).wait_send()

        for view, sem in sent:
            await_bytes(view, sem)
        for recv, send_sem in ((recv_y, ss_y), (recv_a, ss_a), (recv_d, ss_d), (recv_e, ss_e)):
            for x in range(2):
                await_bytes(recv.at[x, pl.ds(0, R - 1)], send_sem.at[x])

    lane = iota((1, 128), 1)
    in_half = lane & 63
    piece = [
        (in_half >= PK * m) & (in_half < PK * (m + 1)) for m in range(3)
    ]
    fwd_sign = jnp.where(lane < 64, 1.0, -1.0)

    def regrouped(held, n):
        total = jnp.zeros(held[0].shape, f32)
        for m, rows in enumerate(held):
            if rows is None:
                continue
            shift = (PK * (m - n)) % 128
            moved = rows if shift == 0 else pltpu.roll(rows, shift, 1)
            total = jnp.where(piece[m], moved, total)
        return total

    def combine(cosines, sines, sign):
        return cosines + sign * pltpu.roll(sines, 64, 1)

    expected = 3 * (R - 1)
    for other, _ in owners + sources:
        expected = expected + jnp.where(other != i, 1, 0)

    s1[320:336, :] = jnp.zeros((16, 384), f32)
    fetch[0].wait()

    @pl.loop(0, 2)
    def _(x):
        pltpu.make_async_copy(field_in.at[x], field.at[x], fetched.at[1 + x]).wait()
        s1[0:320, :] = mm(field[x], t_fwd[...])

        @pl.loop(0, G)
        def _(g):
            lanes = pl.ds(pl.multiple_of(128 * g, 128), 128)
            for t in range(3):
                held = [
                    s1[pl.ds(pl.multiple_of(48 * g + 16 * m, 16), 16), 128 * t : 128 * t + 128]
                    for m in range(3)
                ]
                for n in range(min(3, R - 3 * t)):
                    send_y[3 * t + n, x, :, lanes] = regrouped(held, n).astype(bf16)

        @pl.when(x == 0)
        def _():
            pl.semaphore_wait(barrier, expected)

        start_y(x, send_y, recv_y, ss_y, rs_y)

        @pl.when(x == 0)
        def _():
            start_weights()

    for copy in fetch[3:]:
        copy.wait()

    def spread_map(values, rows, cols, places):
        shift = places.bit_length() - 1
        left = one_hot((iota((rows, 128), 0) >> shift) == iota((rows, 128), 1)).astype(bf16)
        right = one_hot((iota((128, cols), 1) >> shift) == iota((128, cols), 0)).astype(bf16)
        wide = mm(mm(left, values.T.astype(bf16)).astype(bf16), right)
        same = (iota((rows, cols), 0) & (places - 1)) == (iota((rows, cols), 1) & (places - 1))
        return jnp.where(same, wide, 0.0).astype(bf16)

    def column(values, places, width, rows):
        shift = places.bit_length() - 1
        at = one_hot((iota((rows, width), 0) >> shift) == iota((rows, width), 1))
        return jnp.broadcast_to(jnp.sum(at * values, axis=1, keepdims=True), (rows, 128))

    def prepare_clear():
        wpad[...] = jnp.zeros((288, LW), bf16)
        ya[...] = jnp.zeros((192, 128), f32)
        xb[...] = jnp.zeros((576, 128), f32)
        xd[...] = jnp.zeros((384, 128), f32)

    def prepare_rows():
        idrows[...] = jnp.full((8, 256), -1, jnp.int32)
        idrows[0:1, 0:200] = b_ids[...]
        idrows[1:2, 0:200] = s_rows[...]
        idrows[2:3, 0:100] = r_rows[...]
        row = iota((256, 256), 0)
        by_block = one_hot(row == idrows[0:1, :]).astype(bf16)
        by_row = one_hot(row == idrows[1:2, :]).astype(bf16)
        perm[...] = lax.dot_general(
            by_row, by_block, (((1,), (1,)), ((), ())), preferred_element_type=f32
        ).astype(bf16)
        place = iota((256, 128), 0)
        name = ((place >> 2) & 7) * 32 + (place >> 5) * 4 + (place & 3)
        pick[...] = one_hot(name == idrows[2:3, 0:128]).T.astype(bf16)

    def prepare_skip():
        square[...] = jnp.zeros((128, 128), f32)
        square[0:C, 0:C] = skip_w[...].astype(f32)
        skip_k[...] = spread_map(square[...], 320, 320, 16)
        skip_col[...] = column(skip_b[...], 16, C, 320)

    def prepare_hidden():
        square[...] = jnp.zeros((128, 128), f32)
        square[0:C, 0:HID] = hid_w[...].astype(f32)
        hid_k[...] = spread_map(square[...], 512, 160, 8)
        hid_col[...] = column(hid_b[...], 8, HID, 512)

    def prepare_out():
        out_col[...] = column(0.5 * out_w[...].astype(f32), 8, HID, 512)

    prepare_clear()
    prepare_skip()

    @pl.loop(0, 2)
    def _(x):
        finish_y(x, recv_y, rs_y)
        got = mm(y_fwd[...], recv_y[x].reshape(Y, LW))
        for g in range(G):
            part_g = got[:, 128 * g : 128 * g + 128]
            ya[pl.ds(g, MY, stride=8), :] = combine(
                part_g[0:MY], part_g[MY : 2 * MY], fwd_sign
            )
        send_a[:, x] = ya[...].astype(bf16).reshape(R, 24, 128)
        start_z(x, send_a, recv_a, ss_a, rs_a)

    prepare_hidden()
    for x in range(2):
        finish_y(x, recv_a, rs_a)

    for p in range(R):
        for x in range(2):
            xa[48 * p + 24 * x : 48 * p + 24 * x + 24, :] = recv_a[x, p].astype(f32)
    used = [8 * a + g for a in range(3) for g in range(G)]
    data = jnp.concatenate(
        [xa[pl.ds(u, 16, stride=24), :] for u in used], axis=1
    ).astype(bf16)
    got = mm(x_fwd[e], data)
    for n, u in enumerate(used):
        part_u = got[:, 128 * n : 128 * n + 128]
        xb[pl.ds(u, MX, stride=24), :] = combine(part_u[0:MX], part_u[MX : 2 * MX], fwd_sign)
    for p in range(R):
        send_b[p] = xb[72 * p : 72 * p + 72, :].astype(bf16)
    exchange(on_e, e, send_b, recv_b, ss_b, rs_b, beside=prepare_out)
    total = recv_b[0].astype(f32)
    for p in range(1, R):
        total = total + recv_b[p].astype(f32)
    pairs[...] = total
    finish_weights()
    for p in range(9):
        wpad[32 * p : 32 * p + PK, 0:W2] = weight[p // 3, p % 3]

    own_k = one_hot(
        (iota((32, 128), 1) & 63 < 3 * PK)
        & (lax.rem(iota((32, 128), 1) & 63, PK) == iota((32, 128), 0))
    )

    @pl.loop(0, 9)
    def _(p):
        rows = pl.ds(pl.multiple_of(32 * p, 32), 32)
        eight = pairs[pl.ds(pl.multiple_of(8 * p, 8), 8), :]
        for g in range(G):
            row = jnp.broadcast_to(eight[g : g + 1, :], (32, 128))
            amat[rows, 128 * g : 128 * g + 128] = (row * own_k).astype(bf16)

    compact = mm(amat[...], gather[...]).astype(bf16)
    weights = wpad[...].astype(f32)
    straight = (mm(compact, widen[...]) * weights).astype(bf16)
    crossed = (mm(compact, widen_sw[...]) * weights).astype(bf16)
    mixed = (mm(straight, sum_re[...]) + mm(crossed, sum_im[...])).astype(bf16)
    wide[...] = mm(mixed, spread[...])

    @pl.loop(0, 9)
    def _(p):
        rows = pl.ds(pl.multiple_of(32 * p, 32), 32)
        sums = [
            jnp.sum(wide[rows, 128 * g : 128 * g + 128] * own_k, axis=0, keepdims=True)
            for g in range(G)
        ]
        mix[pl.ds(pl.multiple_of(8 * p, 8), 8), :] = jnp.concatenate(
            sums + [jnp.zeros((1, 128), f32)], axis=0
        )

    send_c[...] = mix[...].astype(bf16)
    exchange(on_e, e, send_c, recv_c, ss_c, rs_c, same=True, beside=prepare_rows)

    for p in range(R):
        xc[72 * p : 72 * p + 72, :] = recv_c[p].astype(f32)
    data = jnp.concatenate(
        [xc[pl.ds(u, MX, stride=24), :] for u in used], axis=1
    ).astype(bf16)
    got = mm(x_bwd[e], data)
    for n, u in enumerate(used):
        part_u = got[:, 128 * n : 128 * n + 128]
        xd[pl.ds(u, 16, stride=24), :] = combine(part_u[0:16], part_u[16:32], -fwd_sign)
    for x in range(2):
        for p in range(R):
            send_d[p, x] = xd[48 * p + 24 * x : 48 * p + 24 * x + 24, :].astype(bf16)
        start_z(x, send_d, recv_d, ss_d, rs_d)

    @pl.loop(0, 2)
    def _(x):
        finish_y(x, recv_d, rs_d)
        xe[...] = recv_d[x].astype(f32).reshape(192, 128)
        data = jnp.concatenate(
            [xe[pl.ds(g, MY, stride=8), :] for g in range(G)], axis=1
        ).astype(bf16)
        got = mm(y_bwd[...], data)
        for g in range(G):
            part_g = got[:, 128 * g : 128 * g + 128]
            turned = combine(part_g[0:Y], part_g[Y : 2 * Y], -fwd_sign).astype(bf16)
            send_e[:, x, :, 128 * g : 128 * g + 128] = turned.reshape(R, 16, 128)
        start_y(x, send_e, recv_e, ss_e, rs_e)

    @pl.loop(0, 2)
    def _(x):
        finish_y(x, recv_e, rs_e)

        @pl.loop(0, G)
        def _(g):
            lanes = pl.ds(pl.multiple_of(128 * g, 128), 128)
            for t in range(3):
                held = [
                    recv_e[x, n, :, lanes].astype(f32) if n < R else None
                    for n in range(3 * t, 3 * t + 3)
                ]
                for m in range(3):
                    rows = pl.ds(pl.multiple_of(48 * g + 16 * m, 16), 16)
                    s6[rows, 128 * t : 128 * t + 128] = regrouped(held, m).astype(bf16)

        @pl.loop(0, 4)
        def _(c):
            cut = pl.ds(pl.multiple_of(256 * c, 256), 256)

            def twice(ref):
                return jnp.concatenate([ref[...], ref[...]], axis=1)

            value = mm(s6[0:320, :], t_bwd[:, cut]) + mm(skip_k[...], field[x, :, cut])
            state = 0.5 * twice_gelu(value + twice(skip_col))
            halves = state.reshape(C, 2, 8, 256)
            for h in range(2):
                inner = mm(hid_k[...], halves[:, h].reshape(160, 256).astype(bf16))
                weighed = twice_gelu(inner + twice(hid_col)) * twice(out_col)
                part[pl.ds(pl.multiple_of(x * 16, 16) + 8 * h, 8), cut] = jnp.sum(
                    weighed.reshape(HID, 8, 256), axis=0
                )

    for b in range(8):
        blk[pl.ds(b, 32, stride=8), :] = part[:, 128 * b : 128 * b + 128]

    send_f[...] = mm(perm[...], blk[...].astype(bf16)).astype(bf16).reshape(R, 32, 128)
    exchange(on_z, zh, send_f, recv_f, ss_f, rs_f)
    send_g[...] = mm(regroup[...], recv_f[...].reshape(256, 128)).astype(bf16).reshape(R, 32, 128)
    exchange(on_e, e, send_g, recv_g, ss_g, rs_g)
    owned = mm(pick[...], recv_g[...].reshape(256, 128))
    out[...] = owned[0:100].astype(bf16)
    finish_sends()


def scratch():
    v = pltpu.VMEM
    dma = pltpu.SemaphoreType.DMA
    buffers = [
        v((2, 320, 1024), bf16),
        v((3, 3, PK, W2), bf16),
        v((1024, 384), bf16),
        v((384, 1024), bf16),
        v((48, 128), bf16),
        v((256, 24), bf16),
        v((R, 48, 16), bf16),
        v((R, 32, 24), bf16),
        v((LW, 128), bf16),
        v((128, LW), bf16),
        v((128, LW), bf16),
        v((128, LW), bf16),
        v((LW, 128), bf16),
        v((LW, 128), bf16),
        v((256, 256), bf16),
        v((R, 2, 16, LW), bf16),
        v((2, R, 16, LW), bf16),
        v((192, 128), f32),
        v((R, 2, 24, 128), bf16),
        v((2, R, 24, 128), bf16),
        v((384, 128), f32),
        v((576, 128), f32),
        v((R, 72, 128), bf16),
        v((R, 72, 128), bf16),
        v((72, 128), f32),
        v((288, LW), bf16),
        v((72, 128), f32),
        v((72, 128), bf16),
        v((R, 72, 128), bf16),
        v((576, 128), f32),
        v((384, 128), f32),
        v((R, 2, 24, 128), bf16),
        v((2, R, 24, 128), bf16),
        v((192, 128), f32),
        v((R, 2, 16, LW), bf16),
        v((2, R, 16, LW), bf16),
        v((336, 384), bf16),
        v((336, 384), f32),
        v((288, LW), f32),
        v((32, 1024), f32),
        v((256, 128), f32),
        v((R, 32, 128), bf16),
        v((R, 32, 128), bf16),
        v((R, 32, 128), bf16),
        v((R, 32, 128), bf16),
        v((288, LW), bf16),
        v((256, 256), bf16),
        v((128, 256), bf16),
        v((8, 256), jnp.int32),
        v((128, 128), f32),
        v((320, 320), bf16),
        v((512, 160), bf16),
        v((320, 128), f32),
        v((512, 128), f32),
        v((512, 128), f32),
    ]
    one, by_x = [dma((1,))] * 2, [dma((2,))] * 2
    sems = [dma((15,))] + by_x + by_x + one + [dma((3,))] * 3 + one + by_x + by_x + one + one
    return buffers + sems


def local(
    field,
    spectral_weight,
    skip_weight,
    skip_bias,
    hidden_weight,
    hidden_bias,
    out_weight,
    block_ids,
    send_rows,
    recv_rows,
):
    tables = [jnp.asarray(t) for t in constants()]
    args = [
        jnp.transpose(field, (0, 2, 1, 3)).reshape(2, 320, Z * T_SIZE),
        spectral_weight.reshape(3, 3, PK, W2),
        skip_weight,
        skip_bias.reshape(1, C),
        hidden_weight,
        hidden_bias.reshape(1, HID),
        out_weight.reshape(1, HID),
        block_ids.reshape(1, 200),
        send_rows.reshape(1, 200),
        recv_rows.reshape(1, 100),
    ] + tables
    vmem = pl.BlockSpec(memory_space=pltpu.VMEM)
    hbm = pl.BlockSpec(memory_space=pl.ANY)
    result = pl.pallas_call(
        kernel,
        out_shape=jax.ShapeDtypeStruct((100, 128), bf16),
        in_specs=[hbm] * 2 + [vmem] * 8 + [hbm] * len(tables),
        out_specs=vmem,
        scratch_shapes=scratch(),
        compiler_params=pltpu.CompilerParams(
            collective_id=0, has_side_effects=True, vmem_limit_bytes=56 * 1024 * 1024
        ),
    )(*args)
    return result.reshape(1, 1, 100, 128)


def solution(mesh):
    placed = (
        P("gx", "gy", None, None),
        P("gx", "gy", None),
        P(),
        P(),
        P(),
        P(),
        P(),
        P("gx", "gy", None),
        P("gx", "gy", None),
        P("gx", "gy", None),
    )
    return jax.shard_map(
        local, mesh=mesh, in_specs=placed, out_specs=P("gx", "gy", None, None), check_vma=False
    )
```

```python
import functools
import math

import jax
import jax.numpy as jnp
import ml_dtypes
import numpy as np
from jax import lax
from jax.experimental import pallas as pl
from jax.experimental.pallas import tpu as pltpu
from jax.sharding import PartitionSpec as P

C = 20
HID = 64
MX = 24
MY = 24
MZ = 12
MT = 12
Z = 32
T_SIZE = 32
X = 128
Y = 128
KZT = MZ * MT
PK = 18
G = 6
R = 8
LW = G * 128
WW = 896
W2 = 2 * C * C
MESH = pl.DeviceIdType.MESH
f32 = jnp.float32
bf16 = jnp.bfloat16
GA = math.sqrt(2.0 / math.pi)
GB = GA * 0.044715


def lane_of(ch, r, k):
    if ch < 18:
        return 128 * (ch // 3) + 64 * r + PK * (ch % 3) + k
    tile = 2 * (ch - 18) + k // 10
    return 128 * tile + 64 * r + 54 + k % 10


def constants():
    half = ml_dtypes.bfloat16

    def cos_sin(f, n, length):
        a = 2.0 * np.pi * ((f * n) % length) / length
        return np.cos(a), np.sin(a)

    q = np.arange(Z * T_SIZE)
    forward = np.zeros((Z * T_SIZE, 384))
    backward = np.zeros((384, Z * T_SIZE))
    for j in range(R):
        for k in range(PK):
            kk = PK * j + k
            fz, ft = kk % MZ - MZ // 2, kk // MZ - MT // 2
            a = 2.0 * np.pi * (((fz * (q % Z)) % Z) / Z + ((ft * (q // Z)) % T_SIZE) / T_SIZE)
            lane = 128 * (j // 3) + PK * (j % 3) + k
            forward[:, lane] = np.cos(a) / math.sqrt(Z * T_SIZE)
            forward[:, lane + 64] = -np.sin(a) / math.sqrt(Z * T_SIZE)
            backward[lane] = np.cos(a) / math.sqrt(MX * MY * KZT)
            backward[lane + 64] = -np.sin(a) / math.sqrt(MX * MY * KZT)
    order = (3 * np.arange(R)[None, :] + np.arange(3)[:, None]).reshape(-1)
    fy = order - MY // 2
    c, s = cos_sin(fy[:, None], np.arange(Y)[None, :], Y)
    y_fwd = np.concatenate([c, s], 0) / math.sqrt(Y)
    y_bwd = np.concatenate([c.T, s.T], 0)
    fx = order - MX // 2
    x_fwd = np.zeros((R, 48, 16))
    x_bwd = np.zeros((R, 32, 24))
    for zh in range(R):
        c, s = cos_sin(fx[:, None], 16 * zh + np.arange(16)[None, :], X)
        x_fwd[zh] = np.concatenate([c, s], 0) / math.sqrt(X)
        x_bwd[zh] = np.concatenate([c.T, s.T], 0)
    gather = np.zeros((LW, 128))
    spread = np.zeros((128, LW))
    for ch in range(C):
        for r in range(2):
            for k in range(PK):
                gather[lane_of(ch, r, k), 64 * r + ch] = 1.0
                spread[64 * r + ch, lane_of(ch, r, k)] = 1.0
    widen = np.zeros((128, WW))
    widen_swapped = np.zeros((128, WW))
    sum_re = np.zeros((WW, 128))
    sum_im = np.zeros((WW, 128))
    for r in range(2):
        for ch in range(C):
            for d in range(C):
                col = 400 * r + C * ch + d
                widen[64 * r + ch, col] = 1.0
                widen_swapped[64 * (1 - r) + ch, col] = 1.0
                sum_re[col, d] = 1.0 - 2.0 * r
                sum_im[col, 64 + d] = 1.0
    regroup = np.zeros((256, 256))
    for e in range(R):
        for zh in range(R):
            for n in range(4):
                regroup[32 * e + 4 * zh + n, 32 * zh + 4 * e + n] = 1.0
    tables = (
        forward, backward, y_fwd, y_bwd, x_fwd, x_bwd, gather, spread,
        widen, widen_swapped, sum_re, sum_im, regroup,
    )
    return [t.astype(half) for t in tables]


def mm(a, b):
    return lax.dot_general(a, b, (((1,), (0,)), ((), ())), preferred_element_type=f32)


def iota(shape, dim):
    return lax.broadcasted_iota(jnp.int32, shape, dim)


def one_hot(mask):
    return jnp.where(mask, 1.0, 0.0).astype(f32)


def twice_gelu(v):
    return v + v * jnp.tanh(v * (GA + GB * (v * v)))


def kernel(*refs):
    (
        field_in, weight_in, skip_w, skip_b, hid_w, hid_b, out_w, b_ids, s_rows, r_rows,
        t_fwd_in, t_bwd_in, y_fwd_in, y_bwd_in, x_fwd_in, x_bwd_in, gather_in, spread_in,
        widen_in, widen_sw_in, sum_re_in, sum_im_in, regroup_in,
        out,
        field, weight, t_fwd, t_bwd, y_fwd, y_bwd, x_fwd, x_bwd, gather, spread,
        widen, widen_sw, sum_re, sum_im, regroup,
        send_y, recv_y, ya, send_a, recv_a, xa, xb, send_b, recv_b,
        pairs, amat, mix, send_c, recv_c, xc, xd, send_d, recv_d, xe, send_e, recv_e,
        s6, part, blk, send_f, recv_f, send_g, recv_g, wpad, perm, pick, idrows, square, skip_k, hid_k,
        skip_col, hid_col, out_col,
        fetched,
        ss_y, rs_y, ss_a, rs_a, ss_b, rs_b, ss_p, rs_p, ls_p, ss_c, rs_c,
        ss_d, rs_d, ss_e, rs_e, ss_f, rs_f, ss_g, rs_g,
    ) = refs
    i = lax.axis_index("gx")
    j = lax.axis_index("gy")
    zh = lax.div(i, R)
    e = lax.rem(i, R)

    def turn(n, d):
        return lax.rem(n + d, R)

    def on_y(d):
        return turn(j, d), (i, turn(j, d))

    def on_z(d):
        return turn(zh, d), (R * turn(zh, d) + e, j)

    def on_e(d):
        return turn(e, d), (R * zh + turn(e, d), j)

    owners = []
    for n in range(3):
        first = MY * (3 * zh + n) + 3 * e
        owners.append((lax.div(first, 9), lax.div(lax.rem(first, 9), 3)))
    sources = []
    for a in range(3):
        first = 9 * i + 3 * a
        jx, jy = lax.div(first, MY), lax.rem(first, MY)
        sources.append((R * zh + lax.div(jy, 3), lax.rem(jx, 3)))

    barrier = pltpu.get_barrier_semaphore()
    for near in (on_y, on_z, on_e):
        for d in range(1, R):
            pl.semaphore_signal(barrier, inc=1, device_id=near(d)[1], device_id_type=MESH)

    fetch = []
    wanted = [
        (t_fwd_in, t_fwd), (field_in.at[0], field.at[0]), (field_in.at[1], field.at[1]),
        (y_fwd_in, y_fwd), (x_fwd_in, x_fwd), (gather_in, gather),
        (widen_in, widen), (widen_sw_in, widen_sw), (sum_re_in, sum_re), (sum_im_in, sum_im),
        (spread_in, spread), (x_bwd_in, x_bwd), (y_bwd_in, y_bwd), (t_bwd_in, t_bwd),
        (regroup_in, regroup),
    ]
    for n, (source, target) in enumerate(wanted):
        fetch.append(pltpu.make_async_copy(source, target, fetched.at[n]))
        fetch[n].start()

    sent = []

    def await_bytes(view, sem):
        pltpu.make_async_copy(view, view, sem).wait()

    def start(near, me, send, recv, send_sem, recv_sem):
        for d in range(1, R):
            peer, device = near(d)
            pltpu.make_async_remote_copy(
                src_ref=send(peer),
                dst_ref=recv(me),
                send_sem=send_sem,
                recv_sem=recv_sem,
                device_id=device,
                device_id_type=MESH,
            ).start()

    def exchange(near, me, send, recv, send_sem, recv_sem, same=False, beside=None):
        start(
            near, me, (lambda p: send) if same else (lambda p: send.at[p]), lambda p: recv.at[p],
            send_sem.at[0], recv_sem.at[0],
        )
        recv[me] = send[...] if same else send[me]
        seven = recv.at[pl.ds(0, R - 1)]
        sent.append((seven, send_sem.at[0]))
        if beside is not None:
            beside()
        await_bytes(seven, recv_sem.at[0])

    def start_y(x, send, recv, send_sem, recv_sem):
        start(
            on_y, j, lambda p: send.at[p, x], lambda p: recv.at[x, p], send_sem.at[x], recv_sem.at[x]
        )
        recv[x, j] = send[j, x]

    def finish_y(x, recv, recv_sem):
        await_bytes(recv.at[x, pl.ds(0, R - 1)], recv_sem.at[x])

    def start_e(x, send, recv, send_sem, recv_sem):
        start(
            on_e, e, lambda p: send.at[p, x], lambda p: recv.at[x, p], send_sem.at[x], recv_sem.at[x]
        )
        recv[x, e] = send[e, x]

    def weights_copy(n, a, device):
        return pltpu.make_async_remote_copy(
            src_ref=weight_in.at[n],
            dst_ref=weight.at[a],
            send_sem=ss_p.at[n],
            recv_sem=rs_p.at[a],
            device_id=(device, j),
            device_id_type=MESH,
        )

    def weights_kept(n, a):
        return pltpu.make_async_copy(weight_in.at[n], weight.at[a], ls_p.at[n])

    def start_weights():
        for n, (device, a) in enumerate(sources):

            @pl.when(device != i)
            def _():
                weights_copy(n, a, device).start()

            @pl.when(device == i)
            def _():
                weights_kept(n, a).start()

    def finish_weights():
        for n, (device, a) in enumerate(sources):

            @pl.when(device == i)
            def _():
                weights_kept(n, a).wait()

        for a, (device, n) in enumerate(owners):

            @pl.when(device != i)
            def _():
                weights_copy(n, a, device).wait_recv()

    def finish_sends():
        for n, (device, a) in enumerate(sources):

            @pl.when(device != i)
            def _():
                weights_copy(n, a, device).wait_send()

        for view, sem in sent:
            await_bytes(view, sem)
        for recv, send_sem in ((recv_y, ss_y), (recv_a, ss_a), (recv_d, ss_d), (recv_e, ss_e)):
            for x in range(2):
                await_bytes(recv.at[x, pl.ds(0, R - 1)], send_sem.at[x])

    lane = iota((1, 128), 1)
    in_half = lane & 63
    fwd_sign = jnp.where(lane < 64, 1.0, -1.0)

    def lanes_in(low, high):
        return (in_half >= low) & (in_half < high)

    def put_together(pieces):
        total = jnp.zeros(pieces[0][0].shape, f32)
        for rows, origin, low, high in pieces:
            shift = (low - origin) % 128
            moved = rows if shift == 0 else pltpu.roll(rows, shift, 1)
            total = jnp.where(lanes_in(low, high), moved, total)
        return total

    def combine(cosines, sines, sign):
        return cosines + sign * pltpu.roll(sines, 64, 1)

    def along_zt(x):
        got = mm(field[x], t_fwd[...])
        for t in range(3):
            rows_of = [got[16 * c : 16 * c + 16, 128 * t : 128 * t + 128] for c in range(C)]
            for n in range(min(3, R - 3 * t)):
                for g in range(G):
                    pieces = [
                        (rows_of[3 * g + m], PK * n, PK * m, PK * m + PK) for m in range(3)
                    ]
                    if g < 4:
                        cut = 10 * (g % 2)
                        pieces.append(
                            (rows_of[18 + g // 2], PK * n + cut, 54, 54 + min(10, PK - cut))
                        )
                    send_y[3 * t + n, x, :, 128 * g : 128 * g + 128] = put_together(pieces).astype(
                        bf16
                    )

    fetch[0].wait()
    fetch[1].wait()
    along_zt(0)
    pl.semaphore_wait(barrier, 3 * (R - 1))
    start_y(0, send_y, recv_y, ss_y, rs_y)
    start_weights()
    fetch[2].wait()
    along_zt(1)
    start_y(1, send_y, recv_y, ss_y, rs_y)
    for copy in fetch[3:]:
        copy.wait()

    def spread_map(values, rows, cols, places):
        shift = places.bit_length() - 1
        left = one_hot((iota((rows, 128), 0) >> shift) == iota((rows, 128), 1)).astype(bf16)
        right = one_hot((iota((128, cols), 1) >> shift) == iota((128, cols), 0)).astype(bf16)
        wide = mm(mm(left, values.T.astype(bf16)).astype(bf16), right)
        same = (iota((rows, cols), 0) & (places - 1)) == (iota((rows, cols), 1) & (places - 1))
        return jnp.where(same, wide, 0.0).astype(bf16)

    def column(values, places, width, rows):
        shift = places.bit_length() - 1
        at = one_hot((iota((rows, width), 0) >> shift) == iota((rows, width), 1))
        return jnp.broadcast_to(jnp.sum(at * values, axis=1, keepdims=True), (rows, 128))

    def prepare_clear():
        ya[...] = jnp.zeros((192, 128), f32)
        xb[...] = jnp.zeros((448, 128), f32)
        xd[...] = jnp.zeros((384, 128), f32)
        mix[...] = jnp.zeros((56, 128), f32)

    def prepare_rows():
        idrows[...] = jnp.full((8, 256), -1, jnp.int32)
        idrows[0:1, 0:200] = b_ids[...]
        idrows[1:2, 0:200] = s_rows[...]
        idrows[2:3, 0:100] = r_rows[...]
        row = iota((256, 256), 0)
        by_block = one_hot(row == idrows[0:1, :]).astype(bf16)
        by_row = one_hot(row == idrows[1:2, :]).astype(bf16)
        perm[...] = lax.dot_general(
            by_row, by_block, (((1,), (1,)), ((), ())), preferred_element_type=f32
        ).astype(bf16)
        place = iota((256, 128), 0)
        name = ((place >> 2) & 7) * 32 + (place >> 5) * 4 + (place & 3)
        pick[...] = one_hot(name == idrows[2:3, 0:128]).T.astype(bf16)

    def prepare_weights():
        wpad[...] = jnp.zeros((288, WW), bf16)
        finish_weights()
        for p in range(9):
            wpad[32 * p : 32 * p + PK, 0:W2] = weight[p // 3, p % 3]

    def prepare_skip():
        square[...] = jnp.zeros((128, 128), f32)
        square[0:C, 0:C] = skip_w[...].astype(f32)
        skip_k[...] = spread_map(square[...], 320, 320, 16)
        skip_col[...] = column(skip_b[...], 16, C, 320)

    def prepare_hidden():
        square[...] = jnp.zeros((128, 128), f32)
        square[0:C, 0:HID] = hid_w[...].astype(f32)
        hid_k[...] = spread_map(square[...], 512, 160, 8)
        hid_col[...] = column(hid_b[...], 8, HID, 512)

    def prepare_out():
        out_col[...] = column(0.5 * out_w[...].astype(f32), 8, HID, 512)

    prepare_clear()
    prepare_skip()

    for x in range(2):
        finish_y(x, recv_y, rs_y)
        got = mm(y_fwd[...], recv_y[x].reshape(Y, LW))
        for g in range(G):
            part_g = got[:, 128 * g : 128 * g + 128]
            rows = combine(part_g[0:MY], part_g[MY : 2 * MY], fwd_sign)
            for m in range(3):
                ya[pl.ds(G * m + g, R, stride=24), :] = rows[R * m : R * m + R]
        send_a[:, x] = ya[...].astype(bf16).reshape(R, 24, 128)
        start_e(x, send_a, recv_a, ss_a, rs_a)
    prepare_weights()
    for x in range(2):
        finish_y(x, recv_a, rs_a)

    places = range(3 * G)
    for p in range(R):
        for x in range(2):
            xa[48 * p + 24 * x : 48 * p + 24 * x + 24, :] = recv_a[x, p].astype(f32)
    data = jnp.concatenate(
        [xa[pl.ds(u, 16, stride=24), :] for u in places], axis=1
    ).astype(bf16)
    got = mm(x_fwd[zh], data)
    for u in places:
        part_u = got[:, 128 * u : 128 * u + 128]
        rows = combine(part_u[0:MX], part_u[MX : 2 * MX], fwd_sign)
        for m in range(3):
            xb[pl.ds(3 * G * m + u, R, stride=56), :] = rows[R * m : R * m + R]
    for p in range(R):
        send_b[p] = xb[56 * p : 56 * p + 56, :].astype(bf16)
    exchange(on_z, zh, send_b, recv_b, ss_b, rs_b, beside=prepare_hidden)
    total = recv_b[0].astype(f32)
    for p in range(1, R):
        total = total + recv_b[p].astype(f32)
    pairs[...] = total

    k_row = iota((32, 128), 0)
    k_half = iota((32, 128), 1) & 63
    usual = (k_half < 54) & (lax.rem(k_half, PK) == k_row)
    late = (k_half >= 54) & (k_row < PK)
    own_k = [
        one_hot(usual | (late & (k_half - 54 == k_row))),
        one_hot(usual | (late & (k_half - 44 == k_row))),
    ] * 2 + [one_hot(usual)] * 2
    for p in range(9):
        for g in range(G):
            row = jnp.broadcast_to(pairs[G * p + g : G * p + g + 1, :], (32, 128))
            amat[32 * p : 32 * p + 32, 128 * g : 128 * g + 128] = (row * own_k[g]).astype(bf16)
    compact = mm(amat[...], gather[...]).astype(bf16)
    weights = wpad[...].astype(f32)
    straight = (mm(compact, widen[...]) * weights).astype(bf16)
    crossed = (mm(compact, widen_sw[...]) * weights).astype(bf16)
    mixed = (mm(straight, sum_re[...]) + mm(crossed, sum_im[...])).astype(bf16)
    wide = mm(mixed, spread[...])
    for p in range(9):
        for g in range(G):
            tile = wide[32 * p : 32 * p + 32, 128 * g : 128 * g + 128] * own_k[g]
            mix[G * p + g : G * p + g + 1, :] = jnp.sum(tile, axis=0, keepdims=True)
    send_c[...] = mix[...].astype(bf16)

    def prepare_late():
        prepare_out()
        prepare_rows()

    exchange(on_z, zh, send_c, recv_c, ss_c, rs_c, same=True, beside=prepare_late)

    for p in range(R):
        xc[56 * p : 56 * p + 56, :] = recv_c[p].astype(f32)

    def by_frequency(ref, first, stride):
        return jnp.concatenate(
            [ref[pl.ds(first(m), R, stride=stride), :] for m in range(3)], axis=0
        )

    data = jnp.concatenate(
        [by_frequency(xc, lambda m: 3 * G * m + u, 56) for u in places], axis=1
    ).astype(bf16)
    got = mm(x_bwd[zh], data)
    for u in places:
        part_u = got[:, 128 * u : 128 * u + 128]
        xd[pl.ds(u, 16, stride=24), :] = combine(part_u[0:16], part_u[16:32], -fwd_sign)
    for x in range(2):
        for p in range(R):
            send_d[p, x] = xd[48 * p + 24 * x : 48 * p + 24 * x + 24, :].astype(bf16)
        start_e(x, send_d, recv_d, ss_d, rs_d)

    for x in range(2):
        finish_y(x, recv_d, rs_d)
        xe[...] = recv_d[x].astype(f32).reshape(192, 128)
        data = jnp.concatenate(
            [by_frequency(xe, lambda m: G * m + g, 24) for g in range(G)], axis=1
        ).astype(bf16)
        got = mm(y_bwd[...], data)
        for g in range(G):
            part_g = got[:, 128 * g : 128 * g + 128]
            turned = combine(part_g[0:Y], part_g[Y : 2 * Y], -fwd_sign).astype(bf16)
            send_e[:, x, :, 128 * g : 128 * g + 128] = turned.reshape(R, 16, 128)
        start_y(x, send_e, recv_e, ss_e, rs_e)

    @pl.loop(0, 2)
    def _(x):
        finish_y(x, recv_e, rs_e)
        for t in range(3):
            rows_of = [
                [recv_e[x, n, :, 128 * g : 128 * g + 128].astype(f32) for g in range(G)]
                for n in range(3 * t, min(R, 3 * t + 3))
            ]
            for c in range(C):
                pieces = []
                for n, tiles in enumerate(rows_of):
                    if c < 18:
                        pieces.append((tiles[c // 3], PK * (c % 3), PK * n, PK * n + PK))
                    else:
                        for part_k in range(2):
                            low = PK * n + 10 * part_k
                            tile = tiles[2 * (c - 18) + part_k]
                            pieces.append((tile, 54, low, min(low + 10, PK * n + PK)))
                s6[16 * c : 16 * c + 16, 128 * t : 128 * t + 128] = put_together(pieces).astype(
                    bf16
                )

        def twice(ref):
            return jnp.concatenate([ref[...], ref[...]], axis=1)

        for c in range(4):
            cut = slice(256 * c, 256 * c + 256)
            value = mm(s6[...], t_bwd[:, cut]) + mm(skip_k[...], field[x, :, cut])
            state = 0.5 * twice_gelu(value + twice(skip_col))
            halves = state.reshape(C, 2, 8, 256)
            for h in range(2):
                inner = mm(hid_k[...], halves[:, h].reshape(160, 256).astype(bf16))
                weighed = twice_gelu(inner + twice(hid_col)) * twice(out_col)
                part[pl.ds(pl.multiple_of(x * 16, 16) + 8 * h, 8), cut] = jnp.sum(
                    weighed.reshape(HID, 8, 256), axis=0
                )

    for b in range(8):
        blk[pl.ds(b, 32, stride=8), :] = part[:, 128 * b : 128 * b + 128]

    send_f[...] = mm(perm[...], blk[...].astype(bf16)).astype(bf16).reshape(R, 32, 128)
    exchange(on_z, zh, send_f, recv_f, ss_f, rs_f)
    send_g[...] = mm(regroup[...], recv_f[...].reshape(256, 128)).astype(bf16).reshape(R, 32, 128)
    exchange(on_e, e, send_g, recv_g, ss_g, rs_g)
    owned = mm(pick[...], recv_g[...].reshape(256, 128))
    out[...] = owned[0:100].astype(bf16)
    finish_sends()


def scratch():
    v = pltpu.VMEM
    dma = pltpu.SemaphoreType.DMA
    buffers = [
        v((2, 320, 1024), bf16),
        v((3, 3, PK, W2), bf16),
        v((1024, 384), bf16),
        v((384, 1024), bf16),
        v((48, 128), bf16),
        v((256, 24), bf16),
        v((R, 48, 16), bf16),
        v((R, 32, 24), bf16),
        v((LW, 128), bf16),
        v((128, LW), bf16),
        v((128, WW), bf16),
        v((128, WW), bf16),
        v((WW, 128), bf16),
        v((WW, 128), bf16),
        v((256, 256), bf16),
        v((R, 2, 16, LW), bf16),
        v((2, R, 16, LW), bf16),
        v((192, 128), f32),
        v((R, 2, 24, 128), bf16),
        v((2, R, 24, 128), bf16),
        v((384, 128), f32),
        v((448, 128), f32),
        v((R, 56, 128), bf16),
        v((R, 56, 128), bf16),
        v((56, 128), f32),
        v((288, LW), bf16),
        v((56, 128), f32),
        v((56, 128), bf16),
        v((R, 56, 128), bf16),
        v((448, 128), f32),
        v((384, 128), f32),
        v((R, 2, 24, 128), bf16),
        v((2, R, 24, 128), bf16),
        v((192, 128), f32),
        v((R, 2, 16, LW), bf16),
        v((2, R, 16, LW), bf16),
        v((320, 384), bf16),
        v((32, 1024), f32),
        v((256, 128), f32),
        v((R, 32, 128), bf16),
        v((R, 32, 128), bf16),
        v((R, 32, 128), bf16),
        v((R, 32, 128), bf16),
        v((288, WW), bf16),
        v((256, 256), bf16),
        v((128, 256), bf16),
        v((8, 256), jnp.int32),
        v((128, 128), f32),
        v((320, 320), bf16),
        v((512, 160), bf16),
        v((320, 128), f32),
        v((512, 128), f32),
        v((512, 128), f32),
    ]
    one, by_x = [dma((1,))] * 2, [dma((2,))] * 2
    sems = [dma((15,))] + by_x + by_x + one + [dma((3,))] * 3 + one + by_x + by_x + one + one
    return buffers + sems


def local(
    field,
    spectral_weight,
    skip_weight,
    skip_bias,
    hidden_weight,
    hidden_bias,
    out_weight,
    block_ids,
    send_rows,
    recv_rows,
):
    tables = [jnp.asarray(t) for t in constants()]
    args = [
        jnp.transpose(field, (0, 2, 1, 3)).reshape(2, 320, Z * T_SIZE),
        spectral_weight.reshape(3, 3, PK, W2),
        skip_weight,
        skip_bias.reshape(1, C),
        hidden_weight,
        hidden_bias.reshape(1, HID),
        out_weight.reshape(1, HID),
        block_ids.reshape(1, 200),
        send_rows.reshape(1, 200),
        recv_rows.reshape(1, 100),
    ] + tables
    vmem = pl.BlockSpec(memory_space=pltpu.VMEM)
    hbm = pl.BlockSpec(memory_space=pl.ANY)
    result = pl.pallas_call(
        kernel,
        out_shape=jax.ShapeDtypeStruct((100, 128), bf16),
        in_specs=[hbm] * 2 + [vmem] * 8 + [hbm] * len(tables),
        out_specs=vmem,
        scratch_shapes=scratch(),
        compiler_params=pltpu.CompilerParams(
            collective_id=0, has_side_effects=True, vmem_limit_bytes=56 * 1024 * 1024
        ),
    )(*args)
    return result.reshape(1, 1, 100, 128)


def solution(mesh):
    placed = (
        P("gx", "gy", None, None),
        P("gx", "gy", None),
        P(),
        P(),
        P(),
        P(),
        P(),
        P("gx", "gy", None),
        P("gx", "gy", None),
        P("gx", "gy", None),
    )
    return jax.shard_map(
        local, mesh=mesh, in_specs=placed, out_specs=P("gx", "gy", None, None), check_vma=False
    )
```

```python
import functools
import math

import jax
import jax.numpy as jnp
import ml_dtypes
import numpy as np
from jax import lax
from jax.experimental import pallas as pl
from jax.experimental.pallas import tpu as pltpu
from jax.sharding import PartitionSpec as P

C = 20
HID = 64
MX = 24
MY = 24
MZ = 12
MT = 12
Z = 32
T_SIZE = 32
X = 128
Y = 128
KZT = MZ * MT
PK = 18
G = 6
R = 8
LW = G * 128
WW = 896
W2 = 2 * C * C
BIAS_LANE = 60
FAR_FIRST = (4, 3, 5, 2, 6, 1, 7)
MESH = pl.DeviceIdType.MESH
f32 = jnp.float32
bf16 = jnp.bfloat16
GA = math.sqrt(2.0 / math.pi)
GB = GA * 0.044715


def lane_of(ch, r, k):
    if ch < 18:
        return 128 * (ch // 3) + 64 * r + PK * (ch % 3) + k
    tile = 2 * (ch - 18) + k // 10
    return 128 * tile + 64 * r + 54 + k % 10


def constants():
    half = ml_dtypes.bfloat16

    def cos_sin(f, n, length):
        a = 2.0 * np.pi * ((f * n) % length) / length
        return np.cos(a), np.sin(a)

    q = np.arange(Z * T_SIZE)
    forward = np.zeros((Z * T_SIZE, 384))
    backward = np.zeros((384, Z * T_SIZE))
    for j in range(R):
        for k in range(PK):
            kk = PK * j + k
            fz, ft = kk % MZ - MZ // 2, kk // MZ - MT // 2
            a = 2.0 * np.pi * (((fz * (q % Z)) % Z) / Z + ((ft * (q // Z)) % T_SIZE) / T_SIZE)
            lane = 128 * (j // 3) + PK * (j % 3) + k
            forward[:, lane] = np.cos(a) / math.sqrt(Z * T_SIZE)
            forward[:, lane + 64] = -np.sin(a) / math.sqrt(Z * T_SIZE)
            backward[lane] = np.cos(a) / math.sqrt(MX * MY * KZT)
            backward[lane + 64] = -np.sin(a) / math.sqrt(MX * MY * KZT)
    backward[BIAS_LANE : BIAS_LANE + 3] = 1.0
    order = (3 * np.arange(R)[None, :] + np.arange(3)[:, None]).reshape(-1)
    fy = order - MY // 2
    c, s = cos_sin(fy[:, None], np.arange(Y)[None, :], Y)
    y_fwd = np.concatenate([c, s], 0) / math.sqrt(Y)
    y_bwd = np.concatenate([c.T, s.T], 0)
    fx = order - MX // 2
    x_fwd = np.zeros((R, 48, 16))
    x_bwd = np.zeros((R, 32, 24))
    for zh in range(R):
        c, s = cos_sin(fx[:, None], 16 * zh + np.arange(16)[None, :], X)
        x_fwd[zh] = np.concatenate([c, s], 0) / math.sqrt(X)
        x_bwd[zh] = np.concatenate([c.T, s.T], 0)
    gather = np.zeros((LW, 128))
    spread = np.zeros((128, LW))
    for ch in range(C):
        for r in range(2):
            for k in range(PK):
                gather[lane_of(ch, r, k), 64 * r + ch] = 1.0
                spread[64 * r + ch, lane_of(ch, r, k)] = 1.0
    widen = np.zeros((128, WW))
    widen_swapped = np.zeros((128, WW))
    sum_re = np.zeros((WW, 128))
    sum_im = np.zeros((WW, 128))
    for r in range(2):
        for ch in range(C):
            for d in range(C):
                col = 400 * r + C * ch + d
                widen[64 * r + ch, col] = 1.0
                widen_swapped[64 * (1 - r) + ch, col] = 1.0
                sum_re[col, d] = 1.0 - 2.0 * r
                sum_im[col, 64 + d] = 1.0
    regroup = np.zeros((256, 256))
    for e in range(R):
        for zh in range(R):
            for n in range(4):
                regroup[32 * e + 4 * zh + n, 32 * zh + 4 * e + n] = 1.0
    tables = (
        forward, backward, y_fwd, y_bwd, x_fwd, x_bwd, gather, spread,
        widen, widen_swapped, sum_re, sum_im, regroup,
    )
    return [t.astype(half) for t in tables]


def mm(a, b):
    return lax.dot_general(a, b, (((1,), (0,)), ((), ())), preferred_element_type=f32)


def iota(shape, dim):
    return lax.broadcasted_iota(jnp.int32, shape, dim)


def one_hot(mask):
    return jnp.where(mask, 1.0, 0.0).astype(f32)


def twice_gelu(v):
    return v + v * jnp.tanh(v * (GA + GB * (v * v)))


def kernel(*refs):
    (
        field_in, weight_in, skip_w, skip_b, hid_w, hid_b, out_w, b_ids, s_rows, r_rows,
        t_fwd_in, t_bwd_in, y_fwd_in, y_bwd_in, x_fwd_in, x_bwd_in, gather_in, spread_in,
        widen_in, widen_sw_in, sum_re_in, sum_im_in, regroup_in,
        out,
        field, weight, t_fwd, t_bwd, y_fwd, y_bwd, x_fwd, x_bwd, gather, spread,
        widen, widen_sw, sum_re, sum_im, regroup,
        send_y, recv_y, ya, send_a, recv_a, xa, xb, send_b, recv_b,
        pairs, amat, mix, send_c, recv_c, xc, xd, send_d, recv_d, xe, send_e, recv_e,
        s6, part, blk, send_f, recv_f, send_g, recv_g, wpad, perm, pick, idrows, square, skip_k, hid_k,
        skip_bias, out_k,
        fetched,
        ss_y, rs_y, ss_a, rs_a, ss_b, rs_b, ss_p, rs_p, ls_p, ss_c, rs_c,
        ss_d, rs_d, ss_e, rs_e, ss_f, rs_f, ss_g, rs_g,
    ) = refs
    i = lax.axis_index("gx")
    j = lax.axis_index("gy")
    zh = lax.div(i, R)
    e = lax.rem(i, R)

    def turn(n, d):
        return lax.rem(n + d, R)

    def on_y(d):
        return turn(j, d), (i, turn(j, d))

    def on_z(d):
        return turn(zh, d), (R * turn(zh, d) + e, j)

    def on_e(d):
        return turn(e, d), (R * zh + turn(e, d), j)

    owners = []
    for n in range(3):
        first = MY * (3 * zh + n) + 3 * e
        owners.append((lax.div(first, 9), lax.div(lax.rem(first, 9), 3)))
    sources = []
    for a in range(3):
        first = 9 * i + 3 * a
        jx, jy = lax.div(first, MY), lax.rem(first, MY)
        sources.append((R * zh + lax.div(jy, 3), lax.rem(jx, 3)))

    barrier = pltpu.get_barrier_semaphore()
    for near in (on_y, on_z, on_e):
        for d in range(1, R):
            pl.semaphore_signal(barrier, inc=1, device_id=near(d)[1], device_id_type=MESH)

    fetch = []
    wanted = [
        (t_fwd_in, t_fwd), (field_in.at[0], field.at[0]), (field_in.at[1], field.at[1]),
        (y_fwd_in, y_fwd), (x_fwd_in, x_fwd), (gather_in, gather),
        (widen_in, widen), (widen_sw_in, widen_sw), (sum_re_in, sum_re), (sum_im_in, sum_im),
        (spread_in, spread), (x_bwd_in, x_bwd), (y_bwd_in, y_bwd), (t_bwd_in, t_bwd),
        (regroup_in, regroup),
    ]
    for n, (source, target) in enumerate(wanted):
        fetch.append(pltpu.make_async_copy(source, target, fetched.at[n]))
        fetch[n].start()

    sent = []

    def await_bytes(view, sem):
        pltpu.make_async_copy(view, view, sem).wait()

    def start(near, me, send, recv, send_sem, recv_sem):
        for d in FAR_FIRST:
            peer, device = near(d)
            pltpu.make_async_remote_copy(
                src_ref=send(peer),
                dst_ref=recv(me),
                send_sem=send_sem,
                recv_sem=recv_sem,
                device_id=device,
                device_id_type=MESH,
            ).start()

    def exchange(near, me, send, recv, send_sem, recv_sem, same=False, beside=None):
        start(
            near, me, (lambda p: send) if same else (lambda p: send.at[p]), lambda p: recv.at[p],
            send_sem.at[0], recv_sem.at[0],
        )
        recv[me] = send[...] if same else send[me]
        seven = recv.at[pl.ds(0, R - 1)]
        sent.append((seven, send_sem.at[0]))
        if beside is not None:
            beside()
        await_bytes(seven, recv_sem.at[0])

    def start_y(x, send, recv, send_sem, recv_sem):
        start(
            on_y, j, lambda p: send.at[p, x], lambda p: recv.at[x, p], send_sem.at[x], recv_sem.at[x]
        )
        recv[x, j] = send[j, x]

    def finish_y(x, recv, recv_sem):
        await_bytes(recv.at[x, pl.ds(0, R - 1)], recv_sem.at[x])

    def start_e(x, send, recv, send_sem, recv_sem):
        start(
            on_e, e, lambda p: send.at[p, x], lambda p: recv.at[x, p], send_sem.at[x], recv_sem.at[x]
        )
        recv[x, e] = send[e, x]

    def weights_copy(n, a, device):
        return pltpu.make_async_remote_copy(
            src_ref=weight_in.at[n],
            dst_ref=weight.at[a],
            send_sem=ss_p.at[n],
            recv_sem=rs_p.at[a],
            device_id=(device, j),
            device_id_type=MESH,
        )

    def weights_kept(n, a):
        return pltpu.make_async_copy(weight_in.at[n], weight.at[a], ls_p.at[n])

    def start_weights():
        for n, (device, a) in enumerate(sources):

            @pl.when(device != i)
            def _():
                weights_copy(n, a, device).start()

            @pl.when(device == i)
            def _():
                weights_kept(n, a).start()

    def finish_weights():
        for n, (device, a) in enumerate(sources):

            @pl.when(device == i)
            def _():
                weights_kept(n, a).wait()

        for a, (device, n) in enumerate(owners):

            @pl.when(device != i)
            def _():
                weights_copy(n, a, device).wait_recv()

    def finish_sends():
        for n, (device, a) in enumerate(sources):

            @pl.when(device != i)
            def _():
                weights_copy(n, a, device).wait_send()

        for view, sem in sent:
            await_bytes(view, sem)
        for recv, send_sem in ((recv_y, ss_y), (recv_a, ss_a), (recv_d, ss_d), (recv_e, ss_e)):
            for x in range(2):
                await_bytes(recv.at[x, pl.ds(0, R - 1)], send_sem.at[x])

    lane = iota((1, 128), 1)
    in_half = lane & 63
    fwd_sign = jnp.where(lane < 64, 1.0, -1.0)

    def lanes_in(low, high):
        return (in_half >= low) & (in_half < high)

    def put_together(pieces, total=None):
        if total is None:
            total = jnp.zeros(pieces[0][0].shape, f32)
        for rows, origin, low, high in pieces:
            shift = (low - origin) % 128
            moved = rows if shift == 0 else pltpu.roll(rows, shift, 1)
            total = jnp.where(lanes_in(low, high), moved, total)
        return total

    def combine(cosines, sines, sign):
        return cosines + sign * pltpu.roll(sines, 64, 1)

    def along_zt(x):
        got = mm(field[x], t_fwd[...])
        for t in range(3):
            rows_of = [got[16 * c : 16 * c + 16, 128 * t : 128 * t + 128] for c in range(C)]
            for n in range(min(3, R - 3 * t)):
                for g in range(G):
                    pieces = [
                        (rows_of[3 * g + m], PK * n, PK * m, PK * m + PK) for m in range(3)
                    ]
                    if g < 4:
                        cut = 10 * (g % 2)
                        pieces.append(
                            (rows_of[18 + g // 2], PK * n + cut, 54, 54 + min(10, PK - cut))
                        )
                    send_y[3 * t + n, x, :, 128 * g : 128 * g + 128] = put_together(pieces).astype(
                        bf16
                    )

    fetch[0].wait()
    fetch[1].wait()
    along_zt(0)
    pl.semaphore_wait(barrier, 3 * (R - 1))
    start_y(0, send_y, recv_y, ss_y, rs_y)
    start_weights()
    fetch[2].wait()
    along_zt(1)
    start_y(1, send_y, recv_y, ss_y, rs_y)
    for copy in fetch[3:]:
        copy.wait()

    def spread_map(values, rows, cols, places):
        shift = places.bit_length() - 1
        left = one_hot((iota((rows, 128), 0) >> shift) == iota((rows, 128), 1)).astype(bf16)
        right = one_hot((iota((128, cols), 1) >> shift) == iota((128, cols), 0)).astype(bf16)
        wide = mm(mm(left, values.T.astype(bf16)).astype(bf16), right)
        same = (iota((rows, cols), 0) & (places - 1)) == (iota((rows, cols), 1) & (places - 1))
        return jnp.where(same, wide, 0.0)

    def with_parts(matrix, values, at, first):
        for n in range(3):
            half = values.astype(bf16).astype(f32)
            matrix = jnp.where(at == first + n, half, matrix)
            values = values - half
        return matrix

    def column(values, places, width, rows):
        shift = places.bit_length() - 1
        at = one_hot((iota((rows, width), 0) >> shift) == iota((rows, width), 1))
        return jnp.broadcast_to(jnp.sum(at * values, axis=1, keepdims=True), (rows, 128))

    def prepare_clear():
        ya[...] = jnp.zeros((192, 128), f32)
        xb[...] = jnp.zeros((448, 128), f32)
        xd[...] = jnp.zeros((384, 128), f32)
        mix[...] = jnp.zeros((56, 128), f32)

    def prepare_rows():
        idrows[...] = jnp.full((8, 256), -1, jnp.int32)
        idrows[0:1, 0:200] = b_ids[...]
        idrows[1:2, 0:200] = s_rows[...]
        idrows[2:3, 0:100] = r_rows[...]
        row = iota((256, 256), 0)
        by_block = one_hot(row == idrows[0:1, :]).astype(bf16)
        by_row = one_hot(row == idrows[1:2, :]).astype(bf16)
        perm[...] = lax.dot_general(
            by_row, by_block, (((1,), (1,)), ((), ())), preferred_element_type=f32
        ).astype(bf16)
        place = iota((256, 128), 0)
        name = ((place >> 2) & 7) * 32 + (place >> 5) * 4 + (place & 3)
        pick[...] = one_hot(name == idrows[2:3, 0:128]).T.astype(bf16)

    def prepare_weights():
        wpad[...] = jnp.zeros((288, WW), bf16)
        finish_weights()
        for p in range(9):
            wpad[32 * p : 32 * p + PK, 0:W2] = weight[p // 3, p % 3]

    def prepare_skip():
        square[...] = jnp.zeros((128, 128), f32)
        square[0:C, 0:C] = skip_w[...].astype(f32)
        skip_k[...] = spread_map(square[...], 320, 320, 16).astype(bf16)
        skip_bias[...] = with_parts(
            jnp.zeros((320, 128), f32), column(skip_b[...], 16, C, 320), iota((320, 128), 1), BIAS_LANE
        )

    def prepare_hidden():
        square[...] = jnp.zeros((128, 128), f32)
        square[0:C, 0:HID] = 0.5 * hid_w[...].astype(f32)
        wide = spread_map(square[...], 512, 176, 8)
        bias = column(hid_b[...], 8, HID, 512)
        bias = jnp.concatenate([bias, bias[:, 0:48]], axis=1)
        hid_k[...] = with_parts(wide, bias, iota((512, 176), 1), 160).astype(bf16)

    def prepare_out():
        right = one_hot((iota((HID, 512), 1) >> 3) == iota((HID, 512), 0)).astype(bf16)
        left = jnp.broadcast_to(0.5 * out_w[...].astype(f32), (16, HID)).astype(bf16)
        same = (iota((16, 512), 1) & 7) == iota((16, 512), 0)
        out_k[...] = jnp.where(same, mm(left, right), 0.0).astype(bf16)

    prepare_clear()
    prepare_skip()

    for x in range(2):
        finish_y(x, recv_y, rs_y)
        got = mm(y_fwd[...], recv_y[x].reshape(Y, LW))
        for g in range(G):
            part_g = got[:, 128 * g : 128 * g + 128]
            rows = combine(part_g[0:MY], part_g[MY : 2 * MY], fwd_sign)
            for m in range(3):
                ya[pl.ds(G * m + g, R, stride=24), :] = rows[R * m : R * m + R]
        send_a[:, x] = ya[...].astype(bf16).reshape(R, 24, 128)
        start_e(x, send_a, recv_a, ss_a, rs_a)
    prepare_weights()
    for x in range(2):
        finish_y(x, recv_a, rs_a)

    places = range(3 * G)
    for p in range(R):
        for x in range(2):
            xa[48 * p + 24 * x : 48 * p + 24 * x + 24, :] = recv_a[x, p].astype(f32)
    data = jnp.concatenate(
        [xa[pl.ds(u, 16, stride=24), :] for u in places], axis=1
    ).astype(bf16)
    got = mm(x_fwd[zh], data)
    for u in places:
        part_u = got[:, 128 * u : 128 * u + 128]
        rows = combine(part_u[0:MX], part_u[MX : 2 * MX], fwd_sign)
        for m in range(3):
            xb[pl.ds(3 * G * m + u, R, stride=56), :] = rows[R * m : R * m + R]
    for p in range(R):
        send_b[p] = xb[56 * p : 56 * p + 56, :].astype(bf16)
    exchange(on_z, zh, send_b, recv_b, ss_b, rs_b, beside=prepare_hidden)
    total = recv_b[0].astype(f32)
    for p in range(1, R):
        total = total + recv_b[p].astype(f32)
    pairs[...] = total

    k_row = iota((32, 128), 0)
    k_half = iota((32, 128), 1) & 63
    usual = (k_half < 54) & (lax.rem(k_half, PK) == k_row)
    late = (k_half >= 54) & (k_row < PK)
    own_k = [
        one_hot(usual | (late & (k_half - 54 == k_row))),
        one_hot(usual | (late & (k_half - 44 == k_row))),
    ] * 2 + [one_hot(usual)] * 2
    for p in range(9):
        for g in range(G):
            row = jnp.broadcast_to(pairs[G * p + g : G * p + g + 1, :], (32, 128))
            amat[32 * p : 32 * p + 32, 128 * g : 128 * g + 128] = (row * own_k[g]).astype(bf16)
    compact = mm(amat[...], gather[...]).astype(bf16)
    weights = wpad[...].astype(f32)
    straight = (mm(compact, widen[...]) * weights).astype(bf16)
    crossed = (mm(compact, widen_sw[...]) * weights).astype(bf16)
    mixed = (mm(straight, sum_re[...]) + mm(crossed, sum_im[...])).astype(bf16)
    wide = mm(mixed, spread[...])
    for p in range(9):
        for g in range(G):
            tile = wide[32 * p : 32 * p + 32, 128 * g : 128 * g + 128] * own_k[g]
            mix[G * p + g : G * p + g + 1, :] = jnp.sum(tile, axis=0, keepdims=True)
    send_c[...] = mix[...].astype(bf16)

    def prepare_late():
        prepare_out()
        prepare_rows()

    exchange(on_z, zh, send_c, recv_c, ss_c, rs_c, same=True, beside=prepare_late)

    for p in range(R):
        xc[56 * p : 56 * p + 56, :] = recv_c[p].astype(f32)

    def by_frequency(ref, first, stride):
        return jnp.concatenate(
            [ref[pl.ds(first(m), R, stride=stride), :] for m in range(3)], axis=0
        )

    data = jnp.concatenate(
        [by_frequency(xc, lambda m: 3 * G * m + u, 56) for u in places], axis=1
    ).astype(bf16)
    got = mm(x_bwd[zh], data)
    for u in places:
        part_u = got[:, 128 * u : 128 * u + 128]
        xd[pl.ds(u, 16, stride=24), :] = combine(part_u[0:16], part_u[16:32], -fwd_sign)
    for x in range(2):
        for p in range(R):
            send_d[p, x] = xd[48 * p + 24 * x : 48 * p + 24 * x + 24, :].astype(bf16)
        start_e(x, send_d, recv_d, ss_d, rs_d)

    for x in range(2):
        finish_y(x, recv_d, rs_d)
        xe[...] = recv_d[x].astype(f32).reshape(192, 128)
        data = jnp.concatenate(
            [by_frequency(xe, lambda m: G * m + g, 24) for g in range(G)], axis=1
        ).astype(bf16)
        got = mm(y_bwd[...], data)
        for g in range(G):
            part_g = got[:, 128 * g : 128 * g + 128]
            turned = combine(part_g[0:Y], part_g[Y : 2 * Y], -fwd_sign).astype(bf16)
            send_e[:, x, :, 128 * g : 128 * g + 128] = turned.reshape(R, 16, 128)
        start_y(x, send_e, recv_e, ss_e, rs_e)

    @pl.loop(0, 2)
    def _(x):
        finish_y(x, recv_e, rs_e)
        for t in range(3):
            rows_of = [
                [recv_e[x, n, :, 128 * g : 128 * g + 128].astype(f32) for g in range(G)]
                for n in range(3 * t, min(R, 3 * t + 3))
            ]
            for c in range(C):
                pieces = []
                for n, tiles in enumerate(rows_of):
                    if c < 18:
                        pieces.append((tiles[c // 3], PK * (c % 3), PK * n, PK * n + PK))
                    else:
                        for part_k in range(2):
                            low = PK * n + 10 * part_k
                            tile = tiles[2 * (c - 18) + part_k]
                            pieces.append((tile, 54, low, min(low + 10, PK * n + PK)))
                bias = skip_bias[16 * c : 16 * c + 16, :] if t == 0 else None
                s6[16 * c : 16 * c + 16, 128 * t : 128 * t + 128] = put_together(
                    pieces, bias
                ).astype(bf16)

        for c in range(4):
            cut = slice(256 * c, 256 * c + 256)
            value = mm(s6[...], t_bwd[:, cut]) + mm(skip_k[...], field[x, :, cut])
            halves = value.reshape(C, 2, 8, 256)
            for h in range(2):
                state = twice_gelu(halves[:, h].reshape(160, 256).astype(bf16))
                state = jnp.concatenate([state, jnp.ones((16, 256), bf16)], axis=0)
                hidden = twice_gelu(mm(hid_k[...], state).astype(bf16))
                part[pl.ds(pl.multiple_of(x * 16, 16) + 8 * h, 8), cut] = mm(out_k[...], hidden)[0:8]

    for b in range(8):
        blk[pl.ds(b, 32, stride=8), :] = part[:, 128 * b : 128 * b + 128]

    send_f[...] = mm(perm[...], blk[...].astype(bf16)).astype(bf16).reshape(R, 32, 128)
    exchange(on_z, zh, send_f, recv_f, ss_f, rs_f)
    send_g[...] = mm(regroup[...], recv_f[...].reshape(256, 128)).astype(bf16).reshape(R, 32, 128)
    exchange(on_e, e, send_g, recv_g, ss_g, rs_g)
    owned = mm(pick[...], recv_g[...].reshape(256, 128))
    out[...] = owned[0:100].astype(bf16)
    finish_sends()


def scratch():
    v = pltpu.VMEM
    dma = pltpu.SemaphoreType.DMA
    buffers = [
        v((2, 320, 1024), bf16),
        v((3, 3, PK, W2), bf16),
        v((1024, 384), bf16),
        v((384, 1024), bf16),
        v((48, 128), bf16),
        v((256, 24), bf16),
        v((R, 48, 16), bf16),
        v((R, 32, 24), bf16),
        v((LW, 128), bf16),
        v((128, LW), bf16),
        v((128, WW), bf16),
        v((128, WW), bf16),
        v((WW, 128), bf16),
        v((WW, 128), bf16),
        v((256, 256), bf16),
        v((R, 2, 16, LW), bf16),
        v((2, R, 16, LW), bf16),
        v((192, 128), f32),
        v((R, 2, 24, 128), bf16),
        v((2, R, 24, 128), bf16),
        v((384, 128), f32),
        v((448, 128), f32),
        v((R, 56, 128), bf16),
        v((R, 56, 128), bf16),
        v((56, 128), f32),
        v((288, LW), bf16),
        v((56, 128), f32),
        v((56, 128), bf16),
        v((R, 56, 128), bf16),
        v((448, 128), f32),
        v((384, 128), f32),
        v((R, 2, 24, 128), bf16),
        v((2, R, 24, 128), bf16),
        v((192, 128), f32),
        v((R, 2, 16, LW), bf16),
        v((2, R, 16, LW), bf16),
        v((320, 384), bf16),
        v((32, 1024), f32),
        v((256, 128), f32),
        v((R, 32, 128), bf16),
        v((R, 32, 128), bf16),
        v((R, 32, 128), bf16),
        v((R, 32, 128), bf16),
        v((288, WW), bf16),
        v((256, 256), bf16),
        v((128, 256), bf16),
        v((8, 256), jnp.int32),
        v((128, 128), f32),
        v((320, 320), bf16),
        v((512, 176), bf16),
        v((320, 128), f32),
        v((16, 512), bf16),
    ]
    one, by_x = [dma((1,))] * 2, [dma((2,))] * 2
    sems = [dma((15,))] + by_x + by_x + one + [dma((3,))] * 3 + one + by_x + by_x + one + one
    return buffers + sems


def local(
    field,
    spectral_weight,
    skip_weight,
    skip_bias,
    hidden_weight,
    hidden_bias,
    out_weight,
    block_ids,
    send_rows,
    recv_rows,
):
    tables = [jnp.asarray(t) for t in constants()]
    args = [
        jnp.transpose(field, (0, 2, 1, 3)).reshape(2, 320, Z * T_SIZE),
        spectral_weight.reshape(3, 3, PK, W2),
        skip_weight,
        skip_bias.reshape(1, C),
        hidden_weight,
        hidden_bias.reshape(1, HID),
        out_weight.reshape(1, HID),
        block_ids.reshape(1, 200),
        send_rows.reshape(1, 200),
        recv_rows.reshape(1, 100),
    ] + tables
    vmem = pl.BlockSpec(memory_space=pltpu.VMEM)
    hbm = pl.BlockSpec(memory_space=pl.ANY)
    result = pl.pallas_call(
        kernel,
        out_shape=jax.ShapeDtypeStruct((100, 128), bf16),
        in_specs=[hbm] * 2 + [vmem] * 8 + [hbm] * len(tables),
        out_specs=vmem,
        scratch_shapes=scratch(),
        compiler_params=pltpu.CompilerParams(
            collective_id=0, has_side_effects=True, vmem_limit_bytes=56 * 1024 * 1024
        ),
    )(*args)
    return result.reshape(1, 1, 100, 128)


def solution(mesh):
    placed = (
        P("gx", "gy", None, None),
        P("gx", "gy", None),
        P(),
        P(),
        P(),
        P(),
        P(),
        P("gx", "gy", None),
        P("gx", "gy", None),
        P("gx", "gy", None),
    )
    return jax.shard_map(
        local, mesh=mesh, in_specs=placed, out_specs=P("gx", "gy", None, None), check_vma=False
    )
```

```python
import functools
import math

import jax
import jax.numpy as jnp
import ml_dtypes
import numpy as np
from jax import lax
from jax.experimental import pallas as pl
from jax.experimental.pallas import tpu as pltpu
from jax.sharding import PartitionSpec as P

C = 20
HID = 64
MX = 24
MY = 24
MZ = 12
MT = 12
Z = 32
T_SIZE = 32
X = 128
Y = 128
KZT = MZ * MT
PK = 18
G = 6
R = 8
LW = G * 128
LS = LW // 2
WW = 896
W2 = 2 * C * C
BIAS_LANE = 60
FAR_FIRST = (4, 3, 5, 2, 6, 1, 7)
MESH = pl.DeviceIdType.MESH
f32 = jnp.float32
bf16 = jnp.bfloat16
GA = math.sqrt(2.0 / math.pi)
GB = GA * 0.044715


def lane_of(ch, r, k):
    if ch < 18:
        return 128 * (ch // 3) + 64 * r + PK * (ch % 3) + k
    tile = 2 * (ch - 18) + k // 10
    return 128 * tile + 64 * r + 54 + k % 10


def constants():
    half = ml_dtypes.bfloat16

    def cos_sin(f, n, length):
        a = 2.0 * np.pi * ((f * n) % length) / length
        return np.cos(a), np.sin(a)

    q = np.arange(Z * T_SIZE)
    forward = np.zeros((Z * T_SIZE, 384))
    backward = np.zeros((384, Z * T_SIZE))
    for j in range(R):
        for k in range(PK):
            kk = PK * j + k
            fz, ft = kk % MZ - MZ // 2, kk // MZ - MT // 2
            a = 2.0 * np.pi * (((fz * (q % Z)) % Z) / Z + ((ft * (q // Z)) % T_SIZE) / T_SIZE)
            lane = 128 * (j // 3) + PK * (j % 3) + k
            forward[:, lane] = np.cos(a) / math.sqrt(Z * T_SIZE)
            forward[:, lane + 64] = -np.sin(a) / math.sqrt(Z * T_SIZE)
            backward[lane] = np.cos(a) / math.sqrt(MX * MY * KZT)
            backward[lane + 64] = -np.sin(a) / math.sqrt(MX * MY * KZT)
    backward[BIAS_LANE : BIAS_LANE + 3] = 1.0
    order = (3 * np.arange(R)[None, :] + np.arange(3)[:, None]).reshape(-1)
    fy = order - MY // 2
    c, s = cos_sin(fy[:, None], np.arange(Y)[None, :], Y)
    y_fwd = np.concatenate([c, s], 0) / math.sqrt(Y)
    y_bwd = np.concatenate([c.T, s.T], 0)
    fx = order - MX // 2
    x_fwd = np.zeros((R, 48, 16))
    x_bwd = np.zeros((R, 32, 24))
    for zh in range(R):
        x = (16 * zh + 2 * np.arange(R)[None, :] + np.arange(2)[:, None]).reshape(-1)
        c, s = cos_sin(fx[:, None], x[None, :], X)
        x_fwd[zh] = np.concatenate([c, s], 0) / math.sqrt(X)
        x_bwd[zh] = np.concatenate([c.T, s.T], 0)
    gather = np.zeros((LW, 128))
    spread = np.zeros((128, LW))
    for ch in range(C):
        for r in range(2):
            for k in range(PK):
                gather[lane_of(ch, r, k), 64 * r + ch] = 1.0
                spread[64 * r + ch, lane_of(ch, r, k)] = 1.0
    widen = np.zeros((128, WW))
    widen_swapped = np.zeros((128, WW))
    sum_re = np.zeros((WW, 128))
    sum_im = np.zeros((WW, 128))
    for r in range(2):
        for ch in range(C):
            for d in range(C):
                col = 400 * r + C * ch + d
                widen[64 * r + ch, col] = 1.0
                widen_swapped[64 * (1 - r) + ch, col] = 1.0
                sum_re[col, d] = 1.0 - 2.0 * r
                sum_im[col, 64 + d] = 1.0
    regroup = np.zeros((256, 256))
    for e in range(R):
        for zh in range(R):
            for n in range(4):
                regroup[32 * e + 4 * zh + n, 32 * zh + 4 * e + n] = 1.0
    tables = (
        forward, backward, y_fwd, y_bwd, x_fwd, x_bwd, gather, spread,
        widen, widen_swapped, sum_re, sum_im, regroup,
    )
    return [t.astype(half) for t in tables]


def mm(a, b):
    return lax.dot_general(a, b, (((1,), (0,)), ((), ())), preferred_element_type=f32)


def iota(shape, dim):
    return lax.broadcasted_iota(jnp.int32, shape, dim)


def one_hot(mask):
    return jnp.where(mask, 1.0, 0.0).astype(f32)


def twice_gelu(v):
    return v + v * jnp.tanh(v * (GA + GB * (v * v)))


def kernel(*refs):
    (
        field_in, weight_in, skip_w, skip_b, hid_w, hid_b, out_w, b_ids, s_rows, r_rows,
        t_fwd_in, t_bwd_in, y_fwd_in, y_bwd_in, x_fwd_in, x_bwd_in, gather_in, spread_in,
        widen_in, widen_sw_in, sum_re_in, sum_im_in, regroup_in,
        out,
        field, weight, t_fwd, t_bwd, y_fwd, y_bwd, x_fwd, x_bwd, gather, spread,
        widen, widen_sw, sum_re, sum_im, regroup,
        send_y, recv_y, ya, send_a, recv_a, xa, xb, send_b, recv_b,
        pairs, amat, mix, send_c, recv_c, xc, xd, send_d, recv_d, xe, send_e, recv_e,
        s6, part, blk, send_f, recv_f, send_g, recv_g, wpad, perm, pick, idrows, square, skip_k, hid_k,
        skip_bias, out_k,
        fetched,
        ss_y, rs_y, ss_a, rs_a, ss_b, rs_b, ss_p, rs_p, ls_p, ss_c, rs_c,
        ss_d, rs_d, ss_e, rs_e, ss_f, rs_f, ss_g, rs_g,
    ) = refs
    i = lax.axis_index("gx")
    j = lax.axis_index("gy")
    zh = lax.div(i, R)
    e = lax.rem(i, R)

    def turn(n, d):
        return lax.rem(n + d, R)

    def on_y(d):
        return turn(j, d), (i, turn(j, d))

    def on_z(d):
        return turn(zh, d), (R * turn(zh, d) + e, j)

    def on_e(d):
        return turn(e, d), (R * zh + turn(e, d), j)

    owners = []
    for n in range(3):
        first = MY * (3 * zh + n) + 3 * e
        owners.append((lax.div(first, 9), lax.div(lax.rem(first, 9), 3)))
    sources = []
    for a in range(3):
        first = 9 * i + 3 * a
        jx, jy = lax.div(first, MY), lax.rem(first, MY)
        sources.append((R * zh + lax.div(jy, 3), lax.rem(jx, 3)))

    barrier = pltpu.get_barrier_semaphore()
    for near in (on_y, on_z, on_e):
        for d in range(1, R):
            pl.semaphore_signal(barrier, inc=1, device_id=near(d)[1], device_id_type=MESH)

    fetch = []
    wanted = [
        (t_fwd_in, t_fwd), (field_in.at[0], field.at[0]), (field_in.at[1], field.at[1]),
        (y_fwd_in, y_fwd), (x_fwd_in, x_fwd), (gather_in, gather),
        (widen_in, widen), (widen_sw_in, widen_sw), (sum_re_in, sum_re), (sum_im_in, sum_im),
        (spread_in, spread), (x_bwd_in, x_bwd), (y_bwd_in, y_bwd), (t_bwd_in, t_bwd),
        (regroup_in, regroup),
    ]
    for n, (source, target) in enumerate(wanted):
        fetch.append(pltpu.make_async_copy(source, target, fetched.at[n]))
        fetch[n].start()

    def await_bytes(view, sem):
        pltpu.make_async_copy(view, view, sem).wait()

    def start(near, me, send, recv, send_sem, recv_sem):
        for d in FAR_FIRST:
            peer, device = near(d)
            pltpu.make_async_remote_copy(
                src_ref=send(peer),
                dst_ref=recv(me),
                send_sem=send_sem,
                recv_sem=recv_sem,
                device_id=device,
                device_id_type=MESH,
            ).start()

    def trade(near, me, s, send, recv, send_sem, recv_sem):
        start(
            near, me, lambda p: send.at[p, s], lambda p: recv.at[s, p], send_sem.at[s], recv_sem.at[s]
        )
        pltpu.make_async_copy(send.at[me, s], recv.at[s, me], recv_sem.at[s]).start()

    def trade_same(near, me, s, send, recv, send_sem, recv_sem):
        start(near, me, lambda p: send.at[s], lambda p: recv.at[s, p], send_sem.at[s], recv_sem.at[s])
        pltpu.make_async_copy(send.at[s], recv.at[s, me], recv_sem.at[s]).start()

    def finish(s, recv, recv_sem):
        await_bytes(recv.at[s], recv_sem.at[s])

    def weights_copy(n, a, device):
        return pltpu.make_async_remote_copy(
            src_ref=weight_in.at[n],
            dst_ref=weight.at[a],
            send_sem=ss_p.at[n],
            recv_sem=rs_p.at[a],
            device_id=(device, j),
            device_id_type=MESH,
        )

    def weights_kept(n, a):
        return pltpu.make_async_copy(weight_in.at[n], weight.at[a], ls_p.at[n])

    def start_weights():
        for n, (device, a) in enumerate(sources):

            @pl.when(device != i)
            def _():
                weights_copy(n, a, device).start()

            @pl.when(device == i)
            def _():
                weights_kept(n, a).start()

    def finish_weights():
        for n, (device, a) in enumerate(sources):

            @pl.when(device == i)
            def _():
                weights_kept(n, a).wait()

        for a, (device, n) in enumerate(owners):

            @pl.when(device != i)
            def _():
                weights_copy(n, a, device).wait_recv()

    def finish_sends():
        for n, (device, a) in enumerate(sources):

            @pl.when(device != i)
            def _():
                weights_copy(n, a, device).wait_send()

        for recv, send_sem in (
            (recv_y, ss_y), (recv_a, ss_a), (recv_b, ss_b), (recv_c, ss_c), (recv_d, ss_d),
            (recv_e, ss_e), (recv_f, ss_f), (recv_g, ss_g),
        ):
            for n in range(recv.shape[0]):
                await_bytes(recv.at[n, pl.ds(0, R - 1)], send_sem.at[n])

    lane = iota((1, 128), 1)
    in_half = lane & 63
    fwd_sign = jnp.where(lane < 64, 1.0, -1.0)

    def lanes_in(low, high):
        return (in_half >= low) & (in_half < high)

    def put_together(pieces, total=None):
        if total is None:
            total = jnp.zeros(pieces[0][0].shape, f32)
        for rows, origin, low, high in pieces:
            shift = (low - origin) % 128
            moved = rows if shift == 0 else pltpu.roll(rows, shift, 1)
            total = jnp.where(lanes_in(low, high), moved, total)
        return total

    def combine(cosines, sines, sign):
        return cosines + sign * pltpu.roll(sines, 64, 1)

    rows_of = {}

    def along_zt(channels):
        runs = []
        for x in range(2):
            for low, high in channels:
                runs.append(field[x, 16 * low : 16 * high, :])
        got = mm(jnp.concatenate(runs, axis=0), t_fwd[...])
        row = 0
        for x in range(2):
            for low, high in channels:
                for c in range(low, high):
                    rows_of[x, c] = got[row : row + 16]
                    row += 16

    def place_zt(s):
        for x in range(2):
            for j_to in range(R):
                t, n = j_to // 3, j_to % 3
                lanes = slice(128 * t, 128 * t + 128)
                for g in range(3 * s, 3 * s + 3):
                    pieces = [
                        (rows_of[x, 3 * g + m][:, lanes], PK * n, PK * m, PK * m + PK)
                        for m in range(3)
                    ]
                    if g < 4:
                        cut = 10 * (g % 2)
                        last = rows_of[x, 18 + g // 2][:, lanes]
                        pieces.append((last, PK * n + cut, 54, 54 + min(10, PK - cut)))
                    at = 128 * (g - 3 * s)
                    send_y[j_to, s, x, :, at : at + 128] = put_together(pieces).astype(bf16)

    for n in range(3):
        fetch[n].wait()
    along_zt([(0, 9), (18, 20)])
    place_zt(0)
    pl.semaphore_wait(barrier, 3 * (R - 1))
    trade(on_y, j, 0, send_y, recv_y, ss_y, rs_y)
    start_weights()
    along_zt([(9, 18)])
    place_zt(1)
    trade(on_y, j, 1, send_y, recv_y, ss_y, rs_y)
    for copy in fetch[3:]:
        copy.wait()

    def spread_map(values, rows, cols, places):
        shift = places.bit_length() - 1
        left = one_hot((iota((rows, 128), 0) >> shift) == iota((rows, 128), 1)).astype(bf16)
        right = one_hot((iota((128, cols), 1) >> shift) == iota((128, cols), 0)).astype(bf16)
        wide = mm(mm(left, values.T.astype(bf16)).astype(bf16), right)
        same = (iota((rows, cols), 0) & (places - 1)) == (iota((rows, cols), 1) & (places - 1))
        return jnp.where(same, wide, 0.0)

    def with_parts(matrix, values, at, first):
        for n in range(3):
            half = values.astype(bf16).astype(f32)
            matrix = jnp.where(at == first + n, half, matrix)
            values = values - half
        return matrix

    def column(values, places, width, rows):
        shift = places.bit_length() - 1
        at = one_hot((iota((rows, width), 0) >> shift) == iota((rows, width), 1))
        return jnp.broadcast_to(jnp.sum(at * values, axis=1, keepdims=True), (rows, 128))

    def prepare_clear():
        for ref in (ya, xb, xd, mix):
            ref[...] = jnp.zeros(ref.shape, f32)

    def prepare_rows():
        idrows[...] = jnp.full((8, 256), -1, jnp.int32)
        idrows[0:1, 0:200] = b_ids[...]
        idrows[1:2, 0:200] = s_rows[...]
        idrows[2:3, 0:100] = r_rows[...]
        row = iota((256, 256), 0)
        by_block = one_hot(row == idrows[0:1, :]).astype(bf16)
        by_row = one_hot(row == idrows[1:2, :]).astype(bf16)
        perm[...] = lax.dot_general(
            by_row, by_block, (((1,), (1,)), ((), ())), preferred_element_type=f32
        ).astype(bf16)
        place = iota((256, 128), 0)
        name = ((place >> 2) & 7) * 32 + (place >> 5) * 4 + (place & 3)
        pick[...] = one_hot(name == idrows[2:3, 0:128]).T.astype(bf16)

    def prepare_weights():
        wpad[...] = jnp.zeros((288, WW), bf16)
        finish_weights()
        for p in range(9):
            wpad[32 * p : 32 * p + PK, 0:W2] = weight[p // 3, p % 3]

    def prepare_skip():
        square[...] = jnp.zeros((128, 128), f32)
        square[0:C, 0:C] = skip_w[...].astype(f32)
        skip_k[...] = spread_map(square[...], 320, 320, 16).astype(bf16)
        skip_bias[...] = with_parts(
            jnp.zeros((320, 128), f32), column(skip_b[...], 16, C, 320), iota((320, 128), 1), BIAS_LANE
        )

    def prepare_hidden():
        square[...] = jnp.zeros((128, 128), f32)
        square[0:C, 0:HID] = 0.5 * hid_w[...].astype(f32)
        wide = spread_map(square[...], 512, 176, 8)
        bias = column(hid_b[...], 8, HID, 512)
        bias = jnp.concatenate([bias, bias[:, 0:48]], axis=1)
        hid_k[...] = with_parts(wide, bias, iota((512, 176), 1), 160).astype(bf16)

    def prepare_out():
        right = one_hot((iota((HID, 512), 1) >> 3) == iota((HID, 512), 0)).astype(bf16)
        left = jnp.broadcast_to(0.5 * out_w[...].astype(f32), (16, HID)).astype(bf16)
        same = (iota((16, 512), 1) & 7) == iota((16, 512), 0)
        out_k[...] = jnp.where(same, mm(left, right), 0.0).astype(bf16)

    prepare_clear()
    prepare_skip()

    def along_y(s):
        finish(s, recv_y, rs_y)
        data = jnp.concatenate(
            [recv_y[s, :, x].reshape(Y, LS) for x in range(2)], axis=1
        )
        got = mm(y_fwd[...], data)
        for x in range(2):
            for g in range(3):
                part_g = got[:, LS * x + 128 * g : LS * x + 128 * g + 128]
                rows = combine(part_g[0:MY], part_g[MY : 2 * MY], fwd_sign)
                for m in range(3):
                    ya[pl.ds(9 * x + 3 * m + g, R, stride=24), :] = rows[R * m : R * m + R]
        send_a[:, s] = ya[...].astype(bf16).reshape(R, 24, 128)
        trade(on_e, e, s, send_a, recv_a, ss_a, rs_a)

    def along_x(s):
        finish(s, recv_a, rs_a)
        xa[...] = recv_a[s].astype(f32).reshape(192, 128)
        data = jnp.concatenate(
            [
                jnp.concatenate(
                    [xa[pl.ds(9 * x + u, R, stride=24), :] for x in range(2)], axis=0
                )
                for u in range(9)
            ],
            axis=1,
        ).astype(bf16)
        got = mm(x_fwd[zh], data)
        for u in range(9):
            part_u = got[:, 128 * u : 128 * u + 128]
            rows = combine(part_u[0:MX], part_u[MX : 2 * MX], fwd_sign)
            for m in range(3):
                xb[pl.ds(9 * m + u, R, stride=32), :] = rows[R * m : R * m + R]
        send_b[:, s] = xb[...].astype(bf16).reshape(R, 32, 128)
        trade(on_z, zh, s, send_b, recv_b, ss_b, rs_b)

    along_y(0)
    along_x(0)
    along_y(1)
    prepare_weights()
    along_x(1)
    prepare_hidden()
    for s in range(2):
        finish(s, recv_b, rs_b)
        total = recv_b[s, 0].astype(f32)
        for p in range(1, R):
            total = total + recv_b[s, p].astype(f32)
        pairs[s] = total

    k_row = iota((32, 128), 0)
    k_half = iota((32, 128), 1) & 63
    usual = (k_half < 54) & (lax.rem(k_half, PK) == k_row)
    late = (k_half >= 54) & (k_row < PK)
    own_k = [
        one_hot(usual | (late & (k_half - 54 == k_row))),
        one_hot(usual | (late & (k_half - 44 == k_row))),
    ] * 2 + [one_hot(usual)] * 2
    for p in range(9):
        for g in range(G):
            row = jnp.broadcast_to(pairs[g // 3, 3 * p + g % 3 : 3 * p + g % 3 + 1, :], (32, 128))
            amat[32 * p : 32 * p + 32, 128 * g : 128 * g + 128] = (row * own_k[g]).astype(bf16)
    compact = mm(amat[...], gather[...]).astype(bf16)
    weights = wpad[...].astype(f32)
    straight = (mm(compact, widen[...]) * weights).astype(bf16)
    crossed = (mm(compact, widen_sw[...]) * weights).astype(bf16)
    mixed = (mm(straight, sum_re[...]) + mm(crossed, sum_im[...])).astype(bf16)
    for s in range(2):
        wide = mm(mixed, spread[:, LS * s : LS * s + LS])
        for p in range(9):
            for g in range(3):
                tile = wide[32 * p : 32 * p + 32, 128 * g : 128 * g + 128] * own_k[3 * s + g]
                mix[s, 3 * p + g : 3 * p + g + 1, :] = jnp.sum(tile, axis=0, keepdims=True)
        send_c[s] = mix[s].astype(bf16)
        trade_same(on_z, zh, s, send_c, recv_c, ss_c, rs_c)
    prepare_out()
    prepare_rows()

    def by_frequency(ref, first, stride):
        return jnp.concatenate(
            [ref[pl.ds(first(m), R, stride=stride), :] for m in range(3)], axis=0
        )

    def back_x(s):
        finish(s, recv_c, rs_c)
        xc[...] = recv_c[s].astype(f32).reshape(256, 128)
        data = jnp.concatenate(
            [by_frequency(xc, lambda m: 9 * m + u, 32) for u in range(9)], axis=1
        ).astype(bf16)
        got = mm(x_bwd[zh], data)
        for u in range(9):
            part_u = got[:, 128 * u : 128 * u + 128]
            rows = combine(part_u[0:16], part_u[16:32], -fwd_sign)
            for x in range(2):
                xd[pl.ds(9 * x + u, R, stride=24), :] = rows[R * x : R * x + R]
        send_d[:, s] = xd[...].astype(bf16).reshape(R, 24, 128)
        trade(on_e, e, s, send_d, recv_d, ss_d, rs_d)

    def back_y(s):
        finish(s, recv_d, rs_d)
        xe[...] = recv_d[s].astype(f32).reshape(192, 128)
        for x in range(2):
            data = jnp.concatenate(
                [by_frequency(xe, lambda m: 9 * x + 3 * m + g, 24) for g in range(3)], axis=1
            ).astype(bf16)
            got = mm(y_bwd[...], data)
            for g in range(3):
                part_g = got[:, 128 * g : 128 * g + 128]
                turned = combine(part_g[0:Y], part_g[Y : 2 * Y], -fwd_sign).astype(bf16)
                send_e[:, 2 * s + x, :, 128 * g : 128 * g + 128] = turned.reshape(R, 16, 128)
            trade(on_y, j, 2 * s + x, send_e, recv_e, ss_e, rs_e)

    back_x(0)
    back_y(0)
    back_x(1)
    back_y(1)

    def columns(x, s, channels):
        for t in range(3):
            tiles = {}
            for n in range(3 * t, min(R, 3 * t + 3)):
                for g in range(3 * s + 3):
                    at = 128 * (g % 3)
                    tiles[n - 3 * t, g] = recv_e[2 * (g // 3) + x, n, :, at : at + 128].astype(f32)
            for c in channels:
                pieces = []
                for n in range(min(3, R - 3 * t)):
                    if c < 18:
                        pieces.append((tiles[n, c // 3], PK * (c % 3), PK * n, PK * n + PK))
                    else:
                        for part_k in range(2):
                            low = PK * n + 10 * part_k
                            tile = tiles[n, 2 * (c - 18) + part_k]
                            pieces.append((tile, 54, low, min(low + 10, PK * n + PK)))
                bias = skip_bias[16 * c : 16 * c + 16, :] if t == 0 else None
                s6[x, 16 * c : 16 * c + 16, 128 * t : 128 * t + 128] = put_together(
                    pieces, bias
                ).astype(bf16)

    for x in range(2):
        finish(x, recv_e, rs_e)
        columns(x, 0, [*range(9), 18])

    @pl.loop(0, 2)
    def _(x):
        finish(2 + x, recv_e, rs_e)
        columns(x, 1, [*range(9, 18), 19])
        for c in range(4):
            cut = slice(256 * c, 256 * c + 256)
            value = mm(s6[x], t_bwd[:, cut]) + mm(skip_k[...], field[x, :, cut])
            halves = value.reshape(C, 2, 8, 256)
            for h in range(2):
                state = twice_gelu(halves[:, h].reshape(160, 256)).astype(bf16)
                state = jnp.concatenate([state, jnp.ones((16, 256), bf16)], axis=0)
                hidden = twice_gelu(mm(hid_k[...], state)).astype(bf16)
                part[pl.ds(pl.multiple_of(x * 16, 16) + 8 * h, 8), cut] = mm(out_k[...], hidden)[0:8]

    for b in range(8):
        blk[pl.ds(b, 32, stride=8), :] = part[:, 128 * b : 128 * b + 128]

    send_f[:, 0] = mm(perm[...], blk[...].astype(bf16)).astype(bf16).reshape(R, 32, 128)
    trade(on_z, zh, 0, send_f, recv_f, ss_f, rs_f)
    finish(0, recv_f, rs_f)
    send_g[:, 0] = mm(regroup[...], recv_f[0].reshape(256, 128)).astype(bf16).reshape(R, 32, 128)
    trade(on_e, e, 0, send_g, recv_g, ss_g, rs_g)
    finish(0, recv_g, rs_g)
    owned = mm(pick[...], recv_g[0].reshape(256, 128))
    out[...] = owned[0:100].astype(bf16)
    finish_sends()


def scratch():
    v = pltpu.VMEM
    dma = pltpu.SemaphoreType.DMA
    buffers = [
        v((2, 320, 1024), bf16),
        v((3, 3, PK, W2), bf16),
        v((1024, 384), bf16),
        v((384, 1024), bf16),
        v((48, 128), bf16),
        v((256, 24), bf16),
        v((R, 48, 16), bf16),
        v((R, 32, 24), bf16),
        v((LW, 128), bf16),
        v((128, LW), bf16),
        v((128, WW), bf16),
        v((128, WW), bf16),
        v((WW, 128), bf16),
        v((WW, 128), bf16),
        v((256, 256), bf16),
        v((R, 2, 2, 16, LS), bf16),
        v((2, R, 2, 16, LS), bf16),
        v((192, 128), f32),
        v((R, 2, 24, 128), bf16),
        v((2, R, 24, 128), bf16),
        v((192, 128), f32),
        v((256, 128), f32),
        v((R, 2, 32, 128), bf16),
        v((2, R, 32, 128), bf16),
        v((2, 32, 128), f32),
        v((288, LW), bf16),
        v((2, 32, 128), f32),
        v((2, 32, 128), bf16),
        v((2, R, 32, 128), bf16),
        v((256, 128), f32),
        v((192, 128), f32),
        v((R, 2, 24, 128), bf16),
        v((2, R, 24, 128), bf16),
        v((192, 128), f32),
        v((R, 4, 16, LS), bf16),
        v((4, R, 16, LS), bf16),
        v((2, 320, 384), bf16),
        v((32, 1024), f32),
        v((256, 128), f32),
        v((R, 1, 32, 128), bf16),
        v((1, R, 32, 128), bf16),
        v((R, 1, 32, 128), bf16),
        v((1, R, 32, 128), bf16),
        v((288, WW), bf16),
        v((256, 256), bf16),
        v((128, 256), bf16),
        v((8, 256), jnp.int32),
        v((128, 128), f32),
        v((320, 320), bf16),
        v((512, 176), bf16),
        v((320, 128), f32),
        v((16, 512), bf16),
    ]
    one, two, four = [dma((1,))] * 2, [dma((2,))] * 2, [dma((4,))] * 2
    sems = [dma((15,))] + two * 3 + [dma((3,))] * 3 + two * 2 + four + one * 2
    return buffers + sems


def local(
    field,
    spectral_weight,
    skip_weight,
    skip_bias,
    hidden_weight,
    hidden_bias,
    out_weight,
    block_ids,
    send_rows,
    recv_rows,
):
    tables = [jnp.asarray(t) for t in constants()]
    args = [
        jnp.transpose(field, (0, 2, 1, 3)).reshape(2, 320, Z * T_SIZE),
        spectral_weight.reshape(3, 3, PK, W2),
        skip_weight,
        skip_bias.reshape(1, C),
        hidden_weight,
        hidden_bias.reshape(1, HID),
        out_weight.reshape(1, HID),
        block_ids.reshape(1, 200),
        send_rows.reshape(1, 200),
        recv_rows.reshape(1, 100),
    ] + tables
    vmem = pl.BlockSpec(memory_space=pltpu.VMEM)
    hbm = pl.BlockSpec(memory_space=pl.ANY)
    result = pl.pallas_call(
        kernel,
        out_shape=jax.ShapeDtypeStruct((100, 128), bf16),
        in_specs=[hbm] * 2 + [vmem] * 8 + [hbm] * len(tables),
        out_specs=vmem,
        scratch_shapes=scratch(),
        compiler_params=pltpu.CompilerParams(
            collective_id=0, has_side_effects=True, vmem_limit_bytes=56 * 1024 * 1024
        ),
    )(*args)
    return result.reshape(1, 1, 100, 128)


def solution(mesh):
    placed = (
        P("gx", "gy", None, None),
        P("gx", "gy", None),
        P(),
        P(),
        P(),
        P(),
        P(),
        P("gx", "gy", None),
        P("gx", "gy", None),
        P("gx", "gy", None),
    )
    return jax.shard_map(
        local, mesh=mesh, in_specs=placed, out_specs=P("gx", "gy", None, None), check_vma=False
    )
```

```python
import functools
import math

import jax
import jax.numpy as jnp
import ml_dtypes
import numpy as np
from jax import lax
from jax.experimental import pallas as pl
from jax.experimental.pallas import tpu as pltpu
from jax.sharding import PartitionSpec as P

C = 20
HID = 64
MX = 24
MY = 24
MZ = 12
MT = 12
Z = 32
T_SIZE = 32
X = 128
Y = 128
KZT = MZ * MT
PK = 18
G = 6
R = 8
LW = G * 128
WW = 896
W2 = 2 * C * C
BIAS_LANE = 60
FAR_FIRST = (4, 3, 5, 2, 6, 1, 7)
MESH = pl.DeviceIdType.MESH
f32 = jnp.float32
bf16 = jnp.bfloat16
GA = math.sqrt(2.0 / math.pi)
GB = GA * 0.044715


def lane_of(ch, r, k):
    if ch < 18:
        return 128 * (ch // 3) + 64 * r + PK * (ch % 3) + k
    tile = 2 * (ch - 18) + k // 10
    return 128 * tile + 64 * r + 54 + k % 10


def constants():
    half = ml_dtypes.bfloat16

    def cos_sin(f, n, length):
        a = 2.0 * np.pi * ((f * n) % length) / length
        return np.cos(a), np.sin(a)

    q = np.arange(Z * T_SIZE)
    forward = np.zeros((Z * T_SIZE, 384))
    backward = np.zeros((384, Z * T_SIZE))
    for j in range(R):
        for k in range(PK):
            kk = PK * j + k
            fz, ft = kk % MZ - MZ // 2, kk // MZ - MT // 2
            a = 2.0 * np.pi * (((fz * (q % Z)) % Z) / Z + ((ft * (q // Z)) % T_SIZE) / T_SIZE)
            lane = 128 * (j // 3) + PK * (j % 3) + k
            forward[:, lane] = np.cos(a) / math.sqrt(Z * T_SIZE)
            forward[:, lane + 64] = -np.sin(a) / math.sqrt(Z * T_SIZE)
            backward[lane] = np.cos(a) / math.sqrt(MX * MY * KZT)
            backward[lane + 64] = -np.sin(a) / math.sqrt(MX * MY * KZT)
    backward[BIAS_LANE : BIAS_LANE + 3] = 1.0
    order = (3 * np.arange(R)[None, :] + np.arange(3)[:, None]).reshape(-1)
    fy = order - MY // 2
    c, s = cos_sin(fy[:, None], np.arange(Y)[None, :], Y)
    y_fwd = np.concatenate([c, s], 0) / math.sqrt(Y)
    y_bwd = np.concatenate([c.T, s.T], 0)
    fx = order - MX // 2
    x_fwd = np.zeros((R, 48, 16))
    x_bwd = np.zeros((R, 32, 24))
    for zh in range(R):
        c, s = cos_sin(fx[:, None], 16 * zh + np.arange(16)[None, :], X)
        x_fwd[zh] = np.concatenate([c, s], 0) / math.sqrt(X)
        x_bwd[zh] = np.concatenate([c.T, s.T], 0)
    gather = np.zeros((LW, 128))
    spread = np.zeros((128, LW))
    for ch in range(C):
        for r in range(2):
            for k in range(PK):
                gather[lane_of(ch, r, k), 64 * r + ch] = 1.0
                spread[64 * r + ch, lane_of(ch, r, k)] = 1.0
    widen = np.zeros((128, WW))
    widen_swapped = np.zeros((128, WW))
    sum_re = np.zeros((WW, 128))
    sum_im = np.zeros((WW, 128))
    for r in range(2):
        for ch in range(C):
            for d in range(C):
                col = 400 * r + C * ch + d
                widen[64 * r + ch, col] = 1.0
                widen_swapped[64 * (1 - r) + ch, col] = 1.0
                sum_re[col, d] = 1.0 - 2.0 * r
                sum_im[col, 64 + d] = 1.0
    regroup = np.zeros((256, 256))
    for e in range(R):
        for zh in range(R):
            for n in range(4):
                regroup[32 * e + 4 * zh + n, 32 * zh + 4 * e + n] = 1.0
    tables = (
        forward, backward, y_fwd, y_bwd, x_fwd, x_bwd, gather, spread,
        widen, widen_swapped, sum_re, sum_im, regroup,
    )
    return [t.astype(half) for t in tables]


def mm(a, b):
    return lax.dot_general(a, b, (((1,), (0,)), ((), ())), preferred_element_type=f32)


def iota(shape, dim):
    return lax.broadcasted_iota(jnp.int32, shape, dim)


def one_hot(mask):
    return jnp.where(mask, 1.0, 0.0).astype(f32)


def twice_gelu(v):
    return v + v * jnp.tanh(v * (GA + GB * (v * v)))


def kernel(*refs):
    (
        field_in, weight_in, skip_w, skip_b, hid_w, hid_b, out_w, b_ids, s_rows, r_rows,
        t_fwd_in, t_bwd_in, y_fwd_in, y_bwd_in, x_fwd_in, x_bwd_in, gather_in, spread_in,
        widen_in, widen_sw_in, sum_re_in, sum_im_in, regroup_in,
        out,
        field, weight, t_fwd, t_bwd, y_fwd, y_bwd, x_fwd, x_bwd, gather, spread,
        widen, widen_sw, sum_re, sum_im, regroup,
        send_y, recv_y, ya, send_a, recv_a, xa, xb, send_b, recv_b,
        pairs, amat, mix, send_c, recv_c, xc, xd, send_d, recv_d, xe, send_e, recv_e,
        s6, part, blk, send_f, recv_f, send_g, recv_g, wpad, perm, pick, idrows, square, skip_k, hid_k,
        skip_bias, out_k,
        fetched,
        ss_y, rs_y, ss_a, rs_a, ss_b, rs_b, ss_p, rs_p, ls_p, ss_c, rs_c,
        ss_d, rs_d, ss_e, rs_e, ss_f, rs_f, ss_g, rs_g,
    ) = refs
    i = lax.axis_index("gx")
    j = lax.axis_index("gy")
    zh = lax.div(i, R)
    e = lax.rem(i, R)

    def turn(n, d):
        return lax.rem(n + d, R)

    def on_y(d):
        return turn(j, d), (i, turn(j, d))

    def on_z(d):
        return turn(zh, d), (R * turn(zh, d) + e, j)

    def on_e(d):
        return turn(e, d), (R * zh + turn(e, d), j)

    owners = []
    for n in range(3):
        first = MY * (3 * zh + n) + 3 * e
        owners.append((lax.div(first, 9), lax.div(lax.rem(first, 9), 3)))
    sources = []
    for a in range(3):
        first = 9 * i + 3 * a
        jx, jy = lax.div(first, MY), lax.rem(first, MY)
        sources.append((R * zh + lax.div(jy, 3), lax.rem(jx, 3)))

    fetch = []
    wanted = [
        (t_fwd_in, t_fwd), (field_in.at[0], field.at[0]), (field_in.at[1], field.at[1]),
        (y_fwd_in, y_fwd), (x_fwd_in, x_fwd), (gather_in, gather),
        (widen_in, widen), (widen_sw_in, widen_sw), (sum_re_in, sum_re), (sum_im_in, sum_im),
        (spread_in, spread), (x_bwd_in, x_bwd), (y_bwd_in, y_bwd), (t_bwd_in, t_bwd),
        (regroup_in, regroup),
    ]
    for n, (source, target) in enumerate(wanted):
        fetch.append(pltpu.make_async_copy(source, target, fetched.at[n]))
    for copy in fetch[:3]:
        copy.start()

    barrier = pltpu.get_barrier_semaphore()
    for near in (on_y, on_z, on_e):
        for d in range(1, R):
            pl.semaphore_signal(barrier, inc=1, device_id=near(d)[1], device_id_type=MESH)

    for copy in fetch[3:]:
        copy.start()

    sent = []

    def await_bytes(view, sem):
        pltpu.make_async_copy(view, view, sem).wait()

    def start(near, me, send, recv, send_sem, recv_sem):
        for d in FAR_FIRST:
            peer, device = near(d)
            pltpu.make_async_remote_copy(
                src_ref=send(peer),
                dst_ref=recv(me),
                send_sem=send_sem,
                recv_sem=recv_sem,
                device_id=device,
                device_id_type=MESH,
            ).start()

    def exchange(near, me, send, recv, send_sem, recv_sem, same=False, beside=None):
        start(
            near, me, (lambda p: send) if same else (lambda p: send.at[p]), lambda p: recv.at[p],
            send_sem.at[0], recv_sem.at[0],
        )
        recv[me] = send[...] if same else send[me]
        seven = recv.at[pl.ds(0, R - 1)]
        sent.append((seven, send_sem.at[0]))
        if beside is not None:
            beside()
        await_bytes(seven, recv_sem.at[0])

    def start_y(x, send, recv, send_sem, recv_sem):
        start(
            on_y, j, lambda p: send.at[p, x], lambda p: recv.at[x, p], send_sem.at[x], recv_sem.at[x]
        )
        recv[x, j] = send[j, x]

    def finish_y(x, recv, recv_sem):
        await_bytes(recv.at[x, pl.ds(0, R - 1)], recv_sem.at[x])

    def start_e(x, send, recv, send_sem, recv_sem):
        start(
            on_e, e, lambda p: send.at[p, x], lambda p: recv.at[x, p], send_sem.at[x], recv_sem.at[x]
        )
        recv[x, e] = send[e, x]

    def weights_copy(n, a, device):
        return pltpu.make_async_remote_copy(
            src_ref=weight_in.at[n],
            dst_ref=weight.at[a],
            send_sem=ss_p.at[n],
            recv_sem=rs_p.at[a],
            device_id=(device, j),
            device_id_type=MESH,
        )

    def weights_kept(n, a):
        return pltpu.make_async_copy(weight_in.at[n], weight.at[a], ls_p.at[n])

    def start_weights():
        for n, (device, a) in enumerate(sources):

            @pl.when(device != i)
            def _():
                weights_copy(n, a, device).start()

            @pl.when(device == i)
            def _():
                weights_kept(n, a).start()

    def finish_weights():
        for n, (device, a) in enumerate(sources):

            @pl.when(device == i)
            def _():
                weights_kept(n, a).wait()

        for a, (device, n) in enumerate(owners):

            @pl.when(device != i)
            def _():
                weights_copy(n, a, device).wait_recv()

    def finish_sends():
        for n, (device, a) in enumerate(sources):

            @pl.when(device != i)
            def _():
                weights_copy(n, a, device).wait_send()

        for view, sem in sent:
            await_bytes(view, sem)
        for recv, send_sem in ((recv_y, ss_y), (recv_a, ss_a), (recv_e, ss_e)):
            for x in range(2):
                await_bytes(recv.at[x, pl.ds(0, R - 1)], send_sem.at[x])

    lane = iota((1, 128), 1)
    in_half = lane & 63
    fwd_sign = jnp.where(lane < 64, 1.0, -1.0)

    def lanes_in(low, high):
        return (in_half >= low) & (in_half < high)

    def put_together(pieces, total=None):
        if total is None:
            total = jnp.zeros(pieces[0][0].shape, f32)
        for rows, origin, low, high in pieces:
            shift = (low - origin) % 128
            moved = rows if shift == 0 else pltpu.roll(rows, shift, 1)
            total = jnp.where(lanes_in(low, high), moved, total)
        return total

    def combine(cosines, sines, sign):
        return cosines + sign * pltpu.roll(sines, 64, 1)

    def along_zt(x):
        got = mm(field[x], t_fwd[...])
        for t in range(3):
            rows_of = [got[16 * c : 16 * c + 16, 128 * t : 128 * t + 128] for c in range(C)]
            for n in range(min(3, R - 3 * t)):
                for g in range(G):
                    pieces = [
                        (rows_of[3 * g + m], PK * n, PK * m, PK * m + PK) for m in range(3)
                    ]
                    if g < 4:
                        cut = 10 * (g % 2)
                        pieces.append(
                            (rows_of[18 + g // 2], PK * n + cut, 54, 54 + min(10, PK - cut))
                        )
                    send_y[3 * t + n, x, :, 128 * g : 128 * g + 128] = put_together(pieces).astype(
                        bf16
                    )

    fetch[0].wait()
    fetch[1].wait()
    along_zt(0)
    pl.semaphore_wait(barrier, 3 * (R - 1))
    start_y(0, send_y, recv_y, ss_y, rs_y)
    start_weights()
    fetch[2].wait()
    along_zt(1)
    start_y(1, send_y, recv_y, ss_y, rs_y)
    for copy in fetch[3:]:
        copy.wait()

    def spread_map(values, rows, cols, places):
        shift = places.bit_length() - 1
        left = one_hot((iota((rows, 128), 0) >> shift) == iota((rows, 128), 1)).astype(bf16)
        right = one_hot((iota((128, cols), 1) >> shift) == iota((128, cols), 0)).astype(bf16)
        wide = mm(mm(left, values.T.astype(bf16)).astype(bf16), right)
        same = (iota((rows, cols), 0) & (places - 1)) == (iota((rows, cols), 1) & (places - 1))
        return jnp.where(same, wide, 0.0)

    def with_parts(matrix, values, at, first):
        for n in range(3):
            half = values.astype(bf16).astype(f32)
            matrix = jnp.where(at == first + n, half, matrix)
            values = values - half
        return matrix

    def column(values, places, width, rows):
        shift = places.bit_length() - 1
        at = one_hot((iota((rows, width), 0) >> shift) == iota((rows, width), 1))
        return jnp.broadcast_to(jnp.sum(at * values, axis=1, keepdims=True), (rows, 128))

    def prepare_clear():
        ya[...] = jnp.zeros((192, 128), f32)
        xb[...] = jnp.zeros((448, 128), f32)
        xd[...] = jnp.zeros((384, 128), f32)
        mix[...] = jnp.zeros((56, 128), f32)

    def prepare_rows():
        idrows[...] = jnp.full((8, 256), -1, jnp.int32)
        idrows[0:1, 0:200] = b_ids[...]
        idrows[1:2, 0:200] = s_rows[...]
        idrows[2:3, 0:100] = r_rows[...]
        row = iota((256, 256), 0)
        by_block = one_hot(row == idrows[0:1, :]).astype(bf16)
        by_row = one_hot(row == idrows[1:2, :]).astype(bf16)
        perm[...] = lax.dot_general(
            by_row, by_block, (((1,), (1,)), ((), ())), preferred_element_type=f32
        ).astype(bf16)
        place = iota((256, 128), 0)
        name = ((place >> 2) & 7) * 32 + (place >> 5) * 4 + (place & 3)
        pick[...] = one_hot(name == idrows[2:3, 0:128]).T.astype(bf16)

    def prepare_weights():
        wpad[...] = jnp.zeros((288, WW), bf16)
        finish_weights()
        for p in range(9):
            wpad[32 * p : 32 * p + PK, 0:W2] = weight[p // 3, p % 3]

    def prepare_skip():
        square[...] = jnp.zeros((128, 128), f32)
        square[0:C, 0:C] = skip_w[...].astype(f32)
        skip_k[...] = spread_map(square[...], 320, 320, 16).astype(bf16)
        skip_bias[...] = with_parts(
            jnp.zeros((320, 128), f32), column(skip_b[...], 16, C, 320), iota((320, 128), 1), BIAS_LANE
        )

    def prepare_hidden():
        square[...] = jnp.zeros((128, 128), f32)
        square[0:C, 0:HID] = 0.5 * hid_w[...].astype(f32)
        wide = spread_map(square[...], 512, 176, 8)
        bias = column(hid_b[...], 8, HID, 512)
        bias = jnp.concatenate([bias, bias[:, 0:48]], axis=1)
        hid_k[...] = with_parts(wide, bias, iota((512, 176), 1), 160).astype(bf16)

    def prepare_out():
        right = one_hot((iota((HID, 512), 1) >> 3) == iota((HID, 512), 0)).astype(bf16)
        left = jnp.broadcast_to(0.5 * out_w[...].astype(f32), (16, HID)).astype(bf16)
        same = (iota((16, 512), 1) & 7) == iota((16, 512), 0)
        out_k[...] = jnp.where(same, mm(left, right), 0.0).astype(bf16)

    prepare_clear()
    prepare_skip()

    for x in range(2):
        finish_y(x, recv_y, rs_y)
        got = mm(y_fwd[...], recv_y[x].reshape(Y, LW))
        for g in range(G):
            part_g = got[:, 128 * g : 128 * g + 128]
            rows = combine(part_g[0:MY], part_g[MY : 2 * MY], fwd_sign)
            for m in range(3):
                ya[pl.ds(G * m + g, R, stride=24), :] = rows[R * m : R * m + R]
        send_a[:, x] = ya[...].astype(bf16).reshape(R, 24, 128)
        start_e(x, send_a, recv_a, ss_a, rs_a)
    prepare_weights()
    for x in range(2):
        finish_y(x, recv_a, rs_a)

    places = range(3 * G)
    for p in range(R):
        for x in range(2):
            xa[48 * p + 24 * x : 48 * p + 24 * x + 24, :] = recv_a[x, p].astype(f32)
    data = jnp.concatenate(
        [xa[pl.ds(u, 16, stride=24), :] for u in places], axis=1
    ).astype(bf16)
    got = mm(x_fwd[zh], data)
    for u in places:
        part_u = got[:, 128 * u : 128 * u + 128]
        rows = combine(part_u[0:MX], part_u[MX : 2 * MX], fwd_sign)
        for m in range(3):
            xb[pl.ds(3 * G * m + u, R, stride=56), :] = rows[R * m : R * m + R]
    for p in range(R):
        send_b[p] = xb[56 * p : 56 * p + 56, :].astype(bf16)
    exchange(on_z, zh, send_b, recv_b, ss_b, rs_b, beside=prepare_hidden)
    total = recv_b[0].astype(f32)
    for p in range(1, R):
        total = total + recv_b[p].astype(f32)
    pairs[...] = total

    k_row = iota((32, 128), 0)
    k_half = iota((32, 128), 1) & 63
    usual = (k_half < 54) & (lax.rem(k_half, PK) == k_row)
    late = (k_half >= 54) & (k_row < PK)
    own_k = [
        one_hot(usual | (late & (k_half - 54 == k_row))),
        one_hot(usual | (late & (k_half - 44 == k_row))),
    ] * 2 + [one_hot(usual)] * 2
    for p in range(9):
        for g in range(G):
            row = jnp.broadcast_to(pairs[G * p + g : G * p + g + 1, :], (32, 128))
            amat[32 * p : 32 * p + 32, 128 * g : 128 * g + 128] = (row * own_k[g]).astype(bf16)
    compact = mm(amat[...], gather[...]).astype(bf16)
    weights = wpad[...].astype(f32)
    straight = (mm(compact, widen[...]) * weights).astype(bf16)
    crossed = (mm(compact, widen_sw[...]) * weights).astype(bf16)
    mixed = (mm(straight, sum_re[...]) + mm(crossed, sum_im[...])).astype(bf16)
    wide = mm(mixed, spread[...])
    for p in range(9):
        for g in range(G):
            tile = wide[32 * p : 32 * p + 32, 128 * g : 128 * g + 128] * own_k[g]
            mix[G * p + g : G * p + g + 1, :] = jnp.sum(tile, axis=0, keepdims=True)
    send_c[...] = mix[...].astype(bf16)

    def prepare_late():
        prepare_out()
        prepare_rows()

    exchange(on_z, zh, send_c, recv_c, ss_c, rs_c, same=True, beside=prepare_late)

    for p in range(R):
        xc[56 * p : 56 * p + 56, :] = recv_c[p].astype(f32)

    def by_frequency(ref, first, stride):
        return jnp.concatenate(
            [ref[pl.ds(first(m), R, stride=stride), :] for m in range(3)], axis=0
        )

    data = jnp.concatenate(
        [by_frequency(xc, lambda m: 3 * G * m + u, 56) for u in places], axis=1
    ).astype(bf16)
    got = mm(x_bwd[zh], data)
    for u in places:
        part_u = got[:, 128 * u : 128 * u + 128]
        xd[pl.ds(u, 16, stride=24), :] = combine(part_u[0:16], part_u[16:32], -fwd_sign)
    for x in range(2):
        for p in range(R):
            send_d[p, x] = xd[48 * p + 24 * x : 48 * p + 24 * x + 24, :].astype(bf16)
    exchange(on_e, e, send_d, recv_d, ss_d, rs_d)

    for x in range(2):
        for p in range(R):
            xe[24 * p : 24 * p + 24, :] = recv_d[p, x].astype(f32)
        data = jnp.concatenate(
            [by_frequency(xe, lambda m: G * m + g, 24) for g in range(G)], axis=1
        ).astype(bf16)
        got = mm(y_bwd[...], data)
        for g in range(G):
            part_g = got[:, 128 * g : 128 * g + 128]
            turned = combine(part_g[0:Y], part_g[Y : 2 * Y], -fwd_sign).astype(bf16)
            send_e[:, x, :, 128 * g : 128 * g + 128] = turned.reshape(R, 16, 128)
        start_y(x, send_e, recv_e, ss_e, rs_e)

    @pl.loop(0, 2)
    def _(x):
        finish_y(x, recv_e, rs_e)
        for t in range(3):
            rows_of = [
                [recv_e[x, n, :, 128 * g : 128 * g + 128].astype(f32) for g in range(G)]
                for n in range(3 * t, min(R, 3 * t + 3))
            ]
            for c in range(C):
                pieces = []
                for n, tiles in enumerate(rows_of):
                    if c < 18:
                        pieces.append((tiles[c // 3], PK * (c % 3), PK * n, PK * n + PK))
                    else:
                        for part_k in range(2):
                            low = PK * n + 10 * part_k
                            tile = tiles[2 * (c - 18) + part_k]
                            pieces.append((tile, 54, low, min(low + 10, PK * n + PK)))
                bias = skip_bias[16 * c : 16 * c + 16, :] if t == 0 else None
                s6[16 * c : 16 * c + 16, 128 * t : 128 * t + 128] = put_together(
                    pieces, bias
                ).astype(bf16)

        for c in range(4):
            cut = slice(256 * c, 256 * c + 256)
            value = mm(s6[...], t_bwd[:, cut]) + mm(skip_k[...], field[x, :, cut])
            halves = value.reshape(C, 2, 8, 256)
            for h in range(2):
                state = twice_gelu(halves[:, h].reshape(160, 256)).astype(bf16)
                state = jnp.concatenate([state, jnp.ones((16, 256), bf16)], axis=0)
                hidden = twice_gelu(mm(hid_k[...], state)).astype(bf16)
                part[pl.ds(pl.multiple_of(x * 16, 16) + 8 * h, 8), cut] = mm(out_k[...], hidden)[0:8]

    for b in range(8):
        blk[pl.ds(b, 32, stride=8), :] = part[:, 128 * b : 128 * b + 128]

    send_f[...] = mm(perm[...], blk[...].astype(bf16)).astype(bf16).reshape(R, 32, 128)
    exchange(on_z, zh, send_f, recv_f, ss_f, rs_f)
    send_g[...] = mm(regroup[...], recv_f[...].reshape(256, 128)).astype(bf16).reshape(R, 32, 128)
    exchange(on_e, e, send_g, recv_g, ss_g, rs_g)
    owned = mm(pick[...], recv_g[...].reshape(256, 128))
    out[...] = owned[0:100].astype(bf16)
    finish_sends()


def scratch():
    v = pltpu.VMEM
    dma = pltpu.SemaphoreType.DMA
    buffers = [
        v((2, 320, 1024), bf16),
        v((3, 3, PK, W2), bf16),
        v((1024, 384), bf16),
        v((384, 1024), bf16),
        v((48, 128), bf16),
        v((256, 24), bf16),
        v((R, 48, 16), bf16),
        v((R, 32, 24), bf16),
        v((LW, 128), bf16),
        v((128, LW), bf16),
        v((128, WW), bf16),
        v((128, WW), bf16),
        v((WW, 128), bf16),
        v((WW, 128), bf16),
        v((256, 256), bf16),
        v((R, 2, 16, LW), bf16),
        v((2, R, 16, LW), bf16),
        v((192, 128), f32),
        v((R, 2, 24, 128), bf16),
        v((2, R, 24, 128), bf16),
        v((384, 128), f32),
        v((448, 128), f32),
        v((R, 56, 128), bf16),
        v((R, 56, 128), bf16),
        v((56, 128), f32),
        v((288, LW), bf16),
        v((56, 128), f32),
        v((56, 128), bf16),
        v((R, 56, 128), bf16),
        v((448, 128), f32),
        v((384, 128), f32),
        v((R, 2, 24, 128), bf16),
        v((R, 2, 24, 128), bf16),
        v((192, 128), f32),
        v((R, 2, 16, LW), bf16),
        v((2, R, 16, LW), bf16),
        v((320, 384), bf16),
        v((32, 1024), f32),
        v((256, 128), f32),
        v((R, 32, 128), bf16),
        v((R, 32, 128), bf16),
        v((R, 32, 128), bf16),
        v((R, 32, 128), bf16),
        v((288, WW), bf16),
        v((256, 256), bf16),
        v((128, 256), bf16),
        v((8, 256), jnp.int32),
        v((128, 128), f32),
        v((320, 320), bf16),
        v((512, 176), bf16),
        v((320, 128), f32),
        v((16, 512), bf16),
    ]
    one, by_x = [dma((1,))] * 2, [dma((2,))] * 2
    sems = [dma((15,))] + by_x + by_x + one + [dma((3,))] * 3 + one + one + by_x + one + one
    return buffers + sems


def local(
    field,
    spectral_weight,
    skip_weight,
    skip_bias,
    hidden_weight,
    hidden_bias,
    out_weight,
    block_ids,
    send_rows,
    recv_rows,
):
    tables = [jnp.asarray(t) for t in constants()]
    args = [
        jnp.transpose(field, (0, 2, 1, 3)).reshape(2, 320, Z * T_SIZE),
        spectral_weight.reshape(3, 3, PK, W2),
        skip_weight,
        skip_bias.reshape(1, C),
        hidden_weight,
        hidden_bias.reshape(1, HID),
        out_weight.reshape(1, HID),
        block_ids.reshape(1, 200),
        send_rows.reshape(1, 200),
        recv_rows.reshape(1, 100),
    ] + tables
    vmem = pl.BlockSpec(memory_space=pltpu.VMEM)
    hbm = pl.BlockSpec(memory_space=pl.ANY)
    result = pl.pallas_call(
        kernel,
        out_shape=jax.ShapeDtypeStruct((100, 128), bf16),
        in_specs=[hbm] * 2 + [vmem] * 8 + [hbm] * len(tables),
        out_specs=vmem,
        scratch_shapes=scratch(),
        compiler_params=pltpu.CompilerParams(
            collective_id=0, has_side_effects=True, vmem_limit_bytes=56 * 1024 * 1024
        ),
    )(*args)
    return result.reshape(1, 1, 100, 128)


def solution(mesh):
    placed = (
        P("gx", "gy", None, None),
        P("gx", "gy", None),
        P(),
        P(),
        P(),
        P(),
        P(),
        P("gx", "gy", None),
        P("gx", "gy", None),
        P("gx", "gy", None),
    )
    return jax.shard_map(
        local, mesh=mesh, in_specs=placed, out_specs=P("gx", "gy", None, None), check_vma=False
    )
```

```python
import functools
import math

import jax
import jax.numpy as jnp
import ml_dtypes
import numpy as np
from jax import lax
from jax.experimental import pallas as pl
from jax.experimental.pallas import tpu as pltpu
from jax.sharding import PartitionSpec as P

C = 20
HID = 64
MX = 24
MY = 24
MZ = 12
MT = 12
Z = 32
T_SIZE = 32
X = 128
Y = 128
KZT = MZ * MT
PK = 18
G = 6
R = 8
LW = G * 128
WW = 896
W2 = 2 * C * C
BIAS_LANE = 60
FAR_FIRST = (4, 3, 5, 2, 6, 1, 7)
MESH = pl.DeviceIdType.MESH
f32 = jnp.float32
bf16 = jnp.bfloat16
GA = math.sqrt(2.0 / math.pi)
GB = GA * 0.044715


def lane_of(ch, r, k):
    if ch < 18:
        return 128 * (ch // 3) + 64 * r + PK * (ch % 3) + k
    tile = 2 * (ch - 18) + k // 10
    return 128 * tile + 64 * r + 54 + k % 10


def constants():
    half = ml_dtypes.bfloat16

    def cos_sin(f, n, length):
        a = 2.0 * np.pi * ((f * n) % length) / length
        return np.cos(a), np.sin(a)

    q = np.arange(Z * T_SIZE)
    forward = np.zeros((Z * T_SIZE, 384))
    backward = np.zeros((384, Z * T_SIZE))
    for j in range(R):
        for k in range(PK):
            kk = PK * j + k
            fz, ft = kk % MZ - MZ // 2, kk // MZ - MT // 2
            a = 2.0 * np.pi * (((fz * (q % Z)) % Z) / Z + ((ft * (q // Z)) % T_SIZE) / T_SIZE)
            lane = 128 * (j // 3) + PK * (j % 3) + k
            forward[:, lane] = np.cos(a) / math.sqrt(Z * T_SIZE)
            forward[:, lane + 64] = -np.sin(a) / math.sqrt(Z * T_SIZE)
            backward[lane] = np.cos(a) / math.sqrt(MX * MY * KZT)
            backward[lane + 64] = -np.sin(a) / math.sqrt(MX * MY * KZT)
    backward[BIAS_LANE : BIAS_LANE + 3] = 1.0
    order = (3 * np.arange(R)[None, :] + np.arange(3)[:, None]).reshape(-1)
    fy = order - MY // 2
    c, s = cos_sin(fy[:, None], np.arange(Y)[None, :], Y)
    y_fwd = np.concatenate([c, s], 0) / math.sqrt(Y)
    y_bwd = np.concatenate([c.T, s.T], 0)
    fx = order - MX // 2
    x_fwd = np.zeros((R, 48, 16))
    x_bwd = np.zeros((R, 32, 24))
    for zh in range(R):
        c, s = cos_sin(fx[:, None], 16 * zh + np.arange(16)[None, :], X)
        x_fwd[zh] = np.concatenate([c, s], 0) / math.sqrt(X)
        x_bwd[zh] = np.concatenate([c.T, s.T], 0)
    gather = np.zeros((LW, 128))
    spread = np.zeros((128, LW))
    for ch in range(C):
        for r in range(2):
            for k in range(PK):
                gather[lane_of(ch, r, k), 64 * r + ch] = 1.0
                spread[64 * r + ch, lane_of(ch, r, k)] = 1.0
    widen = np.zeros((128, WW))
    widen_swapped = np.zeros((128, WW))
    sum_re = np.zeros((WW, 128))
    sum_im = np.zeros((WW, 128))
    for r in range(2):
        for ch in range(C):
            for d in range(C):
                col = 400 * r + C * ch + d
                widen[64 * r + ch, col] = 1.0
                widen_swapped[64 * (1 - r) + ch, col] = 1.0
                sum_re[col, d] = 1.0 - 2.0 * r
                sum_im[col, 64 + d] = 1.0
    regroup = np.zeros((256, 256))
    for e in range(R):
        for zh in range(R):
            for n in range(4):
                regroup[32 * e + 4 * zh + n, 32 * zh + 4 * e + n] = 1.0
    tables = (
        forward, backward, y_fwd, y_bwd, x_fwd, x_bwd, gather, spread,
        widen, widen_swapped, sum_re, sum_im, regroup,
    )
    return [t.astype(half) for t in tables]


def mm(a, b):
    return lax.dot_general(a, b, (((1,), (0,)), ((), ())), preferred_element_type=f32)


def iota(shape, dim):
    return lax.broadcasted_iota(jnp.int32, shape, dim)


def one_hot(mask):
    return jnp.where(mask, 1.0, 0.0).astype(f32)


def twice_gelu(v):
    return v + v * jnp.tanh(v * (GA + GB * (v * v)))


def kernel(*refs):
    (
        field_in, weight_in, skip_w, skip_b, hid_w, hid_b, out_w, b_ids, s_rows, r_rows,
        t_fwd_in, t_bwd_in, y_fwd_in, y_bwd_in, x_fwd_in, x_bwd_in, gather_in, spread_in,
        widen_in, widen_sw_in, sum_re_in, sum_im_in, regroup_in,
        out,
        field, weight, t_fwd, t_bwd, y_fwd, y_bwd, x_fwd, x_bwd, gather, spread,
        widen, widen_sw, sum_re, sum_im, regroup,
        send_y, recv_y, ya, send_a, recv_a, xa, xb, send_b, recv_b,
        pairs, amat, mix, send_c, recv_c, xc, xd, send_d, recv_d, xe, send_e, recv_e,
        s6, skipped, part, blk, send_f, recv_f, send_g, recv_g, wpad, perm, pick, idrows, square, skip_k, hid_k,
        skip_bias, out_k,
        fetched,
        ss_y, rs_y, ss_a, rs_a, ss_b, rs_b, ss_p, rs_p, ls_p, ss_c, rs_c,
        ss_d, rs_d, ss_e, rs_e, ss_f, rs_f, ss_g, rs_g,
    ) = refs
    i = lax.axis_index("gx")
    j = lax.axis_index("gy")
    zh = lax.div(i, R)
    e = lax.rem(i, R)

    def turn(n, d):
        return lax.rem(n + d, R)

    def on_y(d):
        return turn(j, d), (i, turn(j, d))

    def on_z(d):
        return turn(zh, d), (R * turn(zh, d) + e, j)

    def on_e(d):
        return turn(e, d), (R * zh + turn(e, d), j)

    owners = []
    for n in range(3):
        first = MY * (3 * zh + n) + 3 * e
        owners.append((lax.div(first, 9), lax.div(lax.rem(first, 9), 3)))
    sources = []
    for a in range(3):
        first = 9 * i + 3 * a
        jx, jy = lax.div(first, MY), lax.rem(first, MY)
        sources.append((R * zh + lax.div(jy, 3), lax.rem(jx, 3)))

    fetch = []
    wanted = [
        (t_fwd_in, t_fwd), (field_in.at[0], field.at[0]), (field_in.at[1], field.at[1]),
        (y_fwd_in, y_fwd), (x_fwd_in, x_fwd), (gather_in, gather),
        (widen_in, widen), (widen_sw_in, widen_sw), (sum_re_in, sum_re), (sum_im_in, sum_im),
        (spread_in, spread), (x_bwd_in, x_bwd), (y_bwd_in, y_bwd), (t_bwd_in, t_bwd),
        (regroup_in, regroup),
    ]
    for n, (source, target) in enumerate(wanted):
        fetch.append(pltpu.make_async_copy(source, target, fetched.at[n]))
    for copy in fetch[:3]:
        copy.start()

    barrier = pltpu.get_barrier_semaphore()
    for near in (on_y, on_z, on_e):
        for d in range(1, R):
            pl.semaphore_signal(barrier, inc=1, device_id=near(d)[1], device_id_type=MESH)

    for copy in fetch[3:]:
        copy.start()

    sent = []

    def await_bytes(view, sem):
        pltpu.make_async_copy(view, view, sem).wait()

    def start(near, me, send, recv, send_sem, recv_sem):
        for d in FAR_FIRST:
            peer, device = near(d)
            pltpu.make_async_remote_copy(
                src_ref=send(peer),
                dst_ref=recv(me),
                send_sem=send_sem,
                recv_sem=recv_sem,
                device_id=device,
                device_id_type=MESH,
            ).start()

    def exchange(near, me, send, recv, send_sem, recv_sem, same=False, beside=None):
        start(
            near, me, (lambda p: send) if same else (lambda p: send.at[p]), lambda p: recv.at[p],
            send_sem.at[0], recv_sem.at[0],
        )
        recv[me] = send[...] if same else send[me]
        seven = recv.at[pl.ds(0, R - 1)]
        sent.append((seven, send_sem.at[0]))
        if beside is not None:
            beside()
        await_bytes(seven, recv_sem.at[0])

    def start_y(x, send, recv, send_sem, recv_sem):
        start(
            on_y, j, lambda p: send.at[p, x], lambda p: recv.at[x, p], send_sem.at[x], recv_sem.at[x]
        )
        recv[x, j] = send[j, x]

    def finish_y(x, recv, recv_sem):
        await_bytes(recv.at[x, pl.ds(0, R - 1)], recv_sem.at[x])

    def start_e(x, send, recv, send_sem, recv_sem):
        start(
            on_e, e, lambda p: send.at[p, x], lambda p: recv.at[x, p], send_sem.at[x], recv_sem.at[x]
        )
        recv[x, e] = send[e, x]

    def weights_copy(n, a, device):
        return pltpu.make_async_remote_copy(
            src_ref=weight_in.at[n],
            dst_ref=weight.at[a],
            send_sem=ss_p.at[n],
            recv_sem=rs_p.at[a],
            device_id=(device, j),
            device_id_type=MESH,
        )

    def weights_kept(n, a):
        return pltpu.make_async_copy(weight_in.at[n], weight.at[a], ls_p.at[n])

    def start_weights():
        for n, (device, a) in enumerate(sources):

            @pl.when(device != i)
            def _():
                weights_copy(n, a, device).start()

            @pl.when(device == i)
            def _():
                weights_kept(n, a).start()

    def finish_weights():
        for n, (device, a) in enumerate(sources):

            @pl.when(device == i)
            def _():
                weights_kept(n, a).wait()

        for a, (device, n) in enumerate(owners):

            @pl.when(device != i)
            def _():
                weights_copy(n, a, device).wait_recv()

    def finish_sends():
        for n, (device, a) in enumerate(sources):

            @pl.when(device != i)
            def _():
                weights_copy(n, a, device).wait_send()

        for view, sem in sent:
            await_bytes(view, sem)
        for recv, send_sem in ((recv_y, ss_y), (recv_a, ss_a), (recv_e, ss_e)):
            for x in range(2):
                await_bytes(recv.at[x, pl.ds(0, R - 1)], send_sem.at[x])

    lane = iota((1, 128), 1)
    in_half = lane & 63
    fwd_sign = jnp.where(lane < 64, 1.0, -1.0)

    def lanes_in(low, high):
        return (in_half >= low) & (in_half < high)

    def put_together(pieces, total=None):
        if total is None:
            total = jnp.zeros(pieces[0][0].shape, f32)
        for rows, origin, low, high in pieces:
            shift = (low - origin) % 128
            moved = rows if shift == 0 else pltpu.roll(rows, shift, 1)
            total = jnp.where(lanes_in(low, high), moved, total)
        return total

    def combine(cosines, sines, sign):
        return cosines + sign * pltpu.roll(sines, 64, 1)

    def along_zt(x):
        got = mm(field[x], t_fwd[...])
        for t in range(3):
            rows_of = [got[16 * c : 16 * c + 16, 128 * t : 128 * t + 128] for c in range(C)]
            for n in range(min(3, R - 3 * t)):
                for g in range(G):
                    pieces = [
                        (rows_of[3 * g + m], PK * n, PK * m, PK * m + PK) for m in range(3)
                    ]
                    if g < 4:
                        cut = 10 * (g % 2)
                        pieces.append(
                            (rows_of[18 + g // 2], PK * n + cut, 54, 54 + min(10, PK - cut))
                        )
                    send_y[3 * t + n, x, :, 128 * g : 128 * g + 128] = put_together(pieces).astype(
                        bf16
                    )

    fetch[0].wait()
    fetch[1].wait()
    along_zt(0)
    pl.semaphore_wait(barrier, 3 * (R - 1))
    start_y(0, send_y, recv_y, ss_y, rs_y)
    start_weights()
    fetch[2].wait()
    along_zt(1)
    start_y(1, send_y, recv_y, ss_y, rs_y)
    for copy in fetch[3:]:
        copy.wait()

    def spread_map(values, rows, cols, places):
        shift = places.bit_length() - 1
        left = one_hot((iota((rows, 128), 0) >> shift) == iota((rows, 128), 1)).astype(bf16)
        right = one_hot((iota((128, cols), 1) >> shift) == iota((128, cols), 0)).astype(bf16)
        wide = mm(mm(left, values.T.astype(bf16)).astype(bf16), right)
        same = (iota((rows, cols), 0) & (places - 1)) == (iota((rows, cols), 1) & (places - 1))
        return jnp.where(same, wide, 0.0)

    def with_parts(matrix, values, at, first):
        for n in range(3):
            half = values.astype(bf16).astype(f32)
            matrix = jnp.where(at == first + n, half, matrix)
            values = values - half
        return matrix

    def column(values, places, width, rows):
        shift = places.bit_length() - 1
        at = one_hot((iota((rows, width), 0) >> shift) == iota((rows, width), 1))
        return jnp.broadcast_to(jnp.sum(at * values, axis=1, keepdims=True), (rows, 128))

    def prepare_clear():
        ya[...] = jnp.zeros((192, 128), f32)
        xb[...] = jnp.zeros((448, 128), f32)
        xd[...] = jnp.zeros((384, 128), f32)
        mix[...] = jnp.zeros((56, 128), f32)

    def prepare_rows():
        idrows[...] = jnp.full((8, 256), -1, jnp.int32)
        idrows[0:1, 0:200] = b_ids[...]
        idrows[1:2, 0:200] = s_rows[...]
        idrows[2:3, 0:100] = r_rows[...]
        row = iota((256, 256), 0)
        by_block = one_hot(row == idrows[0:1, :]).astype(bf16)
        by_row = one_hot(row == idrows[1:2, :]).astype(bf16)
        perm[...] = lax.dot_general(
            by_row, by_block, (((1,), (1,)), ((), ())), preferred_element_type=f32
        ).astype(bf16)
        place = iota((256, 128), 0)
        name = ((place >> 2) & 7) * 32 + (place >> 5) * 4 + (place & 3)
        pick[...] = one_hot(name == idrows[2:3, 0:128]).T.astype(bf16)

    def prepare_weights():
        wpad[...] = jnp.zeros((288, WW), bf16)
        finish_weights()
        for p in range(9):
            wpad[32 * p : 32 * p + PK, 0:W2] = weight[p // 3, p % 3]

    def prepare_skip():
        square[...] = jnp.zeros((128, 128), f32)
        square[0:C, 0:C] = skip_w[...].astype(f32)
        skip_k[...] = spread_map(square[...], 320, 320, 16).astype(bf16)
        skip_bias[...] = with_parts(
            jnp.zeros((320, 128), f32), column(skip_b[...], 16, C, 320), iota((320, 128), 1), BIAS_LANE
        )

    def prepare_hidden():
        square[...] = jnp.zeros((128, 128), f32)
        square[0:C, 0:HID] = 0.5 * hid_w[...].astype(f32)
        wide = spread_map(square[...], 512, 176, 8)
        bias = column(hid_b[...], 8, HID, 512)
        bias = jnp.concatenate([bias, bias[:, 0:48]], axis=1)
        hid_k[...] = with_parts(wide, bias, iota((512, 176), 1), 160).astype(bf16)

    def prepare_out():
        right = one_hot((iota((HID, 512), 1) >> 3) == iota((HID, 512), 0)).astype(bf16)
        left = jnp.broadcast_to(0.5 * out_w[...].astype(f32), (16, HID)).astype(bf16)
        same = (iota((16, 512), 1) & 7) == iota((16, 512), 0)
        out_k[...] = jnp.where(same, mm(left, right), 0.0).astype(bf16)

    prepare_clear()
    prepare_skip()

    for x in range(2):
        finish_y(x, recv_y, rs_y)
        got = mm(y_fwd[...], recv_y[x].reshape(Y, LW))
        for g in range(G):
            part_g = got[:, 128 * g : 128 * g + 128]
            rows = combine(part_g[0:MY], part_g[MY : 2 * MY], fwd_sign)
            for m in range(3):
                ya[pl.ds(G * m + g, R, stride=24), :] = rows[R * m : R * m + R]
        send_a[:, x] = ya[...].astype(bf16).reshape(R, 24, 128)
        start_e(x, send_a, recv_a, ss_a, rs_a)
    prepare_weights()
    for x in range(2):
        finish_y(x, recv_a, rs_a)

    places = range(3 * G)
    for p in range(R):
        for x in range(2):
            xa[48 * p + 24 * x : 48 * p + 24 * x + 24, :] = recv_a[x, p].astype(f32)
    data = jnp.concatenate(
        [xa[pl.ds(u, 16, stride=24), :] for u in places], axis=1
    ).astype(bf16)
    got = mm(x_fwd[zh], data)
    for u in places:
        part_u = got[:, 128 * u : 128 * u + 128]
        rows = combine(part_u[0:MX], part_u[MX : 2 * MX], fwd_sign)
        for m in range(3):
            xb[pl.ds(3 * G * m + u, R, stride=56), :] = rows[R * m : R * m + R]
    for p in range(R):
        send_b[p] = xb[56 * p : 56 * p + 56, :].astype(bf16)
    exchange(on_z, zh, send_b, recv_b, ss_b, rs_b, beside=prepare_hidden)
    total = recv_b[0].astype(f32)
    for p in range(1, R):
        total = total + recv_b[p].astype(f32)
    pairs[...] = total

    k_row = iota((32, 128), 0)
    k_half = iota((32, 128), 1) & 63
    usual = (k_half < 54) & (lax.rem(k_half, PK) == k_row)
    late = (k_half >= 54) & (k_row < PK)
    own_k = [
        one_hot(usual | (late & (k_half - 54 == k_row))),
        one_hot(usual | (late & (k_half - 44 == k_row))),
    ] * 2 + [one_hot(usual)] * 2
    for p in range(9):
        for g in range(G):
            row = jnp.broadcast_to(pairs[G * p + g : G * p + g + 1, :], (32, 128))
            amat[32 * p : 32 * p + 32, 128 * g : 128 * g + 128] = (row * own_k[g]).astype(bf16)
    compact = mm(amat[...], gather[...]).astype(bf16)
    weights = wpad[...].astype(f32)
    straight = (mm(compact, widen[...]) * weights).astype(bf16)
    crossed = (mm(compact, widen_sw[...]) * weights).astype(bf16)
    mixed = (mm(straight, sum_re[...]) + mm(crossed, sum_im[...])).astype(bf16)
    wide = mm(mixed, spread[...])
    for p in range(9):
        for g in range(G):
            tile = wide[32 * p : 32 * p + 32, 128 * g : 128 * g + 128] * own_k[g]
            mix[G * p + g : G * p + g + 1, :] = jnp.sum(tile, axis=0, keepdims=True)
    send_c[...] = mix[...].astype(bf16)

    def prepare_late():
        for x in range(2):
            for c in range(4):
                cut = slice(256 * c, 256 * c + 256)
                skipped[x, :, cut] = mm(skip_k[...], field[x, :, cut])
        prepare_out()
        prepare_rows()

    exchange(on_z, zh, send_c, recv_c, ss_c, rs_c, same=True, beside=prepare_late)

    for p in range(R):
        xc[56 * p : 56 * p + 56, :] = recv_c[p].astype(f32)

    def by_frequency(ref, first, stride):
        return jnp.concatenate(
            [ref[pl.ds(first(m), R, stride=stride), :] for m in range(3)], axis=0
        )

    data = jnp.concatenate(
        [by_frequency(xc, lambda m: 3 * G * m + u, 56) for u in places], axis=1
    ).astype(bf16)
    got = mm(x_bwd[zh], data)
    for u in places:
        part_u = got[:, 128 * u : 128 * u + 128]
        xd[pl.ds(u, 16, stride=24), :] = combine(part_u[0:16], part_u[16:32], -fwd_sign)
    for x in range(2):
        for p in range(R):
            send_d[p, x] = xd[48 * p + 24 * x : 48 * p + 24 * x + 24, :].astype(bf16)
    exchange(on_e, e, send_d, recv_d, ss_d, rs_d)

    for x in range(2):
        for p in range(R):
            xe[24 * p : 24 * p + 24, :] = recv_d[p, x].astype(f32)
        data = jnp.concatenate(
            [by_frequency(xe, lambda m: G * m + g, 24) for g in range(G)], axis=1
        ).astype(bf16)
        got = mm(y_bwd[...], data)
        for g in range(G):
            part_g = got[:, 128 * g : 128 * g + 128]
            turned = combine(part_g[0:Y], part_g[Y : 2 * Y], -fwd_sign).astype(bf16)
            send_e[:, x, :, 128 * g : 128 * g + 128] = turned.reshape(R, 16, 128)
        start_y(x, send_e, recv_e, ss_e, rs_e)

    @pl.loop(0, 2)
    def _(x):
        finish_y(x, recv_e, rs_e)
        for t in range(3):
            rows_of = [
                [recv_e[x, n, :, 128 * g : 128 * g + 128].astype(f32) for g in range(G)]
                for n in range(3 * t, min(R, 3 * t + 3))
            ]
            for c in range(C):
                pieces = []
                for n, tiles in enumerate(rows_of):
                    if c < 18:
                        pieces.append((tiles[c // 3], PK * (c % 3), PK * n, PK * n + PK))
                    else:
                        for part_k in range(2):
                            low = PK * n + 10 * part_k
                            tile = tiles[2 * (c - 18) + part_k]
                            pieces.append((tile, 54, low, min(low + 10, PK * n + PK)))
                bias = skip_bias[16 * c : 16 * c + 16, :] if t == 0 else None
                s6[16 * c : 16 * c + 16, 128 * t : 128 * t + 128] = put_together(
                    pieces, bias
                ).astype(bf16)

        for c in range(4):
            cut = slice(256 * c, 256 * c + 256)
            value = mm(s6[...], t_bwd[:, cut]) + skipped[x, :, cut]
            halves = value.reshape(C, 2, 8, 256)
            for h in range(2):
                state = twice_gelu(halves[:, h].reshape(160, 256)).astype(bf16)
                state = jnp.concatenate([state, jnp.ones((16, 256), bf16)], axis=0)
                hidden = twice_gelu(mm(hid_k[...], state)).astype(bf16)
                part[pl.ds(pl.multiple_of(x * 16, 16) + 8 * h, 8), cut] = mm(out_k[...], hidden)[0:8]

    for b in range(8):
        blk[pl.ds(b, 32, stride=8), :] = part[:, 128 * b : 128 * b + 128]

    send_f[...] = mm(perm[...], blk[...].astype(bf16)).astype(bf16).reshape(R, 32, 128)
    exchange(on_z, zh, send_f, recv_f, ss_f, rs_f)
    send_g[...] = mm(regroup[...], recv_f[...].reshape(256, 128)).astype(bf16).reshape(R, 32, 128)
    exchange(on_e, e, send_g, recv_g, ss_g, rs_g, beside=finish_sends)
    owned = mm(pick[...], recv_g[...].reshape(256, 128))
    out[...] = owned[0:100].astype(bf16)


def scratch():
    v = pltpu.VMEM
    dma = pltpu.SemaphoreType.DMA
    buffers = [
        v((2, 320, 1024), bf16),
        v((3, 3, PK, W2), bf16),
        v((1024, 384), bf16),
        v((384, 1024), bf16),
        v((48, 128), bf16),
        v((256, 24), bf16),
        v((R, 48, 16), bf16),
        v((R, 32, 24), bf16),
        v((LW, 128), bf16),
        v((128, LW), bf16),
        v((128, WW), bf16),
        v((128, WW), bf16),
        v((WW, 128), bf16),
        v((WW, 128), bf16),
        v((256, 256), bf16),
        v((R, 2, 16, LW), bf16),
        v((2, R, 16, LW), bf16),
        v((192, 128), f32),
        v((R, 2, 24, 128), bf16),
        v((2, R, 24, 128), bf16),
        v((384, 128), f32),
        v((448, 128), f32),
        v((R, 56, 128), bf16),
        v((R, 56, 128), bf16),
        v((56, 128), f32),
        v((288, LW), bf16),
        v((56, 128), f32),
        v((56, 128), bf16),
        v((R, 56, 128), bf16),
        v((448, 128), f32),
        v((384, 128), f32),
        v((R, 2, 24, 128), bf16),
        v((R, 2, 24, 128), bf16),
        v((192, 128), f32),
        v((R, 2, 16, LW), bf16),
        v((2, R, 16, LW), bf16),
        v((320, 384), bf16),
        v((2, 320, 1024), f32),
        v((32, 1024), f32),
        v((256, 128), f32),
        v((R, 32, 128), bf16),
        v((R, 32, 128), bf16),
        v((R, 32, 128), bf16),
        v((R, 32, 128), bf16),
        v((288, WW), bf16),
        v((256, 256), bf16),
        v((128, 256), bf16),
        v((8, 256), jnp.int32),
        v((128, 128), f32),
        v((320, 320), bf16),
        v((512, 176), bf16),
        v((320, 128), f32),
        v((16, 512), bf16),
    ]
    one, by_x = [dma((1,))] * 2, [dma((2,))] * 2
    sems = [dma((15,))] + by_x + by_x + one + [dma((3,))] * 3 + one + one + by_x + one + one
    return buffers + sems


def local(
    field,
    spectral_weight,
    skip_weight,
    skip_bias,
    hidden_weight,
    hidden_bias,
    out_weight,
    block_ids,
    send_rows,
    recv_rows,
):
    tables = [jnp.asarray(t) for t in constants()]
    args = [
        jnp.transpose(field, (0, 2, 1, 3)).reshape(2, 320, Z * T_SIZE),
        spectral_weight.reshape(3, 3, PK, W2),
        skip_weight,
        skip_bias.reshape(1, C),
        hidden_weight,
        hidden_bias.reshape(1, HID),
        out_weight.reshape(1, HID),
        block_ids.reshape(1, 200),
        send_rows.reshape(1, 200),
        recv_rows.reshape(1, 100),
    ] + tables
    vmem = pl.BlockSpec(memory_space=pltpu.VMEM)
    hbm = pl.BlockSpec(memory_space=pl.ANY)
    result = pl.pallas_call(
        kernel,
        out_shape=jax.ShapeDtypeStruct((100, 128), bf16),
        in_specs=[hbm] * 2 + [vmem] * 8 + [hbm] * len(tables),
        out_specs=vmem,
        scratch_shapes=scratch(),
        compiler_params=pltpu.CompilerParams(
            collective_id=0, has_side_effects=True, vmem_limit_bytes=56 * 1024 * 1024
        ),
    )(*args)
    return result.reshape(1, 1, 100, 128)


def solution(mesh):
    placed = (
        P("gx", "gy", None, None),
        P("gx", "gy", None),
        P(),
        P(),
        P(),
        P(),
        P(),
        P("gx", "gy", None),
        P("gx", "gy", None),
        P("gx", "gy", None),
    )
    return jax.shard_map(
        local, mesh=mesh, in_specs=placed, out_specs=P("gx", "gy", None, None), check_vma=False
    )
```

```python
import functools
import math

import jax
import jax.numpy as jnp
import ml_dtypes
import numpy as np
from jax import lax
from jax.experimental import pallas as pl
from jax.experimental.pallas import tpu as pltpu
from jax.sharding import PartitionSpec as P

C = 20
HID = 64
MX = 24
MY = 24
MZ = 12
MT = 12
Z = 32
T_SIZE = 32
X = 128
Y = 128
KZT = MZ * MT
PK = 18
G = 6
R = 8
LW = G * 128
WW = 896
W2 = 2 * C * C
BIAS_LANE = 60
FAR_FIRST = (4, 3, 5, 2, 6, 1, 7)
MESH = pl.DeviceIdType.MESH
f32 = jnp.float32
bf16 = jnp.bfloat16
GA = math.sqrt(2.0 / math.pi)
GB = GA * 0.044715


def lane_of(ch, r, k):
    if ch < 18:
        return 128 * (ch // 3) + 64 * r + PK * (ch % 3) + k
    tile = 2 * (ch - 18) + k // 10
    return 128 * tile + 64 * r + 54 + k % 10


def constants():
    half = ml_dtypes.bfloat16

    def cos_sin(f, n, length):
        a = 2.0 * np.pi * ((f * n) % length) / length
        return np.cos(a), np.sin(a)

    q = np.arange(Z * T_SIZE)
    forward = np.zeros((Z * T_SIZE, 384))
    backward = np.zeros((384, Z * T_SIZE))
    for j in range(R):
        for k in range(PK):
            kk = PK * j + k
            fz, ft = kk % MZ - MZ // 2, kk // MZ - MT // 2
            a = 2.0 * np.pi * (((fz * (q % Z)) % Z) / Z + ((ft * (q // Z)) % T_SIZE) / T_SIZE)
            lane = 128 * (j // 3) + PK * (j % 3) + k
            forward[:, lane] = np.cos(a) / math.sqrt(Z * T_SIZE)
            forward[:, lane + 64] = -np.sin(a) / math.sqrt(Z * T_SIZE)
            backward[lane] = np.cos(a) / math.sqrt(MX * MY * KZT)
            backward[lane + 64] = -np.sin(a) / math.sqrt(MX * MY * KZT)
    backward[BIAS_LANE : BIAS_LANE + 3] = 1.0
    order = (3 * np.arange(R)[None, :] + np.arange(3)[:, None]).reshape(-1)
    fy = order - MY // 2
    c, s = cos_sin(fy[:, None], np.arange(Y)[None, :], Y)
    y_fwd = np.concatenate([c, s], 0) / math.sqrt(Y)
    y_bwd = np.concatenate([c.T, s.T], 0)
    fx = order - MX // 2
    x_fwd = np.zeros((R, 48, 16))
    x_bwd = np.zeros((R, 32, 24))
    for zh in range(R):
        c, s = cos_sin(fx[:, None], 16 * zh + np.arange(16)[None, :], X)
        x_fwd[zh] = np.concatenate([c, s], 0) / math.sqrt(X)
        x_bwd[zh] = np.concatenate([c.T, s.T], 0)
    gather = np.zeros((LW, 128))
    spread = np.zeros((128, LW))
    for ch in range(C):
        for r in range(2):
            for k in range(PK):
                gather[lane_of(ch, r, k), 64 * r + ch] = 1.0
                spread[64 * r + ch, lane_of(ch, r, k)] = 1.0
    widen = np.zeros((128, WW))
    widen_swapped = np.zeros((128, WW))
    sum_re = np.zeros((WW, 128))
    sum_im = np.zeros((WW, 128))
    for r in range(2):
        for ch in range(C):
            for d in range(C):
                col = 400 * r + C * ch + d
                widen[64 * r + ch, col] = 1.0
                widen_swapped[64 * (1 - r) + ch, col] = 1.0
                sum_re[col, d] = 1.0 - 2.0 * r
                sum_im[col, 64 + d] = 1.0
    regroup = np.zeros((256, 256))
    for e in range(R):
        for zh in range(R):
            for n in range(4):
                regroup[32 * e + 4 * zh + n, 32 * zh + 4 * e + n] = 1.0
    tables = (
        forward, backward, y_fwd, y_bwd, x_fwd, x_bwd, gather, spread,
        widen, widen_swapped, sum_re, sum_im, regroup,
    )
    return [t.astype(half) for t in tables]


def mm(a, b):
    return lax.dot_general(a, b, (((1,), (0,)), ((), ())), preferred_element_type=f32)


def iota(shape, dim):
    return lax.broadcasted_iota(jnp.int32, shape, dim)


def one_hot(mask):
    return jnp.where(mask, 1.0, 0.0).astype(f32)


def twice_gelu(v):
    return v + v * jnp.tanh(v * (GA + GB * (v * v)))


def kernel(*refs):
    (
        field_in, weight_in, skip_w, skip_b, hid_w, hid_b, out_w, b_ids, s_rows, r_rows,
        t_fwd_in, t_bwd_in, y_fwd_in, y_bwd_in, x_fwd_in, x_bwd_in, gather_in, spread_in,
        widen_in, widen_sw_in, sum_re_in, sum_im_in, regroup_in,
        out,
        field, weight, t_fwd, t_bwd, y_fwd, y_bwd, x_fwd, x_bwd, gather, spread,
        widen, widen_sw, sum_re, sum_im, regroup,
        send_y, recv_y, ya, send_a, recv_a, xa, xb, send_b, recv_b,
        pairs, amat, mix, send_c, recv_c, xc, xd, send_d, recv_d, xe, send_e, recv_e,
        s6, skipped, part, blk, send_f, recv_f, send_g, recv_g, wpad, perm, pick, idrows, square, skip_k, hid_k,
        skip_bias, out_k,
        fetched,
        ss_y, rs_y, ss_a, rs_a, ss_b, rs_b, ss_p, rs_p, ls_p, ss_c, rs_c,
        ss_d, rs_d, ss_e, rs_e, ss_f, rs_f, ss_g, rs_g,
    ) = refs
    i = lax.axis_index("gx")
    j = lax.axis_index("gy")
    zh = lax.div(i, R)
    e = lax.rem(i, R)

    def turn(n, d):
        return lax.rem(n + d, R)

    def on_y(d):
        return turn(j, d), (i, turn(j, d))

    def on_z(d):
        return turn(zh, d), (R * turn(zh, d) + e, j)

    def on_e(d):
        return turn(e, d), (R * zh + turn(e, d), j)

    owners = []
    for n in range(3):
        first = MY * (3 * zh + n) + 3 * e
        owners.append((lax.div(first, 9), lax.div(lax.rem(first, 9), 3)))
    sources = []
    for a in range(3):
        first = 9 * i + 3 * a
        jx, jy = lax.div(first, MY), lax.rem(first, MY)
        sources.append((R * zh + lax.div(jy, 3), lax.rem(jx, 3)))

    fetch = []
    wanted = [
        (t_fwd_in, t_fwd), (field_in.at[0], field.at[0]), (field_in.at[1], field.at[1]),
        (y_fwd_in, y_fwd), (x_fwd_in, x_fwd), (gather_in, gather),
        (widen_in, widen), (widen_sw_in, widen_sw), (sum_re_in, sum_re), (sum_im_in, sum_im),
        (spread_in, spread), (x_bwd_in, x_bwd), (y_bwd_in, y_bwd), (t_bwd_in, t_bwd),
        (regroup_in, regroup),
    ]
    for n, (source, target) in enumerate(wanted):
        fetch.append(pltpu.make_async_copy(source, target, fetched.at[n]))
    for copy in fetch[:3]:
        copy.start()

    barrier = pltpu.get_barrier_semaphore()
    for near in (on_y, on_z, on_e):
        for d in range(1, R):
            pl.semaphore_signal(barrier, inc=1, device_id=near(d)[1], device_id_type=MESH)

    for copy in fetch[3:]:
        copy.start()

    sent = []

    def await_bytes(view, sem):
        pltpu.make_async_copy(view, view, sem).wait()

    def start(near, me, send, recv, send_sem, recv_sem):
        for d in FAR_FIRST:
            peer, device = near(d)
            pltpu.make_async_remote_copy(
                src_ref=send(peer),
                dst_ref=recv(me),
                send_sem=send_sem,
                recv_sem=recv_sem,
                device_id=device,
                device_id_type=MESH,
            ).start()

    def exchange(near, me, send, recv, send_sem, recv_sem, same=False, beside=None):
        start(
            near, me, (lambda p: send) if same else (lambda p: send.at[p]), lambda p: recv.at[p],
            send_sem.at[0], recv_sem.at[0],
        )
        recv[me] = send[...] if same else send[me]
        seven = recv.at[pl.ds(0, R - 1)]
        sent.append((seven, send_sem.at[0]))
        if beside is not None:
            beside()
        await_bytes(seven, recv_sem.at[0])

    def start_y(x, send, recv, send_sem, recv_sem):
        start(
            on_y, j, lambda p: send.at[p, x], lambda p: recv.at[x, p], send_sem.at[x], recv_sem.at[x]
        )
        recv[x, j] = send[j, x]

    def finish_y(x, recv, recv_sem):
        await_bytes(recv.at[x, pl.ds(0, R - 1)], recv_sem.at[x])

    def start_e(x, send, recv, send_sem, recv_sem):
        start(
            on_e, e, lambda p: send.at[p, x], lambda p: recv.at[x, p], send_sem.at[x], recv_sem.at[x]
        )
        recv[x, e] = send[e, x]

    def weights_copy(n, a, device):
        return pltpu.make_async_remote_copy(
            src_ref=weight_in.at[n],
            dst_ref=weight.at[a],
            send_sem=ss_p.at[n],
            recv_sem=rs_p.at[a],
            device_id=(device, j),
            device_id_type=MESH,
        )

    def weights_kept(n, a):
        return pltpu.make_async_copy(weight_in.at[n], weight.at[a], ls_p.at[n])

    def start_weights():
        for n, (device, a) in enumerate(sources):

            @pl.when(device != i)
            def _():
                weights_copy(n, a, device).start()

            @pl.when(device == i)
            def _():
                weights_kept(n, a).start()

    def finish_weights():
        for n, (device, a) in enumerate(sources):

            @pl.when(device == i)
            def _():
                weights_kept(n, a).wait()

        for a, (device, n) in enumerate(owners):

            @pl.when(device != i)
            def _():
                weights_copy(n, a, device).wait_recv()

    def finish_sends():
        for n, (device, a) in enumerate(sources):

            @pl.when(device != i)
            def _():
                weights_copy(n, a, device).wait_send()

        for view, sem in sent:
            await_bytes(view, sem)
        for recv, send_sem in ((recv_y, ss_y), (recv_a, ss_a), (recv_e, ss_e)):
            for x in range(2):
                await_bytes(recv.at[x, pl.ds(0, R - 1)], send_sem.at[x])

    lane = iota((1, 128), 1)
    in_half = lane & 63
    fwd_sign = jnp.where(lane < 64, 1.0, -1.0)

    def lanes_in(low, high):
        return (in_half >= low) & (in_half < high)

    def put_together(pieces, total=None):
        if total is None:
            total = jnp.zeros(pieces[0][0].shape, f32)
        for rows, origin, low, high in pieces:
            shift = (low - origin) % 128
            moved = rows if shift == 0 else pltpu.roll(rows, shift, 1)
            total = jnp.where(lanes_in(low, high), moved, total)
        return total

    def combine(cosines, sines, sign):
        return cosines + sign * pltpu.roll(sines, 64, 1)

    def along_zt(x):
        got = mm(field[x], t_fwd[...])
        for t in range(3):
            rows_of = [got[16 * c : 16 * c + 16, 128 * t : 128 * t + 128] for c in range(C)]
            for n in range(min(3, R - 3 * t)):
                for g in range(G):
                    pieces = [
                        (rows_of[3 * g + m], PK * n, PK * m, PK * m + PK) for m in range(3)
                    ]
                    if g < 4:
                        cut = 10 * (g % 2)
                        pieces.append(
                            (rows_of[18 + g // 2], PK * n + cut, 54, 54 + min(10, PK - cut))
                        )
                    send_y[3 * t + n, x, :, 128 * g : 128 * g + 128] = put_together(pieces).astype(
                        bf16
                    )

    fetch[0].wait()
    fetch[1].wait()
    along_zt(0)
    pl.semaphore_wait(barrier, 3 * (R - 1))
    start_y(0, send_y, recv_y, ss_y, rs_y)
    fetch[2].wait()
    along_zt(1)
    start_y(1, send_y, recv_y, ss_y, rs_y)
    start_weights()
    for copy in fetch[3:]:
        copy.wait()

    def spread_map(values, rows, cols, places):
        shift = places.bit_length() - 1
        left = one_hot((iota((rows, 128), 0) >> shift) == iota((rows, 128), 1)).astype(bf16)
        right = one_hot((iota((128, cols), 1) >> shift) == iota((128, cols), 0)).astype(bf16)
        wide = mm(mm(left, values.T.astype(bf16)).astype(bf16), right)
        same = (iota((rows, cols), 0) & (places - 1)) == (iota((rows, cols), 1) & (places - 1))
        return jnp.where(same, wide, 0.0)

    def with_parts(matrix, values, at, first):
        for n in range(3):
            half = values.astype(bf16).astype(f32)
            matrix = jnp.where(at == first + n, half, matrix)
            values = values - half
        return matrix

    def column(values, places, width, rows):
        shift = places.bit_length() - 1
        at = one_hot((iota((rows, width), 0) >> shift) == iota((rows, width), 1))
        return jnp.broadcast_to(jnp.sum(at * values, axis=1, keepdims=True), (rows, 128))

    def prepare_clear():
        ya[...] = jnp.zeros((192, 128), f32)
        xb[...] = jnp.zeros((448, 128), f32)
        xd[...] = jnp.zeros((384, 128), f32)
        mix[...] = jnp.zeros((56, 128), f32)

    def prepare_rows():
        idrows[...] = jnp.full((8, 256), -1, jnp.int32)
        idrows[0:1, 0:200] = b_ids[...]
        idrows[1:2, 0:200] = s_rows[...]
        idrows[2:3, 0:100] = r_rows[...]
        row = iota((256, 256), 0)
        by_block = one_hot(row == idrows[0:1, :]).astype(bf16)
        by_row = one_hot(row == idrows[1:2, :]).astype(bf16)
        perm[...] = lax.dot_general(
            by_row, by_block, (((1,), (1,)), ((), ())), preferred_element_type=f32
        ).astype(bf16)
        place = iota((256, 128), 0)
        name = ((place >> 2) & 7) * 32 + (place >> 5) * 4 + (place & 3)
        pick[...] = one_hot(name == idrows[2:3, 0:128]).T.astype(bf16)

    def prepare_weights():
        wpad[...] = jnp.zeros((288, WW), bf16)
        finish_weights()
        for p in range(9):
            wpad[32 * p : 32 * p + PK, 0:W2] = weight[p // 3, p % 3]

    def prepare_skip():
        square[...] = jnp.zeros((128, 128), f32)
        square[0:C, 0:C] = skip_w[...].astype(f32)
        skip_k[...] = spread_map(square[...], 320, 320, 16).astype(bf16)
        skip_bias[...] = with_parts(
            jnp.zeros((320, 128), f32), column(skip_b[...], 16, C, 320), iota((320, 128), 1), BIAS_LANE
        )

    def prepare_hidden():
        square[...] = jnp.zeros((128, 128), f32)
        square[0:C, 0:HID] = 0.5 * hid_w[...].astype(f32)
        wide = spread_map(square[...], 512, 176, 8)
        bias = column(hid_b[...], 8, HID, 512)
        bias = jnp.concatenate([bias, bias[:, 0:48]], axis=1)
        hid_k[...] = with_parts(wide, bias, iota((512, 176), 1), 160).astype(bf16)

    def prepare_out():
        right = one_hot((iota((HID, 512), 1) >> 3) == iota((HID, 512), 0)).astype(bf16)
        left = jnp.broadcast_to(0.5 * out_w[...].astype(f32), (16, HID)).astype(bf16)
        same = (iota((16, 512), 1) & 7) == iota((16, 512), 0)
        out_k[...] = jnp.where(same, mm(left, right), 0.0).astype(bf16)

    prepare_clear()
    prepare_skip()

    for x in range(2):
        finish_y(x, recv_y, rs_y)
        got = mm(y_fwd[...], recv_y[x].reshape(Y, LW))
        for g in range(G):
            part_g = got[:, 128 * g : 128 * g + 128]
            rows = combine(part_g[0:MY], part_g[MY : 2 * MY], fwd_sign)
            for m in range(3):
                ya[pl.ds(G * m + g, R, stride=24), :] = rows[R * m : R * m + R]
        send_a[:, x] = ya[...].astype(bf16).reshape(R, 24, 128)
        start_e(x, send_a, recv_a, ss_a, rs_a)
    prepare_weights()
    for x in range(2):
        finish_y(x, recv_a, rs_a)

    places = range(3 * G)
    for p in range(R):
        for x in range(2):
            xa[48 * p + 24 * x : 48 * p + 24 * x + 24, :] = recv_a[x, p].astype(f32)
    data = jnp.concatenate(
        [xa[pl.ds(u, 16, stride=24), :] for u in places], axis=1
    ).astype(bf16)
    got = mm(x_fwd[zh], data)
    for u in places:
        part_u = got[:, 128 * u : 128 * u + 128]
        rows = combine(part_u[0:MX], part_u[MX : 2 * MX], fwd_sign)
        for m in range(3):
            xb[pl.ds(3 * G * m + u, R, stride=56), :] = rows[R * m : R * m + R]
    for p in range(R):
        send_b[p] = xb[56 * p : 56 * p + 56, :].astype(bf16)
    exchange(on_z, zh, send_b, recv_b, ss_b, rs_b, beside=prepare_hidden)
    total = recv_b[0].astype(f32)
    for p in range(1, R):
        total = total + recv_b[p].astype(f32)
    pairs[...] = total

    k_row = iota((32, 128), 0)
    k_half = iota((32, 128), 1) & 63
    usual = (k_half < 54) & (lax.rem(k_half, PK) == k_row)
    late = (k_half >= 54) & (k_row < PK)
    own_k = [
        one_hot(usual | (late & (k_half - 54 == k_row))),
        one_hot(usual | (late & (k_half - 44 == k_row))),
    ] * 2 + [one_hot(usual)] * 2
    for p in range(9):
        for g in range(G):
            row = jnp.broadcast_to(pairs[G * p + g : G * p + g + 1, :], (32, 128))
            amat[32 * p : 32 * p + 32, 128 * g : 128 * g + 128] = (row * own_k[g]).astype(bf16)
    compact = mm(amat[...], gather[...]).astype(bf16)
    weights = wpad[...].astype(f32)
    straight = (mm(compact, widen[...]) * weights).astype(bf16)
    crossed = (mm(compact, widen_sw[...]) * weights).astype(bf16)
    mixed = (mm(straight, sum_re[...]) + mm(crossed, sum_im[...])).astype(bf16)
    wide = mm(mixed, spread[...])
    for p in range(9):
        for g in range(G):
            tile = wide[32 * p : 32 * p + 32, 128 * g : 128 * g + 128] * own_k[g]
            mix[G * p + g : G * p + g + 1, :] = jnp.sum(tile, axis=0, keepdims=True)
    send_c[...] = mix[...].astype(bf16)

    def prepare_late():
        for x in range(2):
            for c in range(4):
                cut = slice(256 * c, 256 * c + 256)
                skipped[x, :, cut] = mm(skip_k[...], field[x, :, cut])
        prepare_out()
        prepare_rows()

    exchange(on_z, zh, send_c, recv_c, ss_c, rs_c, same=True, beside=prepare_late)

    for p in range(R):
        xc[56 * p : 56 * p + 56, :] = recv_c[p].astype(f32)

    def by_frequency(ref, first, stride):
        return jnp.concatenate(
            [ref[pl.ds(first(m), R, stride=stride), :] for m in range(3)], axis=0
        )

    data = jnp.concatenate(
        [by_frequency(xc, lambda m: 3 * G * m + u, 56) for u in places], axis=1
    ).astype(bf16)
    got = mm(x_bwd[zh], data)
    for u in places:
        part_u = got[:, 128 * u : 128 * u + 128]
        xd[pl.ds(u, 16, stride=24), :] = combine(part_u[0:16], part_u[16:32], -fwd_sign)
    for x in range(2):
        for p in range(R):
            send_d[p, x] = xd[48 * p + 24 * x : 48 * p + 24 * x + 24, :].astype(bf16)
    exchange(on_e, e, send_d, recv_d, ss_d, rs_d)

    for x in range(2):
        for p in range(R):
            xe[24 * p : 24 * p + 24, :] = recv_d[p, x].astype(f32)
        data = jnp.concatenate(
            [by_frequency(xe, lambda m: G * m + g, 24) for g in range(G)], axis=1
        ).astype(bf16)
        got = mm(y_bwd[...], data)
        for g in range(G):
            part_g = got[:, 128 * g : 128 * g + 128]
            turned = combine(part_g[0:Y], part_g[Y : 2 * Y], -fwd_sign).astype(bf16)
            send_e[:, x, :, 128 * g : 128 * g + 128] = turned.reshape(R, 16, 128)
        start_y(x, send_e, recv_e, ss_e, rs_e)

    @pl.loop(0, 2)
    def _(x):
        finish_y(x, recv_e, rs_e)
        for t in range(3):
            rows_of = [
                [recv_e[x, n, :, 128 * g : 128 * g + 128].astype(f32) for g in range(G)]
                for n in range(3 * t, min(R, 3 * t + 3))
            ]
            for c in range(C):
                pieces = []
                for n, tiles in enumerate(rows_of):
                    if c < 18:
                        pieces.append((tiles[c // 3], PK * (c % 3), PK * n, PK * n + PK))
                    else:
                        for part_k in range(2):
                            low = PK * n + 10 * part_k
                            tile = tiles[2 * (c - 18) + part_k]
                            pieces.append((tile, 54, low, min(low + 10, PK * n + PK)))
                bias = skip_bias[16 * c : 16 * c + 16, :] if t == 0 else None
                s6[16 * c : 16 * c + 16, 128 * t : 128 * t + 128] = put_together(
                    pieces, bias
                ).astype(bf16)

        for c in range(4):
            cut = slice(256 * c, 256 * c + 256)
            value = mm(s6[...], t_bwd[:, cut]) + skipped[x, :, cut]
            halves = value.reshape(C, 2, 8, 256)
            for h in range(2):
                state = twice_gelu(halves[:, h].reshape(160, 256)).astype(bf16)
                state = jnp.concatenate([state, jnp.ones((16, 256), bf16)], axis=0)
                hidden = twice_gelu(mm(hid_k[...], state)).astype(bf16)
                part[pl.ds(pl.multiple_of(x * 16, 16) + 8 * h, 8), cut] = mm(out_k[...], hidden)[0:8]

    for b in range(8):
        blk[pl.ds(b, 32, stride=8), :] = part[:, 128 * b : 128 * b + 128]

    send_f[...] = mm(perm[...], blk[...].astype(bf16)).astype(bf16).reshape(R, 32, 128)
    exchange(on_z, zh, send_f, recv_f, ss_f, rs_f)
    send_g[...] = mm(regroup[...], recv_f[...].reshape(256, 128)).astype(bf16).reshape(R, 32, 128)
    exchange(on_e, e, send_g, recv_g, ss_g, rs_g, beside=finish_sends)
    owned = mm(pick[...], recv_g[...].reshape(256, 128))
    out[...] = owned[0:100].astype(bf16)


def scratch():
    v = pltpu.VMEM
    dma = pltpu.SemaphoreType.DMA
    buffers = [
        v((2, 320, 1024), bf16),
        v((3, 3, PK, W2), bf16),
        v((1024, 384), bf16),
        v((384, 1024), bf16),
        v((48, 128), bf16),
        v((256, 24), bf16),
        v((R, 48, 16), bf16),
        v((R, 32, 24), bf16),
        v((LW, 128), bf16),
        v((128, LW), bf16),
        v((128, WW), bf16),
        v((128, WW), bf16),
        v((WW, 128), bf16),
        v((WW, 128), bf16),
        v((256, 256), bf16),
        v((R, 2, 16, LW), bf16),
        v((2, R, 16, LW), bf16),
        v((192, 128), f32),
        v((R, 2, 24, 128), bf16),
        v((2, R, 24, 128), bf16),
        v((384, 128), f32),
        v((448, 128), f32),
        v((R, 56, 128), bf16),
        v((R, 56, 128), bf16),
        v((56, 128), f32),
        v((288, LW), bf16),
        v((56, 128), f32),
        v((56, 128), bf16),
        v((R, 56, 128), bf16),
        v((448, 128), f32),
        v((384, 128), f32),
        v((R, 2, 24, 128), bf16),
        v((R, 2, 24, 128), bf16),
        v((192, 128), f32),
        v((R, 2, 16, LW), bf16),
        v((2, R, 16, LW), bf16),
        v((320, 384), bf16),
        v((2, 320, 1024), f32),
        v((32, 1024), f32),
        v((256, 128), f32),
        v((R, 32, 128), bf16),
        v((R, 32, 128), bf16),
        v((R, 32, 128), bf16),
        v((R, 32, 128), bf16),
        v((288, WW), bf16),
        v((256, 256), bf16),
        v((128, 256), bf16),
        v((8, 256), jnp.int32),
        v((128, 128), f32),
        v((320, 320), bf16),
        v((512, 176), bf16),
        v((320, 128), f32),
        v((16, 512), bf16),
    ]
    one, by_x = [dma((1,))] * 2, [dma((2,))] * 2
    sems = [dma((15,))] + by_x + by_x + one + [dma((3,))] * 3 + one + one + by_x + one + one
    return buffers + sems


def local(
    field,
    spectral_weight,
    skip_weight,
    skip_bias,
    hidden_weight,
    hidden_bias,
    out_weight,
    block_ids,
    send_rows,
    recv_rows,
):
    tables = [jnp.asarray(t) for t in constants()]
    args = [
        jnp.transpose(field, (0, 2, 1, 3)).reshape(2, 320, Z * T_SIZE),
        spectral_weight.reshape(3, 3, PK, W2),
        skip_weight,
        skip_bias.reshape(1, C),
        hidden_weight,
        hidden_bias.reshape(1, HID),
        out_weight.reshape(1, HID),
        block_ids.reshape(1, 200),
        send_rows.reshape(1, 200),
        recv_rows.reshape(1, 100),
    ] + tables
    vmem = pl.BlockSpec(memory_space=pltpu.VMEM)
    hbm = pl.BlockSpec(memory_space=pl.ANY)
    result = pl.pallas_call(
        kernel,
        out_shape=jax.ShapeDtypeStruct((100, 128), bf16),
        in_specs=[hbm] * 2 + [vmem] * 8 + [hbm] * len(tables),
        out_specs=vmem,
        scratch_shapes=scratch(),
        compiler_params=pltpu.CompilerParams(
            collective_id=0, has_side_effects=True, vmem_limit_bytes=56 * 1024 * 1024
        ),
    )(*args)
    return result.reshape(1, 1, 100, 128)


def solution(mesh):
    placed = (
        P("gx", "gy", None, None),
        P("gx", "gy", None),
        P(),
        P(),
        P(),
        P(),
        P(),
        P("gx", "gy", None),
        P("gx", "gy", None),
        P("gx", "gy", None),
    )
    return jax.shard_map(
        local, mesh=mesh, in_specs=placed, out_specs=P("gx", "gy", None, None), check_vma=False
    )
```
